256 devices in a mesh: lang: 8 (over x, core), dp: 32 (over z, y).
Axes of the slice: x: 4, y: 4, z: 8, core: 2. Of those that a mesh axis runs over, the one named last changes fastest.
Arguments:
- src_emb: bfloat16 [32768, 768], P(('lang', 'dp')), may hold values from -6 to 6
- tgt_emb: bfloat16 [8, 4096, 768], P(None, ('lang', 'dp')), may hold values from -6 to 6
- slot_group: int32 [8], replicated, may hold values from 0 to 7, each once
- counts: int32 [8], replicated, may hold values from 1024 to 4096, as said below
- align: int32 [8, 4096], P('lang'), may hold values from 0 to 4095, each once within a row
- pair_weight: float32 [8], replicated, may hold values from 4 to 40
Outputs:
- grad_src: bfloat16 [32768, 768], P(('lang', 'dp'))
- grad_tgt: bfloat16 [8, 4096, 768], P(None, ('lang', 'dp'))
- pair_loss: float32 [8], P('lang')
The draws below stay inside these ranges and needn't reach their ends.
Inputs may be any that keep to these rules, and one draw needn't show every extreme that they name: `counts`: at least one pair has all 4096 sentences live. `align`: each row is a permutation.
All inputs are finite; a program needn't handle non-finite values.
Results may differ from the reference program's by a relative error of at most 0.0057.
Values may be sent and summed in bfloat16 or wider, within the bound.
A program may use at most 64 MiB of HBM per device.

```python
import math
import jax
import jax.numpy as jnp
from jax import lax

D = 768
LANGS = 8
PAIR_ROWS = 4096
TOTAL = 32768


def shared_vector(key, salt):
    signs = jnp.where(jax.random.bernoulli(jax.random.fold_in(key, salt), 0.5, (D,)), 1.0, -1.0)
    sizes = jax.random.uniform(jax.random.fold_in(key, salt + 1), (D,), jnp.float32, 4.9, 5.1)
    return signs * sizes


def draw_src_emb(key, part):
    base = jax.random.normal(key, (TOTAL, D), jnp.float32)
    within = jnp.arange(TOTAL) % PAIR_ROWS
    first_vec = shared_vector(key, 7)
    second_vec = shared_vector(key, 9)
    spike_row = (within < 4)[:, None]
    spike_vec = jnp.where((within < 2)[:, None], first_vec[None, :], second_vec[None, :])
    factor = jnp.where(within % 2 == 0, 1.0, 0.95)[:, None]
    values = jnp.where(spike_row, factor * spike_vec, base)
    return jnp.clip(values, -6.0, 6.0).astype(jnp.bfloat16)


def draw_tgt_emb(key, part):
    base = jax.random.normal(jax.random.fold_in(key, 11), (LANGS, PAIR_ROWS, D), jnp.float32)
    strength = jax.random.uniform(jax.random.fold_in(key, 14), (LANGS, PAIR_ROWS, 1), jnp.float32, 0.3, 1.0)
    index = jnp.arange(PAIR_ROWS)
    first_vec = shared_vector(key, 7)
    second_vec = shared_vector(key, 9)
    which_vec = jnp.where((index % 128 == 0)[:, None], first_vec[None, :], second_vec[None, :])
    spike_row = (index % 64 == 0)[None, :, None]
    values = jnp.where(spike_row, strength * which_vec[None, :, :], base)
    return jnp.clip(values, -6.0, 6.0).astype(jnp.bfloat16)


def draw_counts(key, part):
    raw_counts = jax.random.randint(jax.random.fold_in(key, 21), (LANGS,), PAIR_ROWS // 4, PAIR_ROWS + 1)
    chosen = jax.random.randint(jax.random.fold_in(key, 22), (), 0, LANGS)
    return jnp.where(jnp.arange(LANGS) == chosen, PAIR_ROWS, raw_counts).astype(jnp.int32)


def setup_inputs(seed: int = 0) -> dict:
    seeds = jax.random.split(jax.random.key(seed), 7)
    return {
        "src_emb": draw_src_emb(jax.random.fold_in(seeds[6], 71), 0),
        "tgt_emb": draw_tgt_emb(jax.random.fold_in(seeds[6], 71), 0),
        "slot_group": jax.random.permutation(seeds[2], LANGS).astype(jnp.int32),
        "counts": draw_counts(jax.random.fold_in(seeds[6], 71), 0),
        "align": jax.vmap(lambda own: jax.random.permutation(own, PAIR_ROWS))(jax.random.split(seeds[4], LANGS)).reshape((LANGS, PAIR_ROWS)).astype(jnp.int32),
        "pair_weight": jnp.clip(jnp.exp(jax.random.uniform(seeds[5], (LANGS,), jnp.float32, math.log(4.0), math.log(40.0))), 4.0, 40.0),
    }


MARGIN = 0.3
LOW_FILL = -1e+30

def reference(src_emb, tgt_emb, slot_group, counts, align, pair_weight):
    inv_root = 1.0 / math.sqrt(D)
    slot_ids = jnp.arange(LANGS, dtype=jnp.int32)
    slot_of_group = jnp.zeros((LANGS,), jnp.int32).at[slot_group].set(slot_ids)
    sources = src_emb.reshape(LANGS, PAIR_ROWS, D)
    targets = tgt_emb[slot_of_group]

    def one_pair(pair_items):
        src_rows, tgt_rows, link_index, live_count, weight = pair_items
        all_rows = jnp.arange(PAIR_ROWS, dtype=jnp.int32)
        row_live = all_rows < live_count
        col_live = jnp.zeros((PAIR_ROWS,), jnp.int32).at[link_index].set(row_live.astype(jnp.int32)) > 0
        is_pos = all_rows[None, :] == link_index[:, None]
        scores_f = jnp.dot(src_rows, tgt_rows.T, preferred_element_type=jnp.float32) * inv_root
        scores_f = scores_f - MARGIN * is_pos.astype(jnp.float32)
        row_max = lax.optimization_barrier(jnp.max(jnp.where(col_live[None, :], scores_f, LOW_FILL), axis=1))
        row_sum = lax.optimization_barrier(jnp.sum(jnp.where(col_live[None, :], jnp.exp(scores_f - row_max[:, None]), 0.0), axis=1))
        row_lse = row_max + jnp.log(row_sum + (1.0 - row_live.astype(jnp.float32)))
        col_max = lax.optimization_barrier(jnp.max(jnp.where(row_live[:, None], scores_f, LOW_FILL), axis=0))
        col_sum = lax.optimization_barrier(jnp.sum(jnp.where(row_live[:, None], jnp.exp(scores_f - col_max[None, :]), 0.0), axis=0))
        col_lse = col_max + jnp.log(col_sum + (1.0 - col_live.astype(jnp.float32)))
        pos_score = lax.optimization_barrier(jnp.sum(jnp.where(is_pos, scores_f, 0.0), axis=1))
        terms = jnp.where(row_live, row_lse + col_lse[link_index] - 2.0 * pos_score, 0.0)
        loss_value = jnp.sum(terms) / live_count.astype(jnp.float32)
        both_live = row_live[:, None] & col_live[None, :]
        by_row = jnp.where(both_live, jnp.exp(scores_f - row_lse[:, None]), 0.0)
        by_col = jnp.where(both_live, jnp.exp(scores_f - col_lse[None, :]), 0.0)
        pos_hit = (is_pos & row_live[:, None]).astype(jnp.float32)
        grad_tile = (weight * (by_row + by_col - 2.0 * pos_hit)).astype(jnp.bfloat16)
        grad_rows = jnp.dot(grad_tile, tgt_rows, preferred_element_type=jnp.float32) * inv_root
        grad_cols = jnp.dot(grad_tile.T, src_rows, preferred_element_type=jnp.float32) * inv_root
        return (grad_rows.astype(jnp.bfloat16), grad_cols.astype(jnp.bfloat16), loss_value)
    grad_rows, grad_cols, pair_loss = lax.map(one_pair, (sources, targets, align, counts, pair_weight))
    grad_src = grad_rows.reshape(TOTAL, D)
    grad_tgt = grad_cols[slot_group]
    return (grad_src, grad_tgt, pair_loss)
```

```python
import functools
import math

import jax
import jax.numpy as jnp
from jax import lax
from jax.experimental import pallas as pl
from jax.experimental.pallas import tpu as pltpu
from jax.sharding import PartitionSpec as P

MARGIN = 0.3
LOW = -1e30
NY = 4
F32 = jnp.float32
BF16 = jnp.bfloat16


def kernel(
    slots, counts, weights, align, x, t, gsrc, gtgt, loss,
    xs, ys, staged, acol, colok, er, ec, rmax, cmax, gm, psrc, ptgt,
    rst_out, rst_in, cst_out, cst_in, lz_out, lz_in, ly_out, ly_in,
    fz_out, fz_in, fy_out, fy_in, back, ret,
    sa, ra, sgz, rgz, sgy, rgy, srs, rrs, scs, rcs, slz, rlz, sly, rly,
    sfz, rfz, sfy, rfy, sb, rb,
):
    nl, per = t.shape[0], t.shape[1]
    nz = xs.shape[0]
    rows, width = x.shape
    half = rows // 2
    inv_root = 1.0 / math.sqrt(width)
    lang, dp = lax.axis_index("lang"), lax.axis_index("dp")
    z, y = dp // NY, dp % NY
    live = counts[lang]
    weight = weights[lang]

    def z_at(k):
        return {"dp": lax.rem(z + k + nz, nz) * NY + y}

    def y_at(k):
        return {"dp": z * NY + lax.rem(y + k + NY, NY)}

    def lang_at(k):
        return {"lang": lax.rem(lang + k + nl, nl)}

    def remote(src, dst, send, recv, to):
        return pltpu.make_async_remote_copy(
            src_ref=src, dst_ref=dst, send_sem=send, recv_sem=recv,
            device_id=to, device_id_type=pl.DeviceIdType.MESH,
        )

    started = []

    def start(copy):
        copy.start()
        started.append(copy)
        return copy

    barrier = pltpu.get_barrier_semaphore()
    peers = [z_at(k) for k in range(1, nz)] + [y_at(k) for k in range(1, NY)]
    peers += [lang_at(k) for k in range(1, nl)]
    for to in peers:
        pl.semaphore_signal(barrier, inc=1, device_id=to, device_id_type=pl.DeviceIdType.MESH)
    xs[0] = x[...]
    for o in range(nl):
        group = lax.rem(lang + o, nl)
        slot = jnp.int32(0)
        for s in range(nl):
            slot = jnp.where(slots[s] == group, s, slot)
        staged[o] = t[slot]
    ys[0, 0:per] = staged[0]
    pl.semaphore_wait(barrier, len(peers))

    def gather_copies(buf, n, send, recv, at):
        copies = {}
        for k in range(n // 2):
            for h in (0, 1):
                part = pl.ds(h * half, half)
                if k < n // 2 - 1 or h == 0:
                    copies[0, k, h] = remote(
                        buf.at[k, part], buf.at[k + 1, part], send.at[0, k, h], recv.at[k + 1, h], at(1)
                    )
                if k < n // 2 - 1 or h == 1:
                    copies[1, k, h] = remote(
                        buf.at[(n - k) % n, part], buf.at[n - 1 - k, part],
                        send.at[1, k, h], recv.at[n - 1 - k, h], at(-1),
                    )
        return copies

    gz = gather_copies(xs, nz, sgz, rgz, z_at)
    gy = gather_copies(ys, NY, sgy, rgy, y_at)
    for h in (0, 1):
        start(gz[0, 0, h])
        start(gz[1, 0, 1 - h])
    spread = [
        start(remote(staged.at[o], ys.at[0, pl.ds(o * per, per)], sa.at[o], ra.at[o], lang_at(o)))
        for o in range(1, nl)
    ]

    lane = lax.broadcasted_iota(jnp.int32, (1, rows), 1)
    sub = lax.broadcasted_iota(jnp.int32, (rows, rows), 0)

    def target_of(q, position):
        source = lax.rem(lang - position // per + nl, nl)
        return (source * (nz * NY) + z * NY + lax.rem(y - q + NY, NY)) * per + position % per

    def first_row(r):
        return (lax.rem(z - r + nz, nz) * NY + y) * rows

    def prepare():
        for q in range(NY):
            mine = target_of(q, sub)

            def seen(ch, so_far, mine=mine):
                at = pl.multiple_of(ch * rows, rows)
                own = align[0:1, pl.ds(at, rows)]
                own = jnp.where(lane + at < live, own, -1)
                return jnp.where(mine == own, 1.0, so_far)

            hit = lax.fori_loop(0, nz * NY, seen, jnp.zeros((rows, rows), F32))
            hit = jnp.broadcast_to(jnp.max(hit, axis=1, keepdims=True), (rows, rows))
            colok[q : q + 1] = hit.T[0:1]
        for r in range(nz):
            own = align[0:1, pl.ds(pl.multiple_of(first_row(r), rows), rows)]
            acol[r] = jnp.broadcast_to(own.astype(F32), (rows, rows)).T

    prepare()

    target_row = jnp.concatenate([target_of(q, lane) for q in range(NY)], axis=1).astype(F32)
    row_in = lax.broadcasted_iota(jnp.int32, (rows, 1), 0)

    def masks(r):
        column = acol[r][:, 0:1]
        pos = column == target_row
        row_ok = row_in + first_row(r) < live
        return pos, row_ok

    def all_targets():
        return ys[...].reshape(NY * rows, width)

    total_pos = [jnp.zeros((1, NY * rows), F32)]

    def scores(r):
        raw = lax.dot_general(
            xs[r], all_targets(), (((1,), (1,)), ((), ())), preferred_element_type=F32
        )
        pos, row_ok = masks(r)
        col_ok = jnp.concatenate([colok[q : q + 1] for q in range(NY)], axis=1) > 0.5
        s = raw * inv_root - jnp.where(pos, MARGIN, 0.0)
        total_pos[0] += jnp.sum(jnp.where(pos & row_ok, s, 0.0), axis=0, keepdims=True)
        s = jnp.where(row_ok & col_ok, s, LOW)
        top = jnp.max(s, axis=1, keepdims=True)
        e = jnp.exp(s - top)
        er[r] = e
        row_lse = top + jnp.log(jnp.sum(e, axis=1, keepdims=True))
        rmax[r] = jnp.broadcast_to(top, (rows, rows))
        rst_out[r : r + 1] = jnp.broadcast_to(row_lse, (rows, rows)).T[0:1]
        top = jnp.max(s, axis=0, keepdims=True)
        e = jnp.exp(s - top)
        ec[r] = e
        cmax[r, 0:1] = top
        cmax[r, 1:2] = top + jnp.log(jnp.sum(e, axis=0, keepdims=True))

    def z_step(k, h):
        for d in (0, 1):
            part = h if d == 0 else 1 - h
            if (d, k, part) in gz:
                gz[d, k, part].wait_recv()
                if (d, k + 1, part) in gz:
                    start(gz[d, k + 1, part])

    z_step(0, 0)
    for o in range(1, nl):
        spread[o - 1].wait_recv()
        if o == nl // 2 - 1:
            start(gy[0, 0, 0])
            start(gy[1, 0, 0])
        if o == nl - 1:
            start(gy[0, 0, 1])
            start(gy[1, 0, 1])
    z_step(0, 1)
    gy[0, 0, 0].wait_recv()
    gy[1, 0, 0].wait_recv()
    start(gy[0, 1, 0])
    z_step(1, 0)
    gy[0, 0, 1].wait_recv()
    gy[1, 0, 1].wait_recv()
    start(gy[1, 1, 1])
    z_step(1, 1)
    gy[0, 1, 0].wait_recv()
    gy[1, 1, 1].wait_recv()
    scores(0)
    for k in range(2, nz // 2):
        for r in (k - 1, nz - k + 1):
            scores(r)
        z_step(k, 0)
        z_step(k, 1)
    for r in (nz // 2 - 1, nz // 2 + 1):
        scores(r)
    scores(nz // 2)

    parts = cmax[:, 1, :]
    top = jnp.max(parts, axis=0, keepdims=True)
    col_part = top + jnp.log(jnp.sum(jnp.exp(parts - top), axis=0, keepdims=True))
    for q in range(NY):
        cst_out[q : q + 1] = col_part[:, q * rows : (q + 1) * rows]
        cst_out[q + NY : q + NY + 1] = col_part[:, q * rows : (q + 1) * rows]
    rst = [start(remote(rst_out, rst_in.at[k], srs.at[k], rrs.at[k], z_at(k))) for k in range(1, nz)]
    cst = [start(remote(cst_out, cst_in.at[k], scs.at[k], rcs.at[k], y_at(k))) for k in range(1, NY)]

    def combine(pieces):
        top = functools.reduce(jnp.maximum, pieces)
        return top + jnp.log(functools.reduce(jnp.add, [jnp.exp(p - top) for p in pieces]))

    def turn(piece, k):
        return jnp.concatenate([piece[piece.shape[0] - k :], piece[: piece.shape[0] - k]], axis=0)

    for copy in cst:
        copy.wait_recv()
    col_lse = combine([cst_out[0:NY]] + [turn(cst_in[k, 0:NY], k) for k in range(1, NY)])
    for copy in rst:
        copy.wait_recv()
    row_lse = combine([rst_out[...]] + [turn(rst_in[k], k) for k in range(1, nz)])

    def gradient(r):
        pos, row_ok = masks(r)
        own = jnp.broadcast_to(row_lse[r : r + 1], (rows, rows)).T
        by_row = jnp.where(row_ok, weight * jnp.exp(rmax[r] - own), 0.0)
        for q in range(NY):
            at = slice(q * rows, (q + 1) * rows)
            by_col = jnp.where(
                colok[q : q + 1] > 0.5, weight * jnp.exp(cmax[r, 0:1, at] - col_lse[q : q + 1]), 0.0
            )
            g = er[r, :, at] * by_row + ec[r, :, at] * by_col
            g = g - jnp.where(pos[:, at] & row_ok, 2.0 * weight, 0.0)
            gm[r, :, at] = g.astype(BF16)

    def source_part(r):
        psrc[r] = jnp.dot(gm[r], all_targets(), preferred_element_type=F32)

    def target_part(q):
        ptgt[q] = lax.dot_general(
            gm[:, :, q * rows : (q + 1) * rows].reshape(nz * rows, rows),
            xs[...].reshape(nz * rows, width),
            (((0,), (0,)), ((), ())),
            preferred_element_type=F32,
        )

    def ring(part, n, out, inn, send, recv, at):
        last = n // 2
        copies = {}

        def slot(d, k):
            return (n - (last + 1 - k)) % n if d == 0 else last + 1 - k

        def step(d, k, h):
            begins = 1 if h == d else 2
            value = part[slot(d, k), h * half : (h + 1) * half]
            if k > begins:
                copies[d, k - 1, h].wait_recv()
                value = value + inn[d, k - 1, h].astype(F32)
            out[d, k, h] = value.astype(BF16)
            copies[d, k, h] = start(
                remote(out.at[d, k, h], inn.at[d, k, h], send.at[d, k, h], recv.at[d, k, h], at(1 if d == 0 else -1))
            )

        def owned(h):
            copies[0, last, h].wait_recv()
            copies[1, last, h].wait_recv()
            value = part[0, h * half : (h + 1) * half]
            value = value + inn[0, last, h].astype(F32) + inn[1, last, h].astype(F32)
            return (value * inv_root).astype(BF16)

        return step, owned

    z_send, z_owned = ring(psrc, nz, fz_out, fz_in, sfz, rfz, z_at)
    y_send, y_owned = ring(ptgt, NY, fy_out, fy_in, sfy, rfy, y_at)
    mid = nz // 2
    gradient(mid)
    source_part(mid)
    z_send(0, 1, 0)
    z_send(1, 1, 1)
    for r in (mid + 1, mid - 1):
        gradient(r)
        source_part(r)
    z_send(0, 2, 1)
    z_send(1, 2, 0)
    for r in range(nz):
        if abs(r - mid) > 1:
            gradient(r)
    target_part(NY // 2)
    y_send(0, 1, 0)
    y_send(1, 1, 1)
    z_send(0, 2, 0)
    z_send(1, 2, 1)
    for q in (1, 3):
        target_part(q)
    y_send(0, 2, 1)
    y_send(1, 2, 0)
    for r in (mid + 2, mid - 2):
        source_part(r)
    z_send(0, 3, 1)
    z_send(1, 3, 0)
    y_send(0, 2, 0)
    y_send(1, 2, 1)
    target_part(0)

    own_rows = jnp.where(lane + first_row(0) < live, row_lse[0:1], 0.0)
    own_cols = jnp.where(colok[0:1] > 0.5, col_lse[0:1], 0.0)
    pos_sum = functools.reduce(jnp.add, [total_pos[0][:, q * rows : (q + 1) * rows] for q in range(NY)])
    lz_out[...] = jnp.broadcast_to(own_rows + own_cols - 2.0 * pos_sum, lz_out.shape)
    lz = [start(remote(lz_out, lz_in.at[k], slz.at[k], rlz.at[k], z_at(k))) for k in range(1, nz)]
    for r in (mid + 3, mid - 3):
        source_part(r % nz)
    source_part(0)
    z_send(0, 3, 0)
    z_send(1, 3, 1)
    for copy in lz:
        copy.wait_recv()
    ly_out[...] = functools.reduce(jnp.add, [lz_out[...]] + [lz_in[k] for k in range(1, nz)])
    ly = [start(remote(ly_out, ly_in.at[k], sly.at[k], rly.at[k], y_at(k))) for k in range(1, NY)]
    z_send(0, 4, 1)
    z_send(1, 4, 0)

    backs = []
    for h in (0, 1):
        value = y_owned(h)
        for i in range(nl // 2):
            o = h * (nl // 2) + i
            if o == 0:
                ret[0] = value[0:per]
            else:
                back[o] = value[i * per : (i + 1) * per]
                backs.append(start(remote(back.at[o], ret.at[o], sb.at[o], rb.at[o], lang_at(-o))))
    z_send(0, 4, 0)
    z_send(1, 4, 1)
    for copy in ly:
        copy.wait_recv()
    everything = functools.reduce(jnp.add, [ly_out[...]] + [ly_in[k] for k in range(1, NY)])
    loss[0] = jnp.sum(everything[0:1]) / live.astype(F32)
    for copy in backs:
        copy.wait_recv()
    for s in range(nl):
        gtgt[s] = ret[lax.rem(slots[s] - lang + nl, nl)]
    for h in (1, 0):
        gsrc[h * half : (h + 1) * half] = z_owned(h)
    for copy in started:
        copy.wait_send()


def per_device(src_emb, tgt_emb, slot_group, counts, align, pair_weight):
    rows, width = src_emb.shape
    nl, per = tgt_emb.shape[0], tgt_emb.shape[1]
    nd = lax.axis_size("dp")
    nz = nd // NY
    cols = NY * rows
    half = rows // 2
    kz, ky = nz // 2 + 1, NY // 2 + 1
    vmem, smem, dma = pltpu.VMEM, pltpu.SMEM, pltpu.SemaphoreType.DMA
    in_vmem, in_smem = pl.BlockSpec(memory_space=vmem), pl.BlockSpec(memory_space=smem)
    scratch = [
        vmem((nz, rows, width), BF16), vmem((NY, rows, width), BF16), vmem((nl, per, width), BF16),
        vmem((nz, rows, rows), F32), vmem((8, rows), F32),
        vmem((nz, rows, cols), F32), vmem((nz, rows, cols), F32),
        vmem((nz, rows, rows), F32), vmem((nz, 8, cols), F32),
        vmem((nz, rows, cols), BF16), vmem((nz, rows, width), F32), vmem((NY, rows, width), F32),
        vmem((nz, rows), F32), vmem((nz, nz, rows), F32), vmem((8, rows), F32), vmem((NY, 8, rows), F32),
        vmem((8, rows), F32), vmem((nz, 8, rows), F32), vmem((8, rows), F32), vmem((NY, 8, rows), F32),
        vmem((2, kz, 2, half, width), BF16), vmem((2, kz, 2, half, width), BF16),
        vmem((2, ky, 2, half, width), BF16), vmem((2, ky, 2, half, width), BF16),
        vmem((nl, per, width), BF16), vmem((nl, per, width), BF16),
        dma((nl,)), dma((nl,)), dma((2, kz, 2)), dma((nz, 2)), dma((2, ky, 2)), dma((NY, 2)),
        dma((nz,)), dma((nz,)), dma((NY,)), dma((NY,)), dma((nz,)), dma((nz,)), dma((NY,)), dma((NY,)),
        dma((2, kz, 2)), dma((2, kz, 2)), dma((2, ky, 2)), dma((2, ky, 2)), dma((nl,)), dma((nl,)),
    ]
    return tuple(
        pl.pallas_call(
            kernel,
            out_shape=(
                jax.ShapeDtypeStruct((rows, width), BF16),
                jax.ShapeDtypeStruct((nl, per, width), BF16),
                jax.ShapeDtypeStruct((1,), F32),
            ),
            in_specs=[in_smem, in_smem, in_smem, in_vmem, in_vmem, in_vmem],
            out_specs=(in_vmem, in_vmem, in_smem),
            scratch_shapes=scratch,
            compiler_params=pltpu.CompilerParams(
                collective_id=0, has_side_effects=True, vmem_limit_bytes=48 << 20
            ),
        )(slot_group, counts, pair_weight, align, src_emb, tgt_emb)
    )


def solution(mesh):
    in_specs = (
        P(("lang", "dp"), None),
        P(None, ("lang", "dp"), None),
        P(),
        P(),
        P("lang", None),
        P(),
    )
    out_specs = (P(("lang", "dp"), None), P(None, ("lang", "dp"), None), P("lang"))
    return jax.shard_map(
        per_device, mesh=mesh, in_specs=in_specs, out_specs=out_specs, check_vma=False
    )
```

```python
import functools
import math

import jax
import jax.numpy as jnp
from jax import lax
from jax.experimental import pallas as pl
from jax.experimental.pallas import tpu as pltpu
from jax.sharding import PartitionSpec as P

MARGIN = 0.3
LOW = -1e30
NY = 4
F32 = jnp.float32
BF16 = jnp.bfloat16


def kernel(
    slots_hbm, counts_hbm, weights_hbm, align_hbm, x, t_hbm, gsrc, gtgt, loss,
    slots, counts, weights, align, t, xs, ys, staged, acol, colok, er, ec, rmax, cmax, gm, psrc, ptgt,
    rst_out, rst_in, cst_out, cst_in, lz_out, lz_in, ly_out, ly_in,
    fz_out, fz_in, fy_out, fy_in, back, ret,
    sa, ra, sgz, rgz, sgy, rgy, srs, rrs, scs, rcs, slz, rlz, sly, rly,
    sfz, rfz, sfy, rfy, sb, rb, fetched,
):
    nl, per = t.shape[0], t.shape[1]
    nz = xs.shape[0]
    rows, width = x.shape
    half = rows // 2
    inv_root = 1.0 / math.sqrt(width)
    lang, dp = lax.axis_index("lang"), lax.axis_index("dp")
    z, y = dp // NY, dp % NY

    def z_at(k):
        return {"dp": lax.rem(z + k + nz, nz) * NY + y}

    def y_at(k):
        return {"dp": z * NY + lax.rem(y + k + NY, NY)}

    def lang_at(k):
        return {"lang": lax.rem(lang + k + nl, nl)}

    def remote(src, dst, send, recv, to):
        return pltpu.make_async_remote_copy(
            src_ref=src, dst_ref=dst, send_sem=send, recv_sem=recv,
            device_id=to, device_id_type=pl.DeviceIdType.MESH,
        )

    started = []

    def start(copy):
        copy.start()
        started.append(copy)
        return copy

    fetches = [
        pltpu.make_async_copy(src, dst, fetched.at[i])
        for i, (src, dst) in enumerate(
            [(x, xs.at[0]), (slots_hbm, slots), (t_hbm, t), (align_hbm, align), (counts_hbm, counts), (weights_hbm, weights)]
        )
    ]

    barrier = pltpu.get_barrier_semaphore()
    peers = [z_at(k) for k in range(1, nz)] + [y_at(k) for k in range(1, NY)]
    peers += [lang_at(k) for k in range(1, nl)]
    for to in peers:
        pl.semaphore_signal(barrier, inc=1, device_id=to, device_id_type=pl.DeviceIdType.MESH)
    for copy in fetches:
        copy.start()
    for copy in fetches:
        copy.wait()
    live = counts[lang]
    weight = weights[lang]
    for o in range(nl):
        group = lax.rem(lang + o, nl)
        slot = jnp.int32(0)
        for s in range(nl):
            slot = jnp.where(slots[s] == group, s, slot)
        staged[o] = t[slot]
    ys[0, 0:per] = staged[0]
    pl.semaphore_wait(barrier, len(peers))

    def gather_copies(buf, n, send, recv, at):
        copies = {}
        for k in range(n // 2):
            for h in (0, 1):
                part = pl.ds(h * half, half)
                if k < n // 2 - 1 or h == 0:
                    copies[0, k, h] = remote(
                        buf.at[k, part], buf.at[k + 1, part], send.at[0, k, h], recv.at[k + 1, h], at(1)
                    )
                if k < n // 2 - 1 or h == 1:
                    copies[1, k, h] = remote(
                        buf.at[(n - k) % n, part], buf.at[n - 1 - k, part],
                        send.at[1, k, h], recv.at[n - 1 - k, h], at(-1),
                    )
        return copies

    gz = gather_copies(xs, nz, sgz, rgz, z_at)
    gy = gather_copies(ys, NY, sgy, rgy, y_at)
    for h in (0, 1):
        start(gz[0, 0, h])
        start(gz[1, 0, 1 - h])
    spread = [
        start(remote(staged.at[o], ys.at[0, pl.ds(o * per, per)], sa.at[o], ra.at[o], lang_at(o)))
        for o in range(1, nl)
    ]

    lane = lax.broadcasted_iota(jnp.int32, (1, rows), 1)
    sub = lax.broadcasted_iota(jnp.int32, (rows, rows), 0)

    def target_of(q, position):
        source = lax.rem(lang - position // per + nl, nl)
        return (source * (nz * NY) + z * NY + lax.rem(y - q + NY, NY)) * per + position % per

    def first_row(r):
        return (lax.rem(z - r + nz, nz) * NY + y) * rows

    def prepare():
        for q in range(NY):
            mine = target_of(q, sub)

            def seen(ch, so_far, mine=mine):
                at = pl.multiple_of(ch * rows, rows)
                own = align[0:1, pl.ds(at, rows)]
                own = jnp.where(lane + at < live, own, -1)
                return jnp.where(mine == own, 1.0, so_far)

            hit = lax.fori_loop(0, nz * NY, seen, jnp.zeros((rows, rows), F32))
            hit = jnp.broadcast_to(jnp.max(hit, axis=1, keepdims=True), (rows, rows))
            colok[q : q + 1] = hit.T[0:1]
        for r in range(nz):
            own = align[0:1, pl.ds(pl.multiple_of(first_row(r), rows), rows)]
            acol[r] = jnp.broadcast_to(own.astype(F32), (rows, rows)).T

    prepare()

    target_row = jnp.concatenate([target_of(q, lane) for q in range(NY)], axis=1).astype(F32)
    row_in = lax.broadcasted_iota(jnp.int32, (rows, 1), 0)

    def masks(r):
        column = acol[r][:, 0:1]
        pos = column == target_row
        row_ok = row_in + first_row(r) < live
        return pos, row_ok

    def all_targets():
        return ys[...].reshape(NY * rows, width)

    total_pos = [jnp.zeros((1, NY * rows), F32)]

    def scores(r, group):
        raw = lax.dot_general(
            xs[r], all_targets(), (((1,), (1,)), ((), ())), preferred_element_type=F32
        )
        pos, row_ok = masks(r)
        col_ok = jnp.concatenate([colok[q : q + 1] for q in range(NY)], axis=1) > 0.5
        s = raw * inv_root - jnp.where(pos, MARGIN, 0.0)
        total_pos[0] += jnp.sum(jnp.where(pos & row_ok, s, 0.0), axis=0, keepdims=True)
        s = jnp.where(row_ok & col_ok, s, LOW)
        top = jnp.max(s, axis=1, keepdims=True)
        e = jnp.exp(s - top)
        er[r] = e
        row_lse = top + jnp.log(jnp.sum(e, axis=1, keepdims=True))
        rmax[r] = jnp.broadcast_to(top, (rows, rows))
        rst_out[group, r : r + 1] = jnp.broadcast_to(row_lse, (rows, rows)).T[0:1]
        top = jnp.max(s, axis=0, keepdims=True)
        e = jnp.exp(s - top)
        ec[r] = e
        cmax[r, 0:1] = top
        cmax[r, 1:2] = top + jnp.log(jnp.sum(e, axis=0, keepdims=True))

    def z_step(k, h):
        for d in (0, 1):
            part = h if d == 0 else 1 - h
            if (d, k, part) in gz:
                gz[d, k, part].wait_recv()
                if (d, k + 1, part) in gz:
                    start(gz[d, k + 1, part])

    row_copies = {}

    def send_rows(group):
        for k in range(1, nz):
            row_copies[group, k] = start(
                remote(rst_out.at[group], rst_in.at[group, k], srs.at[group, k], rrs.at[group, k], z_at(k))
            )

    z_step(0, 0)
    for o in range(1, nl):
        spread[o - 1].wait_recv()
        if o == nl // 2 - 1:
            start(gy[0, 0, 0])
        if o == nl - 1:
            start(gy[1, 0, 1])
    start(gy[0, 0, 1])
    start(gy[1, 0, 0])
    z_step(0, 1)
    gy[0, 0, 0].wait_recv()
    start(gy[0, 1, 0])
    gy[1, 0, 1].wait_recv()
    start(gy[1, 1, 1])
    z_step(1, 0)
    gy[0, 0, 1].wait_recv()
    gy[1, 0, 0].wait_recv()
    z_step(1, 1)
    gy[0, 1, 0].wait_recv()
    gy[1, 1, 1].wait_recv()
    mid = nz // 2
    scores(0, 0)
    z_step(2, 0)
    for r in (1, nz - 1):
        scores(r, 0)
    for r in (2, nz - 2):
        scores(r, 0)
    send_rows(0)
    z_step(2, 1)
    for r in (mid - 1, mid + 1):
        scores(r, 1)
    send_rows(1)
    z_step(3, 0)
    scores(mid, 2)

    parts = cmax[:, 1, :]
    top = jnp.max(parts, axis=0, keepdims=True)
    col_part = top + jnp.log(jnp.sum(jnp.exp(parts - top), axis=0, keepdims=True))
    for q in range(NY):
        cst_out[q : q + 1] = col_part[:, q * rows : (q + 1) * rows]
        cst_out[q + NY : q + NY + 1] = col_part[:, q * rows : (q + 1) * rows]
    cst = [start(remote(cst_out, cst_in.at[k], scs.at[k], rcs.at[k], y_at(k))) for k in range(1, NY)]
    send_rows(2)

    def combine(pieces):
        top = functools.reduce(jnp.maximum, pieces)
        return top + jnp.log(functools.reduce(jnp.add, [jnp.exp(p - top) for p in pieces]))

    def turn(piece, k):
        return jnp.concatenate([piece[piece.shape[0] - k :], piece[: piece.shape[0] - k]], axis=0)

    for copy in cst:
        copy.wait_recv()
    col_lse = combine([cst_out[0:NY]] + [turn(cst_in[k, 0:NY], k) for k in range(1, NY)])

    def group_of(r):
        return {mid: 2, mid - 1: 1, mid + 1: 1}.get(r, 0)

    arrived = set()
    row_lses = {}

    def row_lse(r):
        if r in row_lses:
            return row_lses[r]
        pieces = [rst_out[group_of(r), r : r + 1]]
        for k in range(1, nz):
            there = (r - k) % nz
            group = group_of(there)
            if (group, k) not in arrived:
                row_copies[group, k].wait_recv()
                arrived.add((group, k))
            pieces.append(rst_in[group, k, there : there + 1])
        row_lses[r] = combine(pieces)
        return row_lses[r]


    def gradient(r):
        pos, row_ok = masks(r)
        own = jnp.broadcast_to(row_lse(r), (rows, rows)).T
        by_row = jnp.where(row_ok, weight * jnp.exp(rmax[r] - own), 0.0)
        for q in range(NY):
            at = slice(q * rows, (q + 1) * rows)
            by_col = jnp.where(
                colok[q : q + 1] > 0.5, weight * jnp.exp(cmax[r, 0:1, at] - col_lse[q : q + 1]), 0.0
            )
            g = er[r, :, at] * by_row + ec[r, :, at] * by_col
            g = g - jnp.where(pos[:, at] & row_ok, 2.0 * weight, 0.0)
            gm[r, :, at] = g.astype(BF16)

    def source_part(r):
        psrc[r] = jnp.dot(gm[r], all_targets(), preferred_element_type=F32)

    def target_part(q):
        ptgt[q] = lax.dot_general(
            gm[:, :, q * rows : (q + 1) * rows].reshape(nz * rows, rows),
            xs[...].reshape(nz * rows, width),
            (((0,), (0,)), ((), ())),
            preferred_element_type=F32,
        )

    def ring(part, n, out, inn, send, recv, at):
        last = n // 2
        copies = {}

        def slot(d, k):
            return (n - (last + 1 - k)) % n if d == 0 else last + 1 - k

        def step(d, k, h):
            begins = 1 if h == d else 2
            value = part[slot(d, k), h * half : (h + 1) * half]
            if k > begins:
                copies[d, k - 1, h].wait_recv()
                value = value + inn[d, k - 1, h].astype(F32)
            out[d, k, h] = value.astype(BF16)
            copies[d, k, h] = start(
                remote(out.at[d, k, h], inn.at[d, k, h], send.at[d, k, h], recv.at[d, k, h], at(1 if d == 0 else -1))
            )

        def owned(h):
            copies[0, last, h].wait_recv()
            copies[1, last, h].wait_recv()
            value = part[0, h * half : (h + 1) * half]
            value = value + inn[0, last, h].astype(F32) + inn[1, last, h].astype(F32)
            return (value * inv_root).astype(BF16)

        return step, owned

    z_send, z_owned = ring(psrc, nz, fz_out, fz_in, sfz, rfz, z_at)
    y_send, y_owned = ring(ptgt, NY, fy_out, fy_in, sfy, rfy, y_at)
    gradient(mid)
    source_part(mid)
    z_send(0, 1, 0)
    z_send(1, 1, 1)
    for r in (mid + 1, mid - 1):
        gradient(r)
        source_part(r)
    z_send(0, 2, 1)
    z_send(1, 2, 0)
    for r in (mid + 2, mid - 2):
        gradient(r)
        source_part(r)
    z_send(0, 2, 0)
    z_send(1, 2, 1)
    for r in (mid + 3, mid - 3, 0):
        gradient(r)
    target_part(NY // 2)
    y_send(0, 1, 0)
    y_send(1, 1, 1)
    z_send(0, 3, 1)
    z_send(1, 3, 0)
    for q in (1, 3):
        target_part(q)
    y_send(0, 2, 1)
    y_send(1, 2, 0)
    for r in (mid + 3, mid - 3):
        source_part(r)
    z_send(0, 3, 0)
    z_send(1, 3, 1)
    y_send(0, 2, 0)
    y_send(1, 2, 1)
    target_part(0)
    source_part(0)

    own_rows = jnp.where(lane + first_row(0) < live, row_lse(0), 0.0)
    own_cols = jnp.where(colok[0:1] > 0.5, col_lse[0:1], 0.0)
    pos_sum = functools.reduce(jnp.add, [total_pos[0][:, q * rows : (q + 1) * rows] for q in range(NY)])
    lz_out[...] = jnp.broadcast_to(own_rows + own_cols - 2.0 * pos_sum, lz_out.shape)
    lz = [start(remote(lz_out, lz_in.at[k], slz.at[k], rlz.at[k], z_at(k))) for k in range(1, nz)]
    z_send(0, 4, 1)
    z_send(1, 4, 0)
    for copy in lz:
        copy.wait_recv()
    ly_out[...] = functools.reduce(jnp.add, [lz_out[...]] + [lz_in[k] for k in range(1, nz)])
    ly = [start(remote(ly_out, ly_in.at[k], sly.at[k], rly.at[k], y_at(k))) for k in range(1, NY)]
    z_send(0, 4, 0)
    z_send(1, 4, 1)

    backs = []
    for h in (0, 1):
        value = y_owned(h)
        for i in range(nl // 2):
            o = h * (nl // 2) + i
            if o == 0:
                ret[0] = value[0:per]
            else:
                back[o] = value[i * per : (i + 1) * per]
                backs.append(start(remote(back.at[o], ret.at[o], sb.at[o], rb.at[o], lang_at(-o))))
    for copy in ly:
        copy.wait_recv()
    everything = functools.reduce(jnp.add, [ly_out[...]] + [ly_in[k] for k in range(1, NY)])
    loss[0] = jnp.sum(everything[0:1]) / live.astype(F32)
    for copy in backs:
        copy.wait_recv()
    for s in range(nl):
        gtgt[s] = ret[lax.rem(slots[s] - lang + nl, nl)]
    for h in (1, 0):
        gsrc[h * half : (h + 1) * half] = z_owned(h)
    for copy in started:
        copy.wait_send()


def per_device(src_emb, tgt_emb, slot_group, counts, align, pair_weight):
    rows, width = src_emb.shape
    nl, per = tgt_emb.shape[0], tgt_emb.shape[1]
    nd = lax.axis_size("dp")
    nz = nd // NY
    cols = NY * rows
    half = rows // 2
    kz, ky = nz // 2 + 1, NY // 2 + 1
    vmem, smem, dma = pltpu.VMEM, pltpu.SMEM, pltpu.SemaphoreType.DMA
    in_vmem, in_smem = pl.BlockSpec(memory_space=vmem), pl.BlockSpec(memory_space=smem)
    scratch = [
        smem((nl,), jnp.int32), smem((nl,), jnp.int32), smem((nl,), F32),
        vmem((1, nd * rows), jnp.int32), vmem((nl, per, width), BF16),
        vmem((nz, rows, width), BF16), vmem((NY, rows, width), BF16), vmem((nl, per, width), BF16),
        vmem((nz, rows, rows), F32), vmem((8, rows), F32),
        vmem((nz, rows, cols), F32), vmem((nz, rows, cols), F32),
        vmem((nz, rows, rows), F32), vmem((nz, 8, cols), F32),
        vmem((nz, rows, cols), BF16), vmem((nz, rows, width), F32), vmem((NY, rows, width), F32),
        vmem((3, nz, rows), F32), vmem((3, nz, nz, rows), F32), vmem((8, rows), F32), vmem((NY, 8, rows), F32),
        vmem((8, rows), F32), vmem((nz, 8, rows), F32), vmem((8, rows), F32), vmem((NY, 8, rows), F32),
        vmem((2, kz, 2, half, width), BF16), vmem((2, kz, 2, half, width), BF16),
        vmem((2, ky, 2, half, width), BF16), vmem((2, ky, 2, half, width), BF16),
        vmem((nl, per, width), BF16), vmem((nl, per, width), BF16),
        dma((nl,)), dma((nl,)), dma((2, kz, 2)), dma((nz, 2)), dma((2, ky, 2)), dma((NY, 2)),
        dma((3, nz)), dma((3, nz)), dma((NY,)), dma((NY,)), dma((nz,)), dma((nz,)), dma((NY,)), dma((NY,)),
        dma((2, kz, 2)), dma((2, kz, 2)), dma((2, ky, 2)), dma((2, ky, 2)), dma((nl,)), dma((nl,)), dma((6,)),
    ]
    return tuple(
        pl.pallas_call(
            kernel,
            out_shape=(
                jax.ShapeDtypeStruct((rows, width), BF16),
                jax.ShapeDtypeStruct((nl, per, width), BF16),
                jax.ShapeDtypeStruct((1,), F32),
            ),
            in_specs=[pl.BlockSpec(memory_space=pltpu.HBM)] * 6,
            out_specs=(in_vmem, in_vmem, in_smem),
            scratch_shapes=scratch,
            compiler_params=pltpu.CompilerParams(
                collective_id=0, has_side_effects=True, vmem_limit_bytes=48 << 20
            ),
        )(slot_group, counts, pair_weight, align, src_emb, tgt_emb)
    )


def solution(mesh):
    in_specs = (
        P(("lang", "dp"), None),
        P(None, ("lang", "dp"), None),
        P(),
        P(),
        P("lang", None),
        P(),
    )
    out_specs = (P(("lang", "dp"), None), P(None, ("lang", "dp"), None), P("lang"))
    return jax.shard_map(
        per_device, mesh=mesh, in_specs=in_specs, out_specs=out_specs, check_vma=False
    )
```

```python
import functools
import math

import jax
import jax.numpy as jnp
from jax import lax
from jax.experimental import pallas as pl
from jax.experimental.pallas import tpu as pltpu
from jax.sharding import PartitionSpec as P

MARGIN = 0.3
LOW = -1e30
NY = 4
F32 = jnp.float32
BF16 = jnp.bfloat16


def kernel(
    slots_hbm, counts_hbm, weights_hbm, align_hbm, x, t_hbm, gsrc, gtgt, loss,
    slots, counts, weights, align, t, xs, ys, staged, acol, colok, er, ec, rmax, cmax, gm, psrc, ptgt,
    rst_out, rst_in, cst_out, cst_in, lz_out, lz_in, ly_out, ly_in,
    fz_out, fz_in, fy_out, fy_in, back, ret,
    sa, ra, sgz, rgz, sgy, rgy, srs, rrs, scs, rcs, slz, rlz, sly, rly,
    sfz, rfz, sfy, rfy, sb, rb, fetched,
):
    nl, per = t.shape[0], t.shape[1]
    nz = xs.shape[0]
    rows, width = x.shape
    half = rows // 2
    inv_root = 1.0 / math.sqrt(width)
    lang, dp = lax.axis_index("lang"), lax.axis_index("dp")
    z, y = dp // NY, dp % NY

    def z_at(k):
        return {"dp": lax.rem(z + k + nz, nz) * NY + y}

    def y_at(k):
        return {"dp": z * NY + lax.rem(y + k + NY, NY)}

    def lang_at(p):
        return {"lang": lang ^ p}

    def remote(src, dst, send, recv, to):
        return pltpu.make_async_remote_copy(
            src_ref=src, dst_ref=dst, send_sem=send, recv_sem=recv,
            device_id=to, device_id_type=pl.DeviceIdType.MESH,
        )

    started = []

    def start(copy):
        copy.start()
        started.append(copy)
        return copy

    fetches = [
        pltpu.make_async_copy(src, dst, fetched.at[i])
        for i, (src, dst) in enumerate(
            [(x, xs.at[0]), (slots_hbm, slots), (t_hbm, t), (align_hbm, align), (counts_hbm, counts), (weights_hbm, weights)]
        )
    ]

    barrier = pltpu.get_barrier_semaphore()
    peers = [z_at(k) for k in range(1, nz)] + [y_at(k) for k in range(1, NY)]
    peers += [lang_at(k) for k in range(1, nl)]
    for to in peers:
        pl.semaphore_signal(barrier, inc=1, device_id=to, device_id_type=pl.DeviceIdType.MESH)
    for copy in fetches:
        copy.start()
    pl.semaphore_wait(barrier, len(peers))

    def gather_copies(first, buf, n, onward, send, recv, at):
        copies = {}
        chunks = len(onward[0]) + len(onward[1])
        size = rows // chunks
        for d in (0, 1):
            for k in range(n // 2):
                for c in range(chunks) if k < n // 2 - 1 else onward[d]:
                    part = pl.ds(c * size, size)
                    src, dst = (k, k + 1) if d == 0 else ((n - k) % n, n - 1 - k)
                    copies[d, k, c] = remote(
                        (buf.at[src] if k else first).at[part], buf.at[dst, part],
                        send.at[d, k, c], recv.at[dst, c], at(1 - 2 * d),
                    )
        return copies

    gz = gather_copies(x, xs, nz, ((0,), (1,)), sgz, rgz, z_at)
    for h in (0, 1):
        start(gz[0, 0, h])
        start(gz[1, 0, 1 - h])

    for copy in fetches[1:3]:
        copy.wait()
    for p in range(nl):
        group = lang ^ p
        slot = jnp.int32(0)
        for s in range(nl):
            slot = jnp.where(slots[s] == group, s, slot)
        if p == 0:
            ys[0, 0:per] = t[slot]
        else:
            staged[p] = t[slot]
    spread = {
        p: start(remote(staged.at[p], ys.at[0, pl.ds(p * per, per)], sa.at[p], ra.at[p], lang_at(p)))
        for p in (1, 4, 5, 2, 6, 3, 7)
    }
    gy = gather_copies(ys.at[0], ys, NY, ((0, 2), (1, 3)), sgy, rgy, y_at)
    spread[1].wait_recv()
    for d in (0, 1):
        start(gy[d, 0, 0])
    for copy in fetches[0:1] + fetches[3:]:
        copy.wait()
    live = counts[lang]
    weight = weights[lang]

    lane = lax.broadcasted_iota(jnp.int32, (1, rows), 1)
    sub = lax.broadcasted_iota(jnp.int32, (rows, rows), 0)

    def target_of(q, position):
        source = lang ^ (position // per)
        return (source * (nz * NY) + z * NY + lax.rem(y - q + NY, NY)) * per + position % per

    def first_row(r):
        return (lax.rem(z - r + nz, nz) * NY + y) * rows

    def prepare():
        for q in range(NY):
            mine = target_of(q, sub)

            def seen(ch, so_far, mine=mine):
                at = pl.multiple_of(ch * rows, rows)
                own = align[0:1, pl.ds(at, rows)]
                own = jnp.where(lane + at < live, own, -1)
                return jnp.where(mine == own, 1.0, so_far)

            hit = lax.fori_loop(0, nz * NY, seen, jnp.zeros((rows, rows), F32))
            hit = jnp.broadcast_to(jnp.max(hit, axis=1, keepdims=True), (rows, rows))
            colok[q : q + 1] = hit.T[0:1]
        for r in range(nz):
            own = align[0:1, pl.ds(pl.multiple_of(first_row(r), rows), rows)]
            acol[r] = jnp.broadcast_to(own.astype(F32), (rows, rows)).T

    prepare()

    target_row = jnp.concatenate([target_of(q, lane) for q in range(NY)], axis=1).astype(F32)
    row_in = lax.broadcasted_iota(jnp.int32, (rows, 1), 0)

    def masks(r):
        column = acol[r][:, 0:1]
        pos = column == target_row
        row_ok = row_in + first_row(r) < live
        return pos, row_ok

    def all_targets():
        return ys[...].reshape(NY * rows, width)

    total_pos = [jnp.zeros((1, NY * rows), F32)]

    def scores(r, group):
        raw = lax.dot_general(
            xs[r], all_targets(), (((1,), (1,)), ((), ())), preferred_element_type=F32
        )
        pos, row_ok = masks(r)
        col_ok = jnp.concatenate([colok[q : q + 1] for q in range(NY)], axis=1) > 0.5
        s = raw * inv_root - jnp.where(pos, MARGIN, 0.0)
        total_pos[0] += jnp.sum(jnp.where(pos & row_ok, s, 0.0), axis=0, keepdims=True)
        s = jnp.where(row_ok & col_ok, s, LOW)
        top = jnp.max(s, axis=1, keepdims=True)
        e = jnp.exp(s - top)
        er[r] = e
        row_lse = top + jnp.log(jnp.sum(e, axis=1, keepdims=True))
        rmax[r] = jnp.broadcast_to(top, (rows, rows))
        rst_out[group, r : r + 1] = jnp.broadcast_to(row_lse, (rows, rows)).T[0:1]
        top = jnp.max(s, axis=0, keepdims=True)
        e = jnp.exp(s - top)
        ec[r] = e
        cmax[r, 0:1] = top
        cmax[r, 1:2] = top + jnp.log(jnp.sum(e, axis=0, keepdims=True))

    def z_step(k, h):
        for d in (0, 1):
            part = h if d == 0 else 1 - h
            if (d, k, part) in gz:
                gz[d, k, part].wait_recv()
                if (d, k + 1, part) in gz:
                    start(gz[d, k + 1, part])

    row_copies = {}

    def send_rows(group):
        for k in range(1, nz):
            row_copies[group, k] = start(
                remote(rst_out.at[group], rst_in.at[group, k], srs.at[group, k], rrs.at[group, k], z_at(k))
            )

    def y_begin(c):
        for p in (2 * c, 2 * c + 1):
            spread[p].wait_recv()
        for d in (0, 1):
            start(gy[d, 0, c])

    def y_on(d, c):
        gy[d, 0, c].wait_recv()
        start(gy[d, 1, c])

    y_begin(1)
    y_begin(3)
    z_step(0, 0)
    y_begin(2)
    y_on(0, 0)
    y_on(1, 1)
    z_step(0, 1)
    y_on(1, 3)
    y_on(0, 2)
    z_step(1, 0)
    for d in (0, 1):
        for c in (1 - d, 3 - d):
            gy[d, 0, c].wait_recv()
    z_step(1, 1)
    for d in (0, 1):
        for c in (d, d + 2):
            gy[d, 1, c].wait_recv()
    mid = nz // 2
    scores(0, 0)
    z_step(2, 0)
    for r in (1, nz - 1):
        scores(r, 0)
    for r in (2, nz - 2):
        scores(r, 0)
    send_rows(0)
    z_step(2, 1)
    for r in (mid - 1, mid + 1):
        scores(r, 1)
    send_rows(1)
    z_step(3, 0)
    scores(mid, 2)

    parts = cmax[:, 1, :]
    top = jnp.max(parts, axis=0, keepdims=True)
    col_part = top + jnp.log(jnp.sum(jnp.exp(parts - top), axis=0, keepdims=True))
    for q in range(NY):
        cst_out[q : q + 1] = col_part[:, q * rows : (q + 1) * rows]
        cst_out[q + NY : q + NY + 1] = col_part[:, q * rows : (q + 1) * rows]
    cst = [start(remote(cst_out, cst_in.at[k], scs.at[k], rcs.at[k], y_at(k))) for k in range(1, NY)]
    send_rows(2)

    def combine(pieces):
        top = functools.reduce(jnp.maximum, pieces)
        return top + jnp.log(functools.reduce(jnp.add, [jnp.exp(p - top) for p in pieces]))

    def turn(piece, k):
        return jnp.concatenate([piece[piece.shape[0] - k :], piece[: piece.shape[0] - k]], axis=0)

    for copy in cst:
        copy.wait_recv()
    col_lse = combine([cst_out[0:NY]] + [turn(cst_in[k, 0:NY], k) for k in range(1, NY)])

    def group_of(r):
        return {mid: 2, mid - 1: 1, mid + 1: 1}.get(r, 0)

    arrived = set()
    row_lses = {}

    def row_lse(r):
        if r in row_lses:
            return row_lses[r]
        pieces = [rst_out[group_of(r), r : r + 1]]
        for k in range(1, nz):
            there = (r - k) % nz
            group = group_of(there)
            if (group, k) not in arrived:
                row_copies[group, k].wait_recv()
                arrived.add((group, k))
            pieces.append(rst_in[group, k, there : there + 1])
        row_lses[r] = combine(pieces)
        return row_lses[r]


    def gradient(r):
        pos, row_ok = masks(r)
        own = jnp.broadcast_to(row_lse(r), (rows, rows)).T
        by_row = jnp.where(row_ok, weight * jnp.exp(rmax[r] - own), 0.0)
        for q in range(NY):
            at = slice(q * rows, (q + 1) * rows)
            by_col = jnp.where(
                colok[q : q + 1] > 0.5, weight * jnp.exp(cmax[r, 0:1, at] - col_lse[q : q + 1]), 0.0
            )
            g = er[r, :, at] * by_row + ec[r, :, at] * by_col
            g = g - jnp.where(pos[:, at] & row_ok, 2.0 * weight, 0.0)
            gm[r, :, at] = g.astype(BF16)

    def source_part(r):
        psrc[r] = jnp.dot(gm[r], all_targets(), preferred_element_type=F32)

    def target_part(q):
        ptgt[q] = lax.dot_general(
            gm[:, :, q * rows : (q + 1) * rows].reshape(nz * rows, rows),
            xs[...].reshape(nz * rows, width),
            (((0,), (0,)), ((), ())),
            preferred_element_type=F32,
        )

    def ring(part, n, out, inn, send, recv, at):
        last = n // 2
        copies = {}

        def slot(d, k):
            return (n - (last + 1 - k)) % n if d == 0 else last + 1 - k

        def step(d, k, h):
            begins = 1 if h == d else 2
            value = part[slot(d, k), h * half : (h + 1) * half]
            if k > begins:
                copies[d, k - 1, h].wait_recv()
                value = value + inn[d, k - 1, h].astype(F32)
            out[d, k, h] = value.astype(BF16)
            copies[d, k, h] = start(
                remote(out.at[d, k, h], inn.at[d, k, h], send.at[d, k, h], recv.at[d, k, h], at(1 if d == 0 else -1))
            )

        def owned(h):
            copies[0, last, h].wait_recv()
            copies[1, last, h].wait_recv()
            value = part[0, h * half : (h + 1) * half]
            value = value + inn[0, last, h].astype(F32) + inn[1, last, h].astype(F32)
            return (value * inv_root).astype(BF16)

        return step, owned

    z_send, z_owned = ring(psrc, nz, fz_out, fz_in, sfz, rfz, z_at)
    y_send, y_owned = ring(ptgt, NY, fy_out, fy_in, sfy, rfy, y_at)
    gradient(mid)
    source_part(mid)
    z_send(0, 1, 0)
    z_send(1, 1, 1)
    for r in (mid + 1, mid - 1):
        gradient(r)
        source_part(r)
    z_send(0, 2, 1)
    z_send(1, 2, 0)
    for r in (mid + 2, mid - 2):
        gradient(r)
        source_part(r)
    z_send(0, 2, 0)
    z_send(1, 2, 1)
    for r in (mid + 3, mid - 3, 0):
        gradient(r)
    target_part(NY // 2)
    y_send(0, 1, 0)
    y_send(1, 1, 1)
    z_send(0, 3, 1)
    z_send(1, 3, 0)
    for q in (1, 3):
        target_part(q)
    y_send(0, 2, 1)
    y_send(1, 2, 0)
    for r in (mid + 3, mid - 3):
        source_part(r)
    z_send(0, 3, 0)
    z_send(1, 3, 1)
    y_send(0, 2, 0)
    y_send(1, 2, 1)
    target_part(0)
    source_part(0)

    own_rows = jnp.where(lane + first_row(0) < live, row_lse(0), 0.0)
    own_cols = jnp.where(colok[0:1] > 0.5, col_lse[0:1], 0.0)
    pos_sum = functools.reduce(jnp.add, [total_pos[0][:, q * rows : (q + 1) * rows] for q in range(NY)])
    lz_out[...] = jnp.broadcast_to(own_rows + own_cols - 2.0 * pos_sum, lz_out.shape)
    lz = [start(remote(lz_out, lz_in.at[k], slz.at[k], rlz.at[k], z_at(k))) for k in range(1, nz)]
    z_send(0, 4, 1)
    z_send(1, 4, 0)
    for copy in lz:
        copy.wait_recv()
    ly_out[...] = functools.reduce(jnp.add, [lz_out[...]] + [lz_in[k] for k in range(1, nz)])
    ly = [start(remote(ly_out, ly_in.at[k], sly.at[k], rly.at[k], y_at(k))) for k in range(1, NY)]
    z_send(0, 4, 0)
    z_send(1, 4, 1)

    backs = []
    for h in (0, 1):
        value = y_owned(h)
        for i in range(nl // 2):
            p = h * (nl // 2) + i
            if p == 0:
                ret[0] = value[0:per]
            else:
                back[p] = value[i * per : (i + 1) * per]
                backs.append(start(remote(back.at[p], ret.at[p], sb.at[p], rb.at[p], lang_at(p))))
    for copy in ly:
        copy.wait_recv()
    everything = functools.reduce(jnp.add, [ly_out[...]] + [ly_in[k] for k in range(1, NY)])
    loss[0] = jnp.sum(everything[0:1]) / live.astype(F32)
    for copy in backs:
        copy.wait_recv()
    for s in range(nl):
        gtgt[s] = ret[slots[s] ^ lang]
    for h in (1, 0):
        gsrc[h * half : (h + 1) * half] = z_owned(h)
    for copy in started:
        copy.wait_send()


def per_device(src_emb, tgt_emb, slot_group, counts, align, pair_weight):
    rows, width = src_emb.shape
    nl, per = tgt_emb.shape[0], tgt_emb.shape[1]
    nd = lax.axis_size("dp")
    nz = nd // NY
    cols = NY * rows
    half = rows // 2
    kz, ky = nz // 2 + 1, NY // 2 + 1
    vmem, smem, dma = pltpu.VMEM, pltpu.SMEM, pltpu.SemaphoreType.DMA
    in_vmem, in_smem = pl.BlockSpec(memory_space=vmem), pl.BlockSpec(memory_space=smem)
    scratch = [
        smem((nl,), jnp.int32), smem((nl,), jnp.int32), smem((nl,), F32),
        vmem((1, nd * rows), jnp.int32), vmem((nl, per, width), BF16),
        vmem((nz, rows, width), BF16), vmem((NY, rows, width), BF16), vmem((nl, per, width), BF16),
        vmem((nz, rows, rows), F32), vmem((8, rows), F32),
        vmem((nz, rows, cols), F32), vmem((nz, rows, cols), F32),
        vmem((nz, rows, rows), F32), vmem((nz, 8, cols), F32),
        vmem((nz, rows, cols), BF16), vmem((nz, rows, width), F32), vmem((NY, rows, width), F32),
        vmem((3, nz, rows), F32), vmem((3, nz, nz, rows), F32), vmem((8, rows), F32), vmem((NY, 8, rows), F32),
        vmem((8, rows), F32), vmem((nz, 8, rows), F32), vmem((8, rows), F32), vmem((NY, 8, rows), F32),
        vmem((2, kz, 2, half, width), BF16), vmem((2, kz, 2, half, width), BF16),
        vmem((2, ky, 2, half, width), BF16), vmem((2, ky, 2, half, width), BF16),
        vmem((nl, per, width), BF16), vmem((nl, per, width), BF16),
        dma((nl,)), dma((nl,)), dma((2, kz, 2)), dma((nz, 2)), dma((2, ky, 4)), dma((NY, 4)),
        dma((3, nz)), dma((3, nz)), dma((NY,)), dma((NY,)), dma((nz,)), dma((nz,)), dma((NY,)), dma((NY,)),
        dma((2, kz, 2)), dma((2, kz, 2)), dma((2, ky, 2)), dma((2, ky, 2)), dma((nl,)), dma((nl,)), dma((6,)),
    ]
    return tuple(
        pl.pallas_call(
            kernel,
            out_shape=(
                jax.ShapeDtypeStruct((rows, width), BF16),
                jax.ShapeDtypeStruct((nl, per, width), BF16),
                jax.ShapeDtypeStruct((1,), F32),
            ),
            in_specs=[pl.BlockSpec(memory_space=pl.ANY)] * 6,
            out_specs=(in_vmem, in_vmem, in_smem),
            scratch_shapes=scratch,
            compiler_params=pltpu.CompilerParams(
                collective_id=0, has_side_effects=True, vmem_limit_bytes=58 << 20
            ),
        )(slot_group, counts, pair_weight, align, src_emb, tgt_emb)
    )


def solution(mesh):
    in_specs = (
        P(("lang", "dp"), None),
        P(None, ("lang", "dp"), None),
        P(),
        P(),
        P("lang", None),
        P(),
    )
    out_specs = (P(("lang", "dp"), None), P(None, ("lang", "dp"), None), P("lang"))
    return jax.shard_map(
        per_device, mesh=mesh, in_specs=in_specs, out_specs=out_specs, check_vma=False
    )
```

```python
import functools
import math

import jax
import jax.numpy as jnp
from jax import lax
from jax.experimental import pallas as pl
from jax.experimental.pallas import tpu as pltpu
from jax.sharding import PartitionSpec as P

MARGIN = 0.3
LOW = -1e30
NY = 4
F32 = jnp.float32
BF16 = jnp.bfloat16


def kernel(
    slots_hbm, counts_hbm, weights_hbm, align_hbm, x, t_hbm, gsrc, gtgt, loss,
    slots, counts, weights, align, t, xs, ys, staged, acol, colok, er, ec, rmax, cmax, gm, psrc, ptgt,
    rst_out, rst_in, cst_out, cst_in, lz_out, lz_in, ly_out, ly_in,
    fz_out, fz_in, fy_out, fy_in, back, ret,
    sends, ra, rgz, rgy, rrs, rcs, rls, rfz, rfy, fetched,
):
    nl, per = t.shape[0], t.shape[1]
    nz = xs.shape[0]
    rows, width = x.shape
    half = rows // 2
    inv_root = 1.0 / math.sqrt(width)
    lang, dp = lax.axis_index("lang"), lax.axis_index("dp")
    z, y = dp // NY, dp % NY

    def z_at(k):
        return {"dp": lax.rem(z + k + nz, nz) * NY + y}

    def y_at(k):
        return {"dp": z * NY + lax.rem(y + k + NY, NY)}

    def lang_at(p):
        return {"lang": lang ^ p}

    def remote(src, dst, send, recv, to):
        return pltpu.make_async_remote_copy(
            src_ref=src, dst_ref=dst, send_sem=send, recv_sem=recv,
            device_id=to, device_id_type=pl.DeviceIdType.MESH,
        )

    def start(copy):
        copy.start()
        return copy

    def wait_for(ref, sem):
        pltpu.make_async_copy(ref, ref, sem).wait()

    fetches = [
        pltpu.make_async_copy(src, dst, fetched.at[i])
        for i, (src, dst) in enumerate(
            [(x, xs.at[0]), (slots_hbm, slots), (t_hbm, t), (align_hbm, align), (counts_hbm, counts), (weights_hbm, weights)]
        )
    ]

    barrier = pltpu.get_barrier_semaphore()
    peers = [z_at(k) for k in range(1, nz)] + [y_at(k) for k in range(1, NY)]
    peers += [lang_at(k) for k in range(1, nl)]
    for to in peers:
        pl.semaphore_signal(barrier, inc=1, device_id=to, device_id_type=pl.DeviceIdType.MESH)
    for copy in fetches:
        copy.start()
    pl.semaphore_wait(barrier, len(peers))

    def gather_copies(first, buf, n, onward, send, recv, at):
        copies = {}
        chunks = len(onward[0]) + len(onward[1])
        size = rows // chunks
        for d in (0, 1):
            for k in range(n // 2):
                for c in range(chunks) if k < n // 2 - 1 else onward[d]:
                    part = pl.ds(c * size, size)
                    src, dst = (k, k + 1) if d == 0 else ((n - k) % n, n - 1 - k)
                    copies[d, k, c] = remote(
                        (buf.at[src] if k else first).at[part], buf.at[dst, part],
                        send, recv.at[dst, c], at(1 - 2 * d),
                    )
        return copies

    gz = gather_copies(x, xs, nz, ((0,), (1,)), sends.at[0], rgz, z_at)
    for h in (0, 1):
        start(gz[0, 0, h])
        start(gz[1, 0, 1 - h])

    for copy in fetches[1:3]:
        copy.wait()
    for p in range(nl):
        group = lang ^ p
        slot = jnp.int32(0)
        for s in range(nl):
            slot = jnp.where(slots[s] == group, s, slot)
        if p == 0:
            ys[0, 0:per] = t[slot]
        else:
            staged[p] = t[slot]
    for p in (1, 4, 5, 2, 6, 3, 7):
        start(remote(staged.at[p], ys.at[0, pl.ds(p * per, per)], sends.at[2], ra.at[p // 2], lang_at(p)))
    gy = gather_copies(ys.at[0], ys, NY, ((0, 2), (1, 3)), sends.at[1], rgy, y_at)
    wait_for(ys.at[0, pl.ds(per, per)], ra.at[0])
    for d in (0, 1):
        start(gy[d, 0, 0])
    for copy in fetches[0:1] + fetches[3:]:
        copy.wait()
    live = counts[lang]
    weight = weights[lang]

    lane = lax.broadcasted_iota(jnp.int32, (1, rows), 1)
    sub = lax.broadcasted_iota(jnp.int32, (rows, rows), 0)

    def target_of(q, position):
        source = lang ^ (position // per)
        return (source * (nz * NY) + z * NY + lax.rem(y - q + NY, NY)) * per + position % per

    def first_row(r):
        return (lax.rem(z - r + nz, nz) * NY + y) * rows

    def prepare():
        for q in range(NY):
            mine = target_of(q, sub)

            def seen(ch, so_far, mine=mine):
                at = pl.multiple_of(ch * rows, rows)
                own = align[0:1, pl.ds(at, rows)]
                own = jnp.where(lane + at < live, own, -1)
                return jnp.where(mine == own, 1.0, so_far)

            hit = lax.fori_loop(0, nz * NY, seen, jnp.zeros((rows, rows), F32))
            hit = jnp.broadcast_to(jnp.max(hit, axis=1, keepdims=True), (rows, rows))
            colok[q : q + 1] = hit.T[0:1]
        for r in range(nz):
            own = align[0:1, pl.ds(pl.multiple_of(first_row(r), rows), rows)]
            acol[r] = jnp.broadcast_to(own.astype(F32), (rows, rows)).T

    prepare()

    target_row = jnp.concatenate([target_of(q, lane) for q in range(NY)], axis=1).astype(F32)
    row_in = lax.broadcasted_iota(jnp.int32, (rows, 1), 0)

    def masks(r):
        column = acol[r][:, 0:1]
        pos = column == target_row
        row_ok = row_in + first_row(r) < live
        return pos, row_ok

    def all_targets():
        return ys[...].reshape(NY * rows, width)

    total_pos = [jnp.zeros((1, NY * rows), F32)]

    def scores(r, group):
        raw = lax.dot_general(
            xs[r], all_targets(), (((1,), (1,)), ((), ())), preferred_element_type=F32
        )
        pos, row_ok = masks(r)
        col_ok = jnp.concatenate([colok[q : q + 1] for q in range(NY)], axis=1) > 0.5
        s = raw * inv_root - jnp.where(pos, MARGIN, 0.0)
        total_pos[0] += jnp.sum(jnp.where(pos & row_ok, s, 0.0), axis=0, keepdims=True)
        s = jnp.where(row_ok & col_ok, s, LOW)
        top = jnp.max(s, axis=1, keepdims=True)
        e = jnp.exp(s - top)
        er[r] = e
        row_lse = top + jnp.log(jnp.sum(e, axis=1, keepdims=True))
        rmax[r] = jnp.broadcast_to(top, (rows, rows))
        rst_out[group, r : r + 1] = jnp.broadcast_to(row_lse, (rows, rows)).T[0:1]
        top = jnp.max(s, axis=0, keepdims=True)
        e = jnp.exp(s - top)
        ec[r] = e
        cmax[r, 0:1] = top
        cmax[r, 1:2] = top + jnp.log(jnp.sum(e, axis=0, keepdims=True))

    def z_step(k, h):
        for d in (0, 1):
            part = h if d == 0 else 1 - h
            if (d, k, part) in gz:
                gz[d, k, part].wait_recv()
                if (d, k + 1, part) in gz:
                    start(gz[d, k + 1, part])

    def rows_from(group, k):
        return 0 if group < 2 else min(k, nz - k)

    def send_rows(group):
        for k in range(1, nz):
            recv = rrs.at[rows_from(group, k)]
            start(remote(rst_out.at[group], rst_in.at[group, k], sends.at[3], recv, z_at(k)))

    def y_begin(c):
        wait_for(ys.at[0, pl.ds(2 * c * per, 2 * per)], ra.at[c])
        for d in (0, 1):
            start(gy[d, 0, c])

    def y_on(d, c):
        gy[d, 0, c].wait_recv()
        start(gy[d, 1, c])

    y_begin(1)
    z_step(0, 0)
    y_begin(3)
    z_step(0, 1)
    y_begin(2)
    y_on(0, 0)
    y_on(1, 1)
    z_step(1, 0)
    y_on(1, 3)
    y_on(0, 2)
    for d in (0, 1):
        for c in (1 - d, 3 - d):
            gy[d, 0, c].wait_recv()
    z_step(1, 1)
    for d in (0, 1):
        for c in (d, d + 2):
            gy[d, 1, c].wait_recv()
    mid = nz // 2
    scores(0, 0)
    z_step(2, 0)
    for r in (1, nz - 1):
        scores(r, 0)
    for r in (2, nz - 2):
        scores(r, 0)
    send_rows(0)
    z_step(2, 1)
    for r in (mid - 1, mid + 1):
        scores(r, 1)
    send_rows(1)
    z_step(3, 0)
    scores(mid, 2)

    parts = cmax[:, 1, :]
    top = jnp.max(parts, axis=0, keepdims=True)
    col_part = top + jnp.log(jnp.sum(jnp.exp(parts - top), axis=0, keepdims=True))
    for q in range(NY):
        cst_out[q : q + 1] = col_part[:, q * rows : (q + 1) * rows]
        cst_out[q + NY : q + NY + 1] = col_part[:, q * rows : (q + 1) * rows]
    for k in range(1, NY):
        start(remote(cst_out, cst_in.at[k], sends.at[4], rcs.at[0], y_at(k)))
    send_rows(2)

    def combine(pieces):
        top = functools.reduce(jnp.maximum, pieces)
        return top + jnp.log(functools.reduce(jnp.add, [jnp.exp(p - top) for p in pieces]))

    def turn(piece, k):
        return jnp.concatenate([piece[piece.shape[0] - k :], piece[: piece.shape[0] - k]], axis=0)

    wait_for(cst_in.at[1:NY], rcs.at[0])
    col_lse = combine([cst_out[0:NY]] + [turn(cst_in[k, 0:NY], k) for k in range(1, NY)])

    def group_of(r):
        return {mid: 2, mid - 1: 1, mid + 1: 1}.get(r, 0)

    arrived = set()
    row_lses = {}

    def row_lse(r):
        if r in row_lses:
            return row_lses[r]
        pieces = [rst_out[group_of(r), r : r + 1]]
        for k in range(1, nz):
            there = (r - k) % nz
            group = group_of(there)
            which = rows_from(group, k)
            if which not in arrived:
                arrived.add(which)
                together = {0: rst_in.at[0:2, 1:nz], nz // 2: rst_in.at[2, 1:2]}
                wait_for(together.get(which, rst_in.at[2, 1:3]), rrs.at[which])
            pieces.append(rst_in[group, k, there : there + 1])
        row_lses[r] = combine(pieces)
        return row_lses[r]


    def gradient(r):
        pos, row_ok = masks(r)
        own = jnp.broadcast_to(row_lse(r), (rows, rows)).T
        by_row = jnp.where(row_ok, weight * jnp.exp(rmax[r] - own), 0.0)
        for q in range(NY):
            at = slice(q * rows, (q + 1) * rows)
            by_col = jnp.where(
                colok[q : q + 1] > 0.5, weight * jnp.exp(cmax[r, 0:1, at] - col_lse[q : q + 1]), 0.0
            )
            g = er[r, :, at] * by_row + ec[r, :, at] * by_col
            g = g - jnp.where(pos[:, at] & row_ok, 2.0 * weight, 0.0)
            gm[r, :, at] = g.astype(BF16)

    def source_part(r):
        psrc[r] = jnp.dot(gm[r], all_targets(), preferred_element_type=F32)

    def target_part(q):
        ptgt[q] = lax.dot_general(
            gm[:, :, q * rows : (q + 1) * rows].reshape(nz * rows, rows),
            xs[...].reshape(nz * rows, width),
            (((0,), (0,)), ((), ())),
            preferred_element_type=F32,
        )

    def ring(part, n, out, inn, send, recv, at):
        last = n // 2
        copies = {}

        def slot(d, k):
            return (n - (last + 1 - k)) % n if d == 0 else last + 1 - k

        def step(d, k, h):
            begins = 1 if h == d else 2
            value = part[slot(d, k), h * half : (h + 1) * half]
            if k > begins:
                copies[d, k - 1, h].wait_recv()
                value = value + inn[d, k - 1, h].astype(F32)
            out[d, k, h] = value.astype(BF16)
            copies[d, k, h] = start(
                remote(out.at[d, k, h], inn.at[d, k, h], send, recv.at[d, k - 1, h], at(1 - 2 * d))
            )

        def owned(h):
            copies[0, last, h].wait_recv()
            copies[1, last, h].wait_recv()
            value = part[0, h * half : (h + 1) * half]
            value = value + inn[0, last, h].astype(F32) + inn[1, last, h].astype(F32)
            return (value * inv_root).astype(BF16)

        return step, owned

    z_send, z_owned = ring(psrc, nz, fz_out, fz_in, sends.at[5], rfz, z_at)
    y_send, y_owned = ring(ptgt, NY, fy_out, fy_in, sends.at[6], rfy, y_at)
    gradient(mid)
    source_part(mid)
    z_send(0, 1, 0)
    z_send(1, 1, 1)
    for r in (mid + 1, mid - 1):
        gradient(r)
        source_part(r)
    z_send(0, 2, 1)
    z_send(1, 2, 0)
    for r in (mid + 2, mid - 2, mid + 3, mid - 3, 0):
        gradient(r)
    target_part(NY // 2)
    y_send(0, 1, 0)
    y_send(1, 1, 1)
    z_send(0, 2, 0)
    z_send(1, 2, 1)
    for q in (1, 3):
        target_part(q)
    y_send(0, 2, 1)
    y_send(1, 2, 0)
    for r in (mid + 2, mid - 2):
        source_part(r)
    z_send(0, 3, 1)
    z_send(1, 3, 0)
    y_send(0, 2, 0)
    y_send(1, 2, 1)
    target_part(0)

    own_rows = jnp.where(lane + first_row(0) < live, row_lse(0), 0.0)
    own_cols = jnp.where(colok[0:1] > 0.5, col_lse[0:1], 0.0)
    pos_sum = functools.reduce(jnp.add, [total_pos[0][:, q * rows : (q + 1) * rows] for q in range(NY)])
    lz_out[...] = jnp.broadcast_to(own_rows + own_cols - 2.0 * pos_sum, lz_out.shape)
    for k in range(1, nz):
        start(remote(lz_out, lz_in.at[k], sends.at[7], rls.at[0], z_at(k)))
    z_send(0, 3, 0)
    z_send(1, 3, 1)
    for r in (mid + 3, mid - 3):
        source_part(r)

    def send_back(h):
        value = y_owned(h)
        for i in range(nl // 2):
            p = h * (nl // 2) + i
            if p == 0:
                ret[0] = value[0:per]
            else:
                back[p] = value[i * per : (i + 1) * per]
                start(remote(back.at[p], ret.at[p], sends.at[9], rls.at[2], lang_at(p)))

    z_send(0, 4, 1)
    z_send(1, 4, 0)
    send_back(1)
    send_back(0)
    z_send(0, 4, 0)
    z_send(1, 4, 1)
    source_part(0)
    wait_for(lz_in.at[1:nz], rls.at[0])
    ly_out[...] = functools.reduce(jnp.add, [lz_out[...]] + [lz_in[k] for k in range(1, nz)])
    for k in range(1, NY):
        start(remote(ly_out, ly_in.at[k], sends.at[8], rls.at[1], y_at(k)))
    wait_for(ly_in.at[1:NY], rls.at[1])
    everything = functools.reduce(jnp.add, [ly_out[...]] + [ly_in[k] for k in range(1, NY)])
    loss[0] = jnp.sum(everything[0:1]) / live.astype(F32)
    wait_for(ret.at[1:nl], rls.at[2])
    for s in range(nl):
        gtgt[s] = ret[slots[s] ^ lang]
    for h in (1, 0):
        gsrc[h * half : (h + 1) * half] = z_owned(h)
    sent = [xs.at[1:nz], ys.at[1:NY], staged.at[1:nl], rst_in.at[:, 1:nz], cst_in.at[1:NY]]
    sent += [xs.at[1:nz], ys.at[1:NY], lz_in.at[1:nz], ly_in.at[1:NY], back.at[1:nl]]
    for i, ref in enumerate(sent):
        wait_for(ref, sends.at[i])


def per_device(src_emb, tgt_emb, slot_group, counts, align, pair_weight):
    rows, width = src_emb.shape
    nl, per = tgt_emb.shape[0], tgt_emb.shape[1]
    nd = lax.axis_size("dp")
    nz = nd // NY
    cols = NY * rows
    half = rows // 2
    kz, ky = nz // 2 + 1, NY // 2 + 1
    vmem, smem, dma = pltpu.VMEM, pltpu.SMEM, pltpu.SemaphoreType.DMA
    in_vmem, in_smem = pl.BlockSpec(memory_space=vmem), pl.BlockSpec(memory_space=smem)
    scratch = [
        smem((nl,), jnp.int32), smem((nl,), jnp.int32), smem((nl,), F32),
        vmem((1, nd * rows), jnp.int32), vmem((nl, per, width), BF16),
        vmem((nz, rows, width), BF16), vmem((NY, rows, width), BF16), vmem((nl, per, width), BF16),
        vmem((nz, rows, rows), F32), vmem((8, rows), F32),
        vmem((nz, rows, cols), F32), vmem((nz, rows, cols), F32),
        vmem((nz, rows, rows), F32), vmem((nz, 8, cols), F32),
        vmem((nz, rows, cols), BF16), vmem((nz, rows, width), F32), vmem((NY, rows, width), F32),
        vmem((3, nz, rows), F32), vmem((3, nz, nz, rows), F32), vmem((8, rows), F32), vmem((NY, 8, rows), F32),
        vmem((8, rows), F32), vmem((nz, 8, rows), F32), vmem((8, rows), F32), vmem((NY, 8, rows), F32),
        vmem((2, kz, 2, half, width), BF16), vmem((2, kz, 2, half, width), BF16),
        vmem((2, ky, 2, half, width), BF16), vmem((2, ky, 2, half, width), BF16),
        vmem((nl, per, width), BF16), vmem((nl, per, width), BF16),
        dma((10,)), dma((4,)), dma((nz, 2)), dma((NY, 4)), dma((5,)), dma((1,)), dma((3,)),
        dma((2, nz // 2, 2)), dma((2, NY // 2, 2)), dma((6,)),
    ]
    return tuple(
        pl.pallas_call(
            kernel,
            out_shape=(
                pltpu.VMEM((rows, width), BF16),
                pltpu.VMEM((nl, per, width), BF16),
                jax.ShapeDtypeStruct((1,), F32),
            ),
            in_specs=[pl.BlockSpec(memory_space=pl.ANY)] * 6,
            out_specs=(in_vmem, in_vmem, in_smem),
            scratch_shapes=scratch,
            compiler_params=pltpu.CompilerParams(
                collective_id=0, has_side_effects=True, vmem_limit_bytes=58 << 20
            ),
        )(slot_group, counts, pair_weight, align, src_emb, tgt_emb)
    )


def solution(mesh):
    in_specs = (
        P(("lang", "dp"), None),
        P(None, ("lang", "dp"), None),
        P(),
        P(),
        P("lang", None),
        P(),
    )
    out_specs = (P(("lang", "dp"), None), P(None, ("lang", "dp"), None), P("lang"))
    return jax.shard_map(
        per_device, mesh=mesh, in_specs=in_specs, out_specs=out_specs, check_vma=False
    )
```

```python
import functools
import math

import jax
import jax.numpy as jnp
from jax import lax
from jax.experimental import pallas as pl
from jax.experimental.pallas import tpu as pltpu
from jax.sharding import PartitionSpec as P

MARGIN = 0.3
LOW = -1e30
NY = 4
F32 = jnp.float32
BF16 = jnp.bfloat16


def kernel(
    slots_hbm, counts_hbm, weights_hbm, align_hbm, x, t_hbm, gsrc, gtgt, loss,
    slots, counts, weights, align, t, xs, ys, staged, acol, colok, er, ec, rmax, cmax, gm, psrc, ptgt,
    rst_out, rst_in, cst_out, cst_in, lz_out, lz_in, ly_out, ly_in,
    fz_out, fz_in, fy_out, fy_in, back, ret,
    sends, ra, rgz, rgy, rrs, rcs, rls, rfz, rfy, fetched,
):
    nl, per = t.shape[0], t.shape[1]
    nz = xs.shape[0]
    rows, width = x.shape
    half = rows // 2
    inv_root = 1.0 / math.sqrt(width)
    lang, dp = lax.axis_index("lang"), lax.axis_index("dp")
    z, y = dp // NY, dp % NY

    def z_at(k):
        return {"dp": lax.rem(z + k + nz, nz) * NY + y}

    def y_at(k):
        return {"dp": z * NY + lax.rem(y + k + NY, NY)}

    def lang_at(p):
        return {"lang": lang ^ p}

    def remote(src, dst, send, recv, to):
        return pltpu.make_async_remote_copy(
            src_ref=src, dst_ref=dst, send_sem=send, recv_sem=recv,
            device_id=to, device_id_type=pl.DeviceIdType.MESH,
        )

    def start(copy):
        copy.start()
        return copy

    def wait_for(ref, sem):
        pltpu.make_async_copy(ref, ref, sem).wait()

    fetches = [
        pltpu.make_async_copy(src, dst, fetched.at[i])
        for i, (src, dst) in enumerate(
            [(x, xs.at[0]), (slots_hbm, slots), (t_hbm, t), (align_hbm, align), (counts_hbm, counts), (weights_hbm, weights)]
        )
    ]

    barrier = pltpu.get_barrier_semaphore()
    peers = [z_at(k) for k in range(1, nz)] + [y_at(k) for k in range(1, NY)]
    peers += [lang_at(k) for k in range(1, nl)]
    for to in peers:
        pl.semaphore_signal(barrier, inc=1, device_id=to, device_id_type=pl.DeviceIdType.MESH)
    for copy in fetches:
        copy.start()
    pl.semaphore_wait(barrier, len(peers))

    def gather_copies(first, buf, n, onward, send, recv, at):
        copies = {}
        chunks = len(onward[0]) + len(onward[1])
        size = rows // chunks
        for d in (0, 1):
            for k in range(n // 2):
                for c in range(chunks) if k < n // 2 - 1 else onward[d]:
                    part = pl.ds(c * size, size)
                    src, dst = (k, k + 1) if d == 0 else ((n - k) % n, n - 1 - k)
                    copies[d, k, c] = remote(
                        (buf.at[src] if k else first).at[part], buf.at[dst, part],
                        send, recv.at[dst, c], at(1 - 2 * d),
                    )
        return copies

    gz = gather_copies(x, xs, nz, ((0,), (1,)), sends.at[0], rgz, z_at)
    for h in (0, 1):
        start(gz[0, 0, h])
        start(gz[1, 0, 1 - h])

    for copy in fetches[1:3]:
        copy.wait()
    for p in range(nl):
        group = lang ^ p
        slot = jnp.int32(0)
        for s in range(nl):
            slot = jnp.where(slots[s] == group, s, slot)
        if p == 0:
            ys[0, 0:per] = t[slot]
        else:
            staged[p] = t[slot]
    for p in (1, 4, 5, 2, 6, 3, 7):
        start(remote(staged.at[p], ys.at[0, pl.ds(p * per, per)], sends.at[2], ra.at[p // 2], lang_at(p)))
    gy = gather_copies(ys.at[0], ys, NY, ((0, 2), (1, 3)), sends.at[1], rgy, y_at)
    wait_for(ys.at[0, pl.ds(per, per)], ra.at[0])
    for d in (0, 1):
        start(gy[d, 0, 0])
    for copy in fetches[0:1] + fetches[3:]:
        copy.wait()
    live = counts[lang]
    weight = weights[lang]

    lane = lax.broadcasted_iota(jnp.int32, (1, rows), 1)
    sub = lax.broadcasted_iota(jnp.int32, (rows, rows), 0)

    def target_of(q, position):
        source = lang ^ (position // per)
        return (source * (nz * NY) + z * NY + lax.rem(y - q + NY, NY)) * per + position % per

    def first_row(r):
        return (lax.rem(z - r + nz, nz) * NY + y) * rows

    def prepare():
        for q in range(NY):
            mine = target_of(q, sub)

            def seen(ch, so_far, mine=mine):
                at = pl.multiple_of(ch * rows, rows)
                own = align[0:1, pl.ds(at, rows)]
                own = jnp.where(lane + at < live, own, -1)
                return jnp.where(mine == own, 1.0, so_far)

            hit = lax.fori_loop(0, nz * NY, seen, jnp.zeros((rows, rows), F32))
            hit = jnp.broadcast_to(jnp.max(hit, axis=1, keepdims=True), (rows, rows))
            colok[q : q + 1] = hit.T[0:1]
        for r in range(nz):
            own = align[0:1, pl.ds(pl.multiple_of(first_row(r), rows), rows)]
            acol[r] = jnp.broadcast_to(own.astype(F32), (rows, rows)).T

    prepare()

    target_row = jnp.concatenate([target_of(q, lane) for q in range(NY)], axis=1).astype(F32)
    row_in = lax.broadcasted_iota(jnp.int32, (rows, 1), 0)

    def masks(r):
        column = acol[r][:, 0:1]
        pos = column == target_row
        row_ok = row_in + first_row(r) < live
        return pos, row_ok

    def all_targets():
        return ys[...].reshape(NY * rows, width)

    total_pos = [jnp.zeros((1, NY * rows), F32)]

    def scores(r, group):
        raw = lax.dot_general(
            xs[r], all_targets(), (((1,), (1,)), ((), ())), preferred_element_type=F32
        )
        pos, row_ok = masks(r)
        col_ok = jnp.concatenate([colok[q : q + 1] for q in range(NY)], axis=1) > 0.5
        s = raw * inv_root - jnp.where(pos, MARGIN, 0.0)
        total_pos[0] += jnp.sum(jnp.where(pos & row_ok, s, 0.0), axis=0, keepdims=True)
        s = jnp.where(row_ok & col_ok, s, LOW)
        top = jnp.max(s, axis=1, keepdims=True)
        e = jnp.exp(s - top)
        er[r] = e
        row_lse = top + jnp.log(jnp.sum(e, axis=1, keepdims=True))
        rmax[r] = jnp.broadcast_to(top, (rows, rows))
        rst_out[group, r : r + 1] = jnp.broadcast_to(row_lse, (rows, rows)).T[0:1]
        top = jnp.max(s, axis=0, keepdims=True)
        e = jnp.exp(s - top)
        ec[r] = e
        cmax[r, 0:1] = top
        cmax[r, 1:2] = top + jnp.log(jnp.sum(e, axis=0, keepdims=True))

    def z_step(k, h):
        for d in (0, 1):
            part = h if d == 0 else 1 - h
            if (d, k, part) in gz:
                gz[d, k, part].wait_recv()
                if (d, k + 1, part) in gz:
                    start(gz[d, k + 1, part])

    def rows_from(group, k):
        return 0 if group < 2 else min(k, nz - k)

    def send_rows(group):
        for k in range(1, nz):
            recv = rrs.at[rows_from(group, k)]
            start(remote(rst_out.at[group], rst_in.at[group, k], sends.at[3], recv, z_at(k)))

    def y_begin(c):
        wait_for(ys.at[0, pl.ds(2 * c * per, 2 * per)], ra.at[c])
        for d in (0, 1):
            start(gy[d, 0, c])

    def y_on(d, c):
        gy[d, 0, c].wait_recv()
        start(gy[d, 1, c])

    y_begin(1)
    z_step(0, 0)
    y_begin(3)
    z_step(0, 1)
    y_begin(2)
    y_on(0, 0)
    y_on(1, 1)
    z_step(1, 0)
    y_on(1, 3)
    y_on(0, 2)
    for d in (0, 1):
        for c in (1 - d, 3 - d):
            gy[d, 0, c].wait_recv()
    z_step(1, 1)
    for d in (0, 1):
        for c in (d, d + 2):
            gy[d, 1, c].wait_recv()
    mid = nz // 2
    scores(0, 0)
    z_step(2, 0)
    for r in (1, nz - 1):
        scores(r, 0)
    for r in (2, nz - 2):
        scores(r, 0)
    send_rows(0)
    z_step(2, 1)
    for r in (mid - 1, mid + 1):
        scores(r, 1)
    send_rows(1)
    z_step(3, 0)
    scores(mid, 2)

    parts = cmax[:, 1, :]
    top = jnp.max(parts, axis=0, keepdims=True)
    col_part = top + jnp.log(jnp.sum(jnp.exp(parts - top), axis=0, keepdims=True))
    for q in range(NY):
        cst_out[q : q + 1] = col_part[:, q * rows : (q + 1) * rows]
        cst_out[q + NY : q + NY + 1] = col_part[:, q * rows : (q + 1) * rows]
    for k in range(1, NY):
        start(remote(cst_out, cst_in.at[k], sends.at[4], rcs.at[0], y_at(k)))
    send_rows(2)

    def combine(pieces):
        top = functools.reduce(jnp.maximum, pieces)
        return top + jnp.log(functools.reduce(jnp.add, [jnp.exp(p - top) for p in pieces]))

    def turn(piece, k):
        return jnp.concatenate([piece[piece.shape[0] - k :], piece[: piece.shape[0] - k]], axis=0)

    wait_for(cst_in.at[1:NY], rcs.at[0])
    col_lse = combine([cst_out[0:NY]] + [turn(cst_in[k, 0:NY], k) for k in range(1, NY)])

    def group_of(r):
        return {mid: 2, mid - 1: 1, mid + 1: 1}.get(r, 0)

    arrived = set()
    row_lses = {}

    def row_lse(r):
        if r in row_lses:
            return row_lses[r]
        pieces = [rst_out[group_of(r), r : r + 1]]
        for k in range(1, nz):
            there = (r - k) % nz
            group = group_of(there)
            which = rows_from(group, k)
            if which not in arrived:
                arrived.add(which)
                together = {0: rst_in.at[0:2, 1:nz], nz // 2: rst_in.at[2, 1:2]}
                wait_for(together.get(which, rst_in.at[2, 1:3]), rrs.at[which])
            pieces.append(rst_in[group, k, there : there + 1])
        row_lses[r] = combine(pieces)
        return row_lses[r]


    def gradient(r):
        pos, row_ok = masks(r)
        own = jnp.broadcast_to(row_lse(r), (rows, rows)).T
        by_row = jnp.where(row_ok, weight * jnp.exp(rmax[r] - own), 0.0)
        for q in range(NY):
            at = slice(q * rows, (q + 1) * rows)
            by_col = jnp.where(
                colok[q : q + 1] > 0.5, weight * jnp.exp(cmax[r, 0:1, at] - col_lse[q : q + 1]), 0.0
            )
            g = er[r, :, at] * by_row + ec[r, :, at] * by_col
            g = g - jnp.where(pos[:, at] & row_ok, 2.0 * weight, 0.0)
            gm[r, :, at] = g.astype(BF16)

    def source_part(r):
        psrc[r] = jnp.dot(gm[r], all_targets(), preferred_element_type=F32)

    def target_part(q):
        ptgt[q] = lax.dot_general(
            gm[:, :, q * rows : (q + 1) * rows].reshape(nz * rows, rows),
            xs[...].reshape(nz * rows, width),
            (((0,), (0,)), ((), ())),
            preferred_element_type=F32,
        )

    def ring(part, n, out, inn, send, recv, at):
        last = n // 2
        copies = {}

        def slot(d, k):
            return (n - (last + 1 - k)) % n if d == 0 else last + 1 - k

        def step(d, k, h):
            begins = 1 if h == d else 2
            value = part[slot(d, k), h * half : (h + 1) * half]
            if k > begins:
                copies[d, k - 1, h].wait_recv()
                value = value + inn[d, k - 1, h].astype(F32)
            out[d, k, h] = value.astype(BF16)
            copies[d, k, h] = start(
                remote(out.at[d, k, h], inn.at[d, k, h], send, recv.at[d, k - 1, h], at(1 - 2 * d))
            )

        def owned(h):
            copies[0, last, h].wait_recv()
            copies[1, last, h].wait_recv()
            value = part[0, h * half : (h + 1) * half]
            value = value + inn[0, last, h].astype(F32) + inn[1, last, h].astype(F32)
            return (value * inv_root).astype(BF16)

        return step, owned

    z_send, z_owned = ring(psrc, nz, fz_out, fz_in, sends.at[5], rfz, z_at)
    y_send, y_owned = ring(ptgt, NY, fy_out, fy_in, sends.at[6], rfy, y_at)
    gradient(mid)
    source_part(mid)
    z_send(0, 1, 0)
    z_send(1, 1, 1)
    for r in (mid + 1, mid - 1):
        gradient(r)
        source_part(r)
    z_send(0, 2, 1)
    z_send(1, 2, 0)
    for r in (mid + 2, mid - 2, mid + 3, mid - 3, 0):
        gradient(r)
    target_part(NY // 2)
    y_send(0, 1, 0)
    y_send(1, 1, 1)
    z_send(0, 2, 0)
    z_send(1, 2, 1)
    for q in (1, 3):
        target_part(q)
    y_send(0, 2, 1)
    y_send(1, 2, 0)
    for r in (mid + 2, mid - 2):
        source_part(r)
    z_send(0, 3, 1)
    z_send(1, 3, 0)
    y_send(0, 2, 0)
    y_send(1, 2, 1)
    target_part(0)

    own_rows = jnp.where(lane + first_row(0) < live, row_lse(0), 0.0)
    own_cols = jnp.where(colok[0:1] > 0.5, col_lse[0:1], 0.0)
    pos_sum = functools.reduce(jnp.add, [total_pos[0][:, q * rows : (q + 1) * rows] for q in range(NY)])
    lz_out[...] = jnp.broadcast_to(own_rows + own_cols - 2.0 * pos_sum, lz_out.shape)
    for k in range(1, nz):
        start(remote(lz_out, lz_in.at[k], sends.at[7], rls.at[0], z_at(k)))
    z_send(0, 3, 0)
    z_send(1, 3, 1)
    for r in (mid + 3, mid - 3):
        source_part(r)

    def send_back(h):
        value = y_owned(h)
        for i in range(nl // 2):
            p = h * (nl // 2) + i
            if p == 0:
                ret[0] = value[0:per]
            else:
                back[p] = value[i * per : (i + 1) * per]
                start(remote(back.at[p], ret.at[p], sends.at[9], rls.at[2], lang_at(p)))

    z_send(0, 4, 1)
    z_send(1, 4, 0)
    send_back(1)
    send_back(0)
    z_send(0, 4, 0)
    z_send(1, 4, 1)
    source_part(0)
    wait_for(lz_in.at[1:nz], rls.at[0])
    ly_out[...] = functools.reduce(jnp.add, [lz_out[...]] + [lz_in[k] for k in range(1, nz)])
    for k in range(1, NY):
        start(remote(ly_out, ly_in.at[k], sends.at[8], rls.at[1], y_at(k)))
    wait_for(ly_in.at[1:NY], rls.at[1])
    everything = functools.reduce(jnp.add, [ly_out[...]] + [ly_in[k] for k in range(1, NY)])
    loss[...] = jnp.broadcast_to(jnp.sum(everything[0:1], keepdims=True) / live.astype(F32), loss.shape)
    wait_for(ret.at[1:nl], rls.at[2])
    for s in range(nl):
        gtgt[s] = ret[slots[s] ^ lang]
    for h in (1, 0):
        gsrc[h * half : (h + 1) * half] = z_owned(h)
    sent = [xs.at[1:nz], ys.at[1:NY], staged.at[1:nl], rst_in.at[:, 1:nz], cst_in.at[1:NY]]
    sent += [xs.at[1:nz], ys.at[1:NY], lz_in.at[1:nz], ly_in.at[1:NY], back.at[1:nl]]
    for i, ref in enumerate(sent):
        wait_for(ref, sends.at[i])


def write_out(gsrc, gtgt, loss, gsrc_hbm, gtgt_hbm, loss_hbm, total, sem):
    copies = [pltpu.make_async_copy(gsrc, gsrc_hbm, sem.at[0]), pltpu.make_async_copy(gtgt, gtgt_hbm, sem.at[1])]
    for copy in copies:
        copy.start()
    total[0] = loss[0, 0]
    copies.append(pltpu.make_async_copy(total, loss_hbm, sem.at[2]))
    copies[2].start()
    for copy in copies:
        copy.wait()


def per_device(src_emb, tgt_emb, slot_group, counts, align, pair_weight):
    rows, width = src_emb.shape
    nl, per = tgt_emb.shape[0], tgt_emb.shape[1]
    nd = lax.axis_size("dp")
    nz = nd // NY
    cols = NY * rows
    half = rows // 2
    kz, ky = nz // 2 + 1, NY // 2 + 1
    vmem, smem, dma = pltpu.VMEM, pltpu.SMEM, pltpu.SemaphoreType.DMA
    in_vmem, in_smem = pl.BlockSpec(memory_space=vmem), pl.BlockSpec(memory_space=smem)
    scratch = [
        smem((nl,), jnp.int32), smem((nl,), jnp.int32), smem((nl,), F32),
        vmem((1, nd * rows), jnp.int32), vmem((nl, per, width), BF16),
        vmem((nz, rows, width), BF16), vmem((NY, rows, width), BF16), vmem((nl, per, width), BF16),
        vmem((nz, rows, rows), F32), vmem((8, rows), F32),
        vmem((nz, rows, cols), F32), vmem((nz, rows, cols), F32),
        vmem((nz, rows, rows), F32), vmem((nz, 8, cols), F32),
        vmem((nz, rows, cols), BF16), vmem((nz, rows, width), F32), vmem((NY, rows, width), F32),
        vmem((3, nz, rows), F32), vmem((3, nz, nz, rows), F32), vmem((8, rows), F32), vmem((NY, 8, rows), F32),
        vmem((8, rows), F32), vmem((nz, 8, rows), F32), vmem((8, rows), F32), vmem((NY, 8, rows), F32),
        vmem((2, kz, 2, half, width), BF16), vmem((2, kz, 2, half, width), BF16),
        vmem((2, ky, 2, half, width), BF16), vmem((2, ky, 2, half, width), BF16),
        vmem((nl, per, width), BF16), vmem((nl, per, width), BF16),
        dma((10,)), dma((4,)), dma((nz, 2)), dma((NY, 4)), dma((5,)), dma((1,)), dma((3,)),
        dma((2, nz // 2, 2)), dma((2, NY // 2, 2)), dma((6,)),
    ]
    found = tuple(
        pl.pallas_call(
            kernel,
            out_shape=(
                pltpu.VMEM((rows, width), BF16),
                pltpu.VMEM((nl, per, width), BF16),
                pltpu.VMEM((8, rows), F32),
            ),
            in_specs=[pl.BlockSpec(memory_space=pl.ANY)] * 6,
            out_specs=(in_vmem, in_vmem, in_vmem),
            scratch_shapes=scratch,
            compiler_params=pltpu.CompilerParams(
                collective_id=0, has_side_effects=True, vmem_limit_bytes=58 << 20
            ),
        )(slot_group, counts, pair_weight, align, src_emb, tgt_emb)
    )
    shapes = [(src_emb.shape, BF16), (tgt_emb.shape, BF16), ((1,), F32)]
    return pl.pallas_call(
        write_out,
        out_shape=tuple(jax.ShapeDtypeStruct(*shape) for shape in shapes),
        in_specs=[in_vmem] * 3,
        out_specs=(pl.BlockSpec(memory_space=pl.ANY),) * 3,
        scratch_shapes=[smem((1,), F32), dma((3,))],
    )(*(pltpu.with_memory_space_constraint(a, pltpu.VMEM) for a in found))


def solution(mesh):
    in_specs = (
        P(("lang", "dp"), None),
        P(None, ("lang", "dp"), None),
        P(),
        P(),
        P("lang", None),
        P(),
    )
    out_specs = (P(("lang", "dp"), None), P(None, ("lang", "dp"), None), P("lang"))
    return jax.shard_map(
        per_device, mesh=mesh, in_specs=in_specs, out_specs=out_specs, check_vma=False
    )
```

```python
import functools
import math

import jax
import jax.numpy as jnp
from jax import lax
from jax.experimental import pallas as pl
from jax.experimental.pallas import tpu as pltpu
from jax.sharding import PartitionSpec as P

MARGIN = 0.3
LOW = -1e30
NY = 4
F32 = jnp.float32
BF16 = jnp.bfloat16


def kernel(
    slots_hbm, counts_hbm, weights_hbm, align_hbm, x, t_hbm, gsrc, gtgt, loss,
    slots, counts, weights, align, t, xs, ys, staged, acol, colok, er, ec, rmax, cmax, gm, psrc, ptgt,
    rst_out, rst_in, cst_out, cst_in, lz_out, lz_in, ly_out, ly_in,
    fz_out, fz_in, fy_out, fy_in, back, ret,
    sends, ra, rgz, rgy, rrs, rcs, rls, rfz, rfy, fetched,
):
    nl, per = t.shape[0], t.shape[1]
    nz = xs.shape[0]
    rows, width = x.shape
    half = rows // 2
    inv_root = 1.0 / math.sqrt(width)
    lang, dp = lax.axis_index("lang"), lax.axis_index("dp")
    z, y = dp // NY, dp % NY

    def z_at(k):
        return {"dp": lax.rem(z + k + nz, nz) * NY + y}

    def y_at(k):
        return {"dp": z * NY + lax.rem(y + k + NY, NY)}

    def lang_at(p):
        return {"lang": lang ^ p}

    def remote(src, dst, send, recv, to):
        return pltpu.make_async_remote_copy(
            src_ref=src, dst_ref=dst, send_sem=send, recv_sem=recv,
            device_id=to, device_id_type=pl.DeviceIdType.MESH,
        )

    def start(copy):
        copy.start()
        return copy

    def wait_for(ref, sem):
        pltpu.make_async_copy(ref, ref, sem).wait()

    fetches = [
        pltpu.make_async_copy(src, dst, fetched.at[i])
        for i, (src, dst) in enumerate(
            [(x, xs.at[0]), (slots_hbm, slots), (t_hbm, t), (align_hbm, align), (counts_hbm, counts), (weights_hbm, weights)]
        )
    ]

    barrier = pltpu.get_barrier_semaphore()
    peers = [z_at(k) for k in range(1, nz)] + [y_at(k) for k in range(1, NY)]
    peers += [lang_at(k) for k in range(1, nl)]
    for to in peers:
        pl.semaphore_signal(barrier, inc=1, device_id=to, device_id_type=pl.DeviceIdType.MESH)
    for copy in fetches:
        copy.start()
    pl.semaphore_wait(barrier, len(peers))

    def gather_copies(first, buf, n, onward, send, recv, at):
        copies = {}
        chunks = len(onward[0]) + len(onward[1])
        size = rows // chunks
        for d in (0, 1):
            for k in range(n // 2):
                for c in range(chunks) if k < n // 2 - 1 else onward[d]:
                    part = pl.ds(c * size, size)
                    src, dst = (k, k + 1) if d == 0 else ((n - k) % n, n - 1 - k)
                    copies[d, k, c] = remote(
                        (buf.at[src] if k else first).at[part], buf.at[dst, part],
                        send, recv.at[dst, c], at(1 - 2 * d),
                    )
        return copies

    gz = gather_copies(x, xs, nz, ((0,), (1,)), sends.at[0], rgz, z_at)

    def z_begin():
        for h in (0, 1):
            start(gz[0, 0, h])
            start(gz[1, 0, 1 - h])

    z_begin()
    for copy in fetches[1:3]:
        copy.wait()
    for p in range(nl):
        group = lang ^ p
        slot = jnp.int32(0)
        for s in range(nl):
            slot = jnp.where(slots[s] == group, s, slot)
        if p == 0:
            ys[0, 0:per] = t[slot]
        else:
            staged[p] = t[slot]
    for p in (1, 4, 5, 2, 6, 3, 7):
        start(remote(staged.at[p], ys.at[0, pl.ds(p * per, per)], sends.at[2], ra.at[p // 2], lang_at(p)))
    gy = gather_copies(ys.at[0], ys, NY, ((0, 2), (1, 3)), sends.at[1], rgy, y_at)

    def y_first():
        wait_for(ys.at[0, pl.ds(per, per)], ra.at[0])
        for d in (0, 1):
            start(gy[d, 0, 0])

    y_first()
    for copy in fetches[0:1] + fetches[3:]:
        copy.wait()
    live = counts[lang]
    weight = weights[lang]

    lane = lax.broadcasted_iota(jnp.int32, (1, rows), 1)
    sub = lax.broadcasted_iota(jnp.int32, (rows, rows), 0)

    def target_of(q, position):
        source = lang ^ (position // per)
        return (source * (nz * NY) + z * NY + lax.rem(y - q + NY, NY)) * per + position % per

    def first_row(r):
        return (lax.rem(z - r + nz, nz) * NY + y) * rows

    def prepare():
        for q in range(NY):
            mine = target_of(q, sub)

            def seen(ch, so_far, mine=mine):
                at = pl.multiple_of(ch * rows, rows)
                own = align[0:1, pl.ds(at, rows)]
                own = jnp.where(lane + at < live, own, -1)
                return jnp.where(mine == own, 1.0, so_far)

            hit = lax.fori_loop(0, nz * NY, seen, jnp.zeros((rows, rows), F32))
            hit = jnp.broadcast_to(jnp.max(hit, axis=1, keepdims=True), (rows, rows))
            colok[q : q + 1] = hit.T[0:1]
        for r in range(nz):
            own = align[0:1, pl.ds(pl.multiple_of(first_row(r), rows), rows)]
            acol[r] = jnp.broadcast_to(own.astype(F32), (rows, rows)).T

    prepare()

    target_row = jnp.concatenate([target_of(q, lane) for q in range(NY)], axis=1).astype(F32)
    row_in = lax.broadcasted_iota(jnp.int32, (rows, 1), 0)

    def masks(r):
        column = acol[r][:, 0:1]
        pos = column == target_row
        row_ok = row_in + first_row(r) < live
        return pos, row_ok

    def all_targets():
        return ys[...].reshape(NY * rows, width)

    total_pos = [jnp.zeros((1, NY * rows), F32)]

    def scores(r, group):
        raw = lax.dot_general(
            xs[r], all_targets(), (((1,), (1,)), ((), ())), preferred_element_type=F32
        )
        pos, row_ok = masks(r)
        col_ok = jnp.concatenate([colok[q : q + 1] for q in range(NY)], axis=1) > 0.5
        s = raw * inv_root - jnp.where(pos, MARGIN, 0.0)
        total_pos[0] += jnp.sum(jnp.where(pos & row_ok, s, 0.0), axis=0, keepdims=True)
        s = jnp.where(row_ok & col_ok, s, LOW)
        top = jnp.max(s, axis=1, keepdims=True)
        e = jnp.exp(s - top)
        er[r] = e
        row_lse = top + jnp.log(jnp.sum(e, axis=1, keepdims=True))
        rmax[r] = jnp.broadcast_to(top, (rows, rows))
        rst_out[group, r : r + 1] = jnp.broadcast_to(row_lse, (rows, rows)).T[0:1]
        top = jnp.max(s, axis=0, keepdims=True)
        e = jnp.exp(s - top)
        ec[r] = e
        cmax[r, 0:1] = top
        cmax[r, 1:2] = top + jnp.log(jnp.sum(e, axis=0, keepdims=True))

    def z_step(k, h):
        for d in (0, 1):
            part = h if d == 0 else 1 - h
            if (d, k, part) in gz:
                gz[d, k, part].wait_recv()
                if (d, k + 1, part) in gz:
                    start(gz[d, k + 1, part])

    def rows_from(group, k):
        return 0 if group < 2 else min(k, nz - k)

    def send_rows(group):
        for k in range(1, nz):
            recv = rrs.at[rows_from(group, k)]
            start(remote(rst_out.at[group], rst_in.at[group, k], sends.at[3], recv, z_at(k)))

    def y_begin(c):
        wait_for(ys.at[0, pl.ds(2 * c * per, 2 * per)], ra.at[c])
        for d in (0, 1):
            start(gy[d, 0, c])

    def y_on(d, c):
        gy[d, 0, c].wait_recv()
        start(gy[d, 1, c])

    def y_rest(k):
        for d in (0, 1):
            for c in (d, d + 2) if k else (1 - d, 3 - d):
                gy[d, k, c].wait_recv()

    y_begin(1)
    z_step(0, 0)
    y_begin(3)
    z_step(0, 1)
    y_begin(2)
    y_on(0, 0)
    y_on(1, 1)
    z_step(1, 0)
    y_on(1, 3)
    y_on(0, 2)
    z_step(1, 1)
    y_rest(0)
    z_step(2, 0)
    y_rest(1)

    mid = nz // 2
    scores(0, 0)
    for r in (1, nz - 1):
        scores(r, 0)
    for r in (2, nz - 2):
        scores(r, 0)
    send_rows(0)
    z_step(2, 1)
    for r in (mid - 1, mid + 1):
        scores(r, 1)
    send_rows(1)
    z_step(3, 0)
    scores(mid, 2)

    parts = cmax[:, 1, :]
    top = jnp.max(parts, axis=0, keepdims=True)
    col_part = top + jnp.log(jnp.sum(jnp.exp(parts - top), axis=0, keepdims=True))
    for q in range(NY):
        cst_out[q : q + 1] = col_part[:, q * rows : (q + 1) * rows]
        cst_out[q + NY : q + NY + 1] = col_part[:, q * rows : (q + 1) * rows]
    for k in range(1, NY):
        start(remote(cst_out, cst_in.at[k], sends.at[4], rcs.at[0], y_at(k)))
    send_rows(2)

    def combine(pieces):
        top = functools.reduce(jnp.maximum, pieces)
        return top + jnp.log(functools.reduce(jnp.add, [jnp.exp(p - top) for p in pieces]))

    def turn(piece, k):
        return jnp.concatenate([piece[piece.shape[0] - k :], piece[: piece.shape[0] - k]], axis=0)

    def group_of(r):
        return {mid: 2, mid - 1: 1, mid + 1: 1}.get(r, 0)

    arrived = set()
    row_lses = {}

    def row_lse(r):
        if r in row_lses:
            return row_lses[r]
        pieces = [rst_out[group_of(r), r : r + 1]]
        for k in range(1, nz):
            there = (r - k) % nz
            group = group_of(there)
            which = rows_from(group, k)
            if which not in arrived:
                arrived.add(which)
                together = {0: rst_in.at[0:2, 1:nz], nz // 2: rst_in.at[2, 1:2]}
                wait_for(together.get(which, rst_in.at[2, 1:3]), rrs.at[which])
            pieces.append(rst_in[group, k, there : there + 1])
        row_lses[r] = combine(pieces)
        return row_lses[r]


    def row_gradient(r):
        pos, row_ok = masks(r)
        own = jnp.broadcast_to(row_lse(r), (rows, rows)).T
        by_row = jnp.where(row_ok, weight * jnp.exp(rmax[r] - own), 0.0)
        for q in range(NY):
            at = slice(q * rows, (q + 1) * rows)
            er[r, :, at] = er[r, :, at] * by_row - jnp.where(pos[:, at] & row_ok, 2.0 * weight, 0.0)

    row_gradient(mid)
    wait_for(cst_in.at[1:NY], rcs.at[0])
    col_lse = combine([cst_out[0:NY]] + [turn(cst_in[k, 0:NY], k) for k in range(1, NY)])

    def gradient(r):
        if r != mid:
            row_gradient(r)
        for q in range(NY):
            at = slice(q * rows, (q + 1) * rows)
            by_col = jnp.where(
                colok[q : q + 1] > 0.5, weight * jnp.exp(cmax[r, 0:1, at] - col_lse[q : q + 1]), 0.0
            )
            gm[r, :, at] = (er[r, :, at] + ec[r, :, at] * by_col).astype(BF16)

    def source_part(r):
        psrc[r] = jnp.dot(gm[r], all_targets(), preferred_element_type=F32)

    def target_part(q):
        ptgt[q] = lax.dot_general(
            gm[:, :, q * rows : (q + 1) * rows].reshape(nz * rows, rows),
            xs[...].reshape(nz * rows, width),
            (((0,), (0,)), ((), ())),
            preferred_element_type=F32,
        )

    def ring(part, n, out, inn, send, recv, at):
        last = n // 2
        copies = {}

        def slot(d, k):
            return (n - (last + 1 - k)) % n if d == 0 else last + 1 - k

        def step(d, k, h):
            begins = 1 if h == d else 2
            value = part[slot(d, k), h * half : (h + 1) * half]
            if k > begins:
                copies[d, k - 1, h].wait_recv()
                value = value + inn[d, k - 1, h].astype(F32)
            out[d, k, h] = value.astype(BF16)
            copies[d, k, h] = start(
                remote(out.at[d, k, h], inn.at[d, k, h], send, recv.at[d, k - 1, h], at(1 - 2 * d))
            )

        def owned(h):
            copies[0, last, h].wait_recv()
            copies[1, last, h].wait_recv()
            value = part[0, h * half : (h + 1) * half]
            value = value + inn[0, last, h].astype(F32) + inn[1, last, h].astype(F32)
            return (value * inv_root).astype(BF16)

        return step, owned

    z_send, z_owned = ring(psrc, nz, fz_out, fz_in, sends.at[5], rfz, z_at)
    y_send, y_owned = ring(ptgt, NY, fy_out, fy_in, sends.at[6], rfy, y_at)
    gradient(mid)
    source_part(mid)
    z_send(0, 1, 0)
    z_send(1, 1, 1)
    for r in (mid + 1, mid - 1):
        gradient(r)
        source_part(r)
    z_send(0, 2, 1)
    z_send(1, 2, 0)
    for r in (mid + 2, mid - 2, mid + 3, mid - 3, 0):
        gradient(r)
    target_part(NY // 2)
    y_send(0, 1, 0)
    y_send(1, 1, 1)
    z_send(0, 2, 0)
    z_send(1, 2, 1)
    for q in (1, 3):
        target_part(q)
    y_send(0, 2, 1)
    y_send(1, 2, 0)
    for r in (mid + 2, mid - 2):
        source_part(r)
    z_send(0, 3, 1)
    z_send(1, 3, 0)
    y_send(0, 2, 0)
    y_send(1, 2, 1)
    target_part(0)

    own_rows = jnp.where(lane + first_row(0) < live, row_lse(0), 0.0)
    own_cols = jnp.where(colok[0:1] > 0.5, col_lse[0:1], 0.0)
    pos_sum = functools.reduce(jnp.add, [total_pos[0][:, q * rows : (q + 1) * rows] for q in range(NY)])
    lz_out[...] = jnp.broadcast_to(own_rows + own_cols - 2.0 * pos_sum, lz_out.shape)
    for k in range(1, nz):
        start(remote(lz_out, lz_in.at[k], sends.at[7], rls.at[0], z_at(k)))
    z_send(0, 3, 0)
    z_send(1, 3, 1)
    for r in (mid + 3, mid - 3):
        source_part(r)

    def send_back(h):
        value = y_owned(h)
        for i in range(nl // 2):
            p = h * (nl // 2) + i
            if p == 0:
                ret[0] = value[0:per]
            else:
                back[p] = value[i * per : (i + 1) * per]
                start(remote(back.at[p], ret.at[p], sends.at[9], rls.at[2], lang_at(p)))

    z_send(0, 4, 1)
    z_send(1, 4, 0)
    send_back(1)
    send_back(0)
    z_send(0, 4, 0)
    z_send(1, 4, 1)
    source_part(0)
    wait_for(lz_in.at[1:nz], rls.at[0])
    ly_out[...] = functools.reduce(jnp.add, [lz_out[...]] + [lz_in[k] for k in range(1, nz)])
    for k in range(1, NY):
        start(remote(ly_out, ly_in.at[k], sends.at[8], rls.at[1], y_at(k)))
    wait_for(ly_in.at[1:NY], rls.at[1])
    everything = functools.reduce(jnp.add, [ly_out[...]] + [ly_in[k] for k in range(1, NY)])
    loss[...] = jnp.broadcast_to(jnp.sum(everything[0:1], keepdims=True) / live.astype(F32), loss.shape)
    wait_for(ret.at[1:nl], rls.at[2])
    for s in range(nl):
        gtgt[s] = ret[slots[s] ^ lang]
    for h in (1, 0):
        gsrc[h * half : (h + 1) * half] = z_owned(h)
    sent = [xs.at[1:nz], ys.at[1:NY], staged.at[1:nl], rst_in.at[:, 1:nz], cst_in.at[1:NY]]
    sent += [xs.at[1:nz], ys.at[1:NY], lz_in.at[1:nz], ly_in.at[1:NY], back.at[1:nl]]
    for i, ref in enumerate(sent):
        wait_for(ref, sends.at[i])


def write_out(gsrc, gtgt, loss, gsrc_hbm, gtgt_hbm, loss_hbm, total, sem):
    copies = [pltpu.make_async_copy(gsrc, gsrc_hbm, sem.at[0]), pltpu.make_async_copy(gtgt, gtgt_hbm, sem.at[1])]
    for copy in copies:
        copy.start()
    total[0] = loss[0, 0]
    copies.append(pltpu.make_async_copy(total, loss_hbm, sem.at[2]))
    copies[2].start()
    for copy in copies:
        copy.wait()


def per_device(src_emb, tgt_emb, slot_group, counts, align, pair_weight):
    rows, width = src_emb.shape
    nl, per = tgt_emb.shape[0], tgt_emb.shape[1]
    nd = lax.axis_size("dp")
    nz = nd // NY
    cols = NY * rows
    half = rows // 2
    kz, ky = nz // 2 + 1, NY // 2 + 1
    vmem, smem, dma = pltpu.VMEM, pltpu.SMEM, pltpu.SemaphoreType.DMA
    in_vmem, in_smem = pl.BlockSpec(memory_space=vmem), pl.BlockSpec(memory_space=smem)
    scratch = [
        smem((nl,), jnp.int32), smem((nl,), jnp.int32), smem((nl,), F32),
        vmem((1, nd * rows), jnp.int32), vmem((nl, per, width), BF16),
        vmem((nz, rows, width), BF16), vmem((NY, rows, width), BF16), vmem((nl, per, width), BF16),
        vmem((nz, rows, rows), F32), vmem((8, rows), F32),
        vmem((nz, rows, cols), F32), vmem((nz, rows, cols), F32),
        vmem((nz, rows, rows), F32), vmem((nz, 8, cols), F32),
        vmem((nz, rows, cols), BF16), vmem((nz, rows, width), F32), vmem((NY, rows, width), F32),
        vmem((3, nz, rows), F32), vmem((3, nz, nz, rows), F32), vmem((8, rows), F32), vmem((NY, 8, rows), F32),
        vmem((8, rows), F32), vmem((nz, 8, rows), F32), vmem((8, rows), F32), vmem((NY, 8, rows), F32),
        vmem((2, kz, 2, half, width), BF16), vmem((2, kz, 2, half, width), BF16),
        vmem((2, ky, 2, half, width), BF16), vmem((2, ky, 2, half, width), BF16),
        vmem((nl, per, width), BF16), vmem((nl, per, width), BF16),
        dma((10,)), dma((4,)), dma((nz, 2)), dma((NY, 4)), dma((5,)), dma((1,)), dma((3,)),
        dma((2, nz // 2, 2)), dma((2, NY // 2, 2)), dma((6,)),
    ]
    found = tuple(
        pl.pallas_call(
            kernel,
            out_shape=(
                pltpu.VMEM((rows, width), BF16),
                pltpu.VMEM((nl, per, width), BF16),
                pltpu.VMEM((8, rows), F32),
            ),
            in_specs=[pl.BlockSpec(memory_space=pl.ANY)] * 6,
            out_specs=(in_vmem, in_vmem, in_vmem),
            scratch_shapes=scratch,
            compiler_params=pltpu.CompilerParams(
                collective_id=0, has_side_effects=True, vmem_limit_bytes=58 << 20
            ),
        )(slot_group, counts, pair_weight, align, src_emb, tgt_emb)
    )
    shapes = [(src_emb.shape, BF16), (tgt_emb.shape, BF16), ((1,), F32)]
    return pl.pallas_call(
        write_out,
        out_shape=tuple(jax.ShapeDtypeStruct(*shape) for shape in shapes),
        in_specs=[in_vmem] * 3,
        out_specs=(pl.BlockSpec(memory_space=pl.ANY),) * 3,
        scratch_shapes=[smem((1,), F32), dma((3,))],
    )(*(pltpu.with_memory_space_constraint(a, pltpu.VMEM) for a in found))


def solution(mesh):
    in_specs = (
        P(("lang", "dp"), None),
        P(None, ("lang", "dp"), None),
        P(),
        P(),
        P("lang", None),
        P(),
    )
    out_specs = (P(("lang", "dp"), None), P(None, ("lang", "dp"), None), P("lang"))
    return jax.shard_map(
        per_device, mesh=mesh, in_specs=in_specs, out_specs=out_specs, check_vma=False
    )
```

```python
import functools
import math

import jax
import jax.numpy as jnp
from jax import lax
from jax.experimental import pallas as pl
from jax.experimental.pallas import tpu as pltpu
from jax.sharding import PartitionSpec as P

MARGIN = 0.3
LOW = -1e30
NY = 4
CZ = 4
F32 = jnp.float32
BF16 = jnp.bfloat16


def kernel(
    slots_hbm, counts_hbm, weights_hbm, align_hbm, x, t_hbm, gsrc, gtgt, loss,
    slots, counts, weights, align, t, xs, ys, staged, acol, colok, er, ec, rmax, cmax, gm, psrc, ptgt,
    rst_out, rst_in, cst_out, cst_in, lz_out, lz_in, ly_out, ly_in,
    fz_out, fz_in, fy_out, fy_in, back, ret,
    sends, ra, rgz, rgy, rrs, rcs, rls, rfz, rfy, fetched,
):
    nl, per = t.shape[0], t.shape[1]
    nz = xs.shape[0]
    rows, width = x.shape
    half = rows // 2
    cz = rgz.shape[1]
    inv_root = 1.0 / math.sqrt(width)
    lang, dp = lax.axis_index("lang"), lax.axis_index("dp")
    z, y = dp // NY, dp % NY

    def z_at(k):
        return {"dp": lax.rem(z + k + nz, nz) * NY + y}

    def y_at(k):
        return {"dp": z * NY + lax.rem(y + k + NY, NY)}

    def lang_at(p):
        return {"lang": lang ^ p}

    def remote(src, dst, send, recv, to):
        return pltpu.make_async_remote_copy(
            src_ref=src, dst_ref=dst, send_sem=send, recv_sem=recv,
            device_id=to, device_id_type=pl.DeviceIdType.MESH,
        )

    def start(copy):
        copy.start()
        return copy

    def wait_for(ref, sem):
        pltpu.make_async_copy(ref, ref, sem).wait()

    fetches = [
        pltpu.make_async_copy(src, dst, fetched.at[i])
        for i, (src, dst) in enumerate(
            [(x, xs.at[0]), (slots_hbm, slots), (t_hbm, t), (align_hbm, align), (counts_hbm, counts), (weights_hbm, weights)]
        )
    ]

    barrier = pltpu.get_barrier_semaphore()
    peers = [z_at(k) for k in range(1, nz)] + [y_at(k) for k in range(1, NY)]
    peers += [lang_at(k) for k in range(1, nl)]
    for to in peers:
        pl.semaphore_signal(barrier, inc=1, device_id=to, device_id_type=pl.DeviceIdType.MESH)
    for copy in fetches:
        copy.start()
    pl.semaphore_wait(barrier, len(peers))

    def gather_copies(first, buf, n, onward, send, recv, at):
        copies = {}
        chunks = len(onward[0]) + len(onward[1])
        size = rows // chunks
        for d in (0, 1):
            for k in range(n // 2):
                for c in range(chunks) if k < n // 2 - 1 else onward[d]:
                    part = pl.ds(c * size, size)
                    src, dst = (k, k + 1) if d == 0 else ((n - k) % n, n - 1 - k)
                    copies[d, k, c] = remote(
                        (buf.at[src] if k else first).at[part], buf.at[dst, part],
                        send, recv.at[dst, c], at(1 - 2 * d),
                    )
        return copies

    gz = gather_copies(x, xs, nz, (range(cz // 2), range(cz // 2, cz)), sends.at[0], rgz, z_at)

    def z_begin():
        for i in range(cz):
            start(gz[0, 0, i])
            start(gz[1, 0, cz - 1 - i])

    z_begin()
    for copy in fetches[1:3]:
        copy.wait()
    for p in range(nl):
        group = lang ^ p
        slot = jnp.int32(0)
        for s in range(nl):
            slot = jnp.where(slots[s] == group, s, slot)
        if p == 0:
            ys[0, 0:per] = t[slot]
        else:
            staged[p] = t[slot]
    for p in (1, 4, 5, 2, 6, 3, 7):
        start(remote(staged.at[p], ys.at[0, pl.ds(p * per, per)], sends.at[2], ra.at[p // 2], lang_at(p)))
    gy = gather_copies(ys.at[0], ys, NY, ((0, 2), (1, 3)), sends.at[1], rgy, y_at)

    def y_first():
        wait_for(ys.at[0, pl.ds(per, per)], ra.at[0])
        for d in (0, 1):
            start(gy[d, 0, 0])

    y_first()
    for copy in fetches[0:1] + fetches[3:]:
        copy.wait()
    live = counts[lang]
    weight = weights[lang]

    lane = lax.broadcasted_iota(jnp.int32, (1, rows), 1)
    sub = lax.broadcasted_iota(jnp.int32, (rows, rows), 0)

    def target_of(q, position):
        source = lang ^ (position // per)
        return (source * (nz * NY) + z * NY + lax.rem(y - q + NY, NY)) * per + position % per

    def first_row(r):
        return (lax.rem(z - r + nz, nz) * NY + y) * rows

    def prepare():
        for q in range(NY):
            mine = target_of(q, sub)

            def seen(ch, so_far, mine=mine):
                at = pl.multiple_of(ch * rows, rows)
                own = align[0:1, pl.ds(at, rows)]
                own = jnp.where(lane + at < live, own, -1)
                return jnp.where(mine == own, 1.0, so_far)

            hit = lax.fori_loop(0, nz * NY, seen, jnp.zeros((rows, rows), F32))
            hit = jnp.broadcast_to(jnp.max(hit, axis=1, keepdims=True), (rows, rows))
            colok[q : q + 1] = hit.T[0:1]
        for r in range(nz):
            own = align[0:1, pl.ds(pl.multiple_of(first_row(r), rows), rows)]
            acol[r] = jnp.broadcast_to(own.astype(F32), (rows, rows)).T

    prepare()

    target_row = jnp.concatenate([target_of(q, lane) for q in range(NY)], axis=1).astype(F32)
    row_in = lax.broadcasted_iota(jnp.int32, (rows, 1), 0)

    def masks(r):
        column = acol[r][:, 0:1]
        pos = column == target_row
        row_ok = row_in + first_row(r) < live
        return pos, row_ok

    def all_targets():
        return ys[...].reshape(NY * rows, width)

    total_pos = [jnp.zeros((1, NY * rows), F32)]

    def scores(r, group):
        raw = lax.dot_general(
            xs[r], all_targets(), (((1,), (1,)), ((), ())), preferred_element_type=F32
        )
        pos, row_ok = masks(r)
        col_ok = jnp.concatenate([colok[q : q + 1] for q in range(NY)], axis=1) > 0.5
        s = raw * inv_root - jnp.where(pos, MARGIN, 0.0)
        total_pos[0] += jnp.sum(jnp.where(pos & row_ok, s, 0.0), axis=0, keepdims=True)
        s = jnp.where(row_ok & col_ok, s, LOW)
        top = jnp.max(s, axis=1, keepdims=True)
        e = jnp.exp(s - top)
        er[r] = e
        row_lse = top + jnp.log(jnp.sum(e, axis=1, keepdims=True))
        rmax[r] = jnp.broadcast_to(top, (rows, rows))
        rst_out[group, r : r + 1] = jnp.broadcast_to(row_lse, (rows, rows)).T[0:1]
        top = jnp.max(s, axis=0, keepdims=True)
        e = jnp.exp(s - top)
        ec[r] = e
        cmax[r, 0:1] = top
        cmax[r, 1:2] = top + jnp.log(jnp.sum(e, axis=0, keepdims=True))

    def z_step(k, h):
        for i in range(h * cz // 2, (h + 1) * cz // 2):
            for d in (0, 1):
                part = i if d == 0 else cz - 1 - i
                if (d, k, part) in gz:
                    gz[d, k, part].wait_recv()
                    if (d, k + 1, part) in gz:
                        start(gz[d, k + 1, part])

    def rows_from(group, k):
        return 0 if group < 2 else min(k, nz - k)

    def send_rows(group):
        for k in range(1, nz):
            recv = rrs.at[rows_from(group, k)]
            start(remote(rst_out.at[group], rst_in.at[group, k], sends.at[3], recv, z_at(k)))

    def y_begin(c):
        wait_for(ys.at[0, pl.ds(2 * c * per, 2 * per)], ra.at[c])
        for d in (0, 1):
            start(gy[d, 0, c])

    def y_on(d, c):
        gy[d, 0, c].wait_recv()
        start(gy[d, 1, c])

    def y_rest(k):
        for d in (0, 1):
            for c in (d, d + 2) if k else (1 - d, 3 - d):
                gy[d, k, c].wait_recv()

    y_begin(1)
    z_step(0, 0)
    y_begin(3)
    z_step(0, 1)
    y_begin(2)
    y_on(0, 0)
    y_on(1, 1)
    z_step(1, 0)
    y_on(1, 3)
    y_on(0, 2)
    z_step(1, 1)
    y_rest(0)
    z_step(2, 0)
    y_rest(1)

    mid = nz // 2
    scores(0, 0)
    for r in (1, nz - 1):
        scores(r, 0)
    for r in (2, nz - 2):
        scores(r, 0)
    send_rows(0)
    z_step(2, 1)
    for r in (mid - 1, mid + 1):
        scores(r, 1)
    send_rows(1)
    z_step(3, 0)
    scores(mid, 2)

    parts = cmax[:, 1, :]
    top = jnp.max(parts, axis=0, keepdims=True)
    col_part = top + jnp.log(jnp.sum(jnp.exp(parts - top), axis=0, keepdims=True))
    for q in range(NY):
        cst_out[q : q + 1] = col_part[:, q * rows : (q + 1) * rows]
        cst_out[q + NY : q + NY + 1] = col_part[:, q * rows : (q + 1) * rows]
    for k in range(1, NY):
        start(remote(cst_out, cst_in.at[k], sends.at[4], rcs.at[0], y_at(k)))
    send_rows(2)

    def combine(pieces):
        top = functools.reduce(jnp.maximum, pieces)
        return top + jnp.log(functools.reduce(jnp.add, [jnp.exp(p - top) for p in pieces]))

    def turn(piece, k):
        return jnp.concatenate([piece[piece.shape[0] - k :], piece[: piece.shape[0] - k]], axis=0)

    def group_of(r):
        return {mid: 2, mid - 1: 1, mid + 1: 1}.get(r, 0)

    arrived = set()
    row_lses = {}

    def row_lse(r):
        if r in row_lses:
            return row_lses[r]
        pieces = [rst_out[group_of(r), r : r + 1]]
        for k in range(1, nz):
            there = (r - k) % nz
            group = group_of(there)
            which = rows_from(group, k)
            if which not in arrived:
                arrived.add(which)
                together = {0: rst_in.at[0:2, 1:nz], nz // 2: rst_in.at[2, 1:2]}
                wait_for(together.get(which, rst_in.at[2, 1:3]), rrs.at[which])
            pieces.append(rst_in[group, k, there : there + 1])
        row_lses[r] = combine(pieces)
        return row_lses[r]


    def row_gradient(r):
        pos, row_ok = masks(r)
        own = jnp.broadcast_to(row_lse(r), (rows, rows)).T
        by_row = jnp.where(row_ok, weight * jnp.exp(rmax[r] - own), 0.0)
        for q in range(NY):
            at = slice(q * rows, (q + 1) * rows)
            er[r, :, at] = er[r, :, at] * by_row - jnp.where(pos[:, at] & row_ok, 2.0 * weight, 0.0)

    row_gradient(mid)
    wait_for(cst_in.at[1:NY], rcs.at[0])
    col_lse = combine([cst_out[0:NY]] + [turn(cst_in[k, 0:NY], k) for k in range(1, NY)])

    def gradient(r):
        if r != mid:
            row_gradient(r)
        for q in range(NY):
            at = slice(q * rows, (q + 1) * rows)
            by_col = jnp.where(
                colok[q : q + 1] > 0.5, weight * jnp.exp(cmax[r, 0:1, at] - col_lse[q : q + 1]), 0.0
            )
            gm[r, :, at] = (er[r, :, at] + ec[r, :, at] * by_col).astype(BF16)

    def source_part(r):
        psrc[r] = jnp.dot(gm[r], all_targets(), preferred_element_type=F32)

    def target_part(q):
        ptgt[q] = lax.dot_general(
            gm[:, :, q * rows : (q + 1) * rows].reshape(nz * rows, rows),
            xs[...].reshape(nz * rows, width),
            (((0,), (0,)), ((), ())),
            preferred_element_type=F32,
        )

    def ring(part, n, out, inn, send, recv, at):
        last = n // 2
        copies = {}
        pieces = out.shape[2]
        size = rows // pieces

        def slot(d, k):
            return (n - (last + 1 - k)) % n if d == 0 else last + 1 - k

        def step(d, k, h):
            begins = 1 if h == d else 2
            for c in range(h * pieces // 2, (h + 1) * pieces // 2):
                value = part[slot(d, k), c * size : (c + 1) * size]
                if k > begins:
                    copies[d, k - 1, c].wait_recv()
                    value = value + inn[d, k - 1, c].astype(F32)
                out[d, k, c] = value.astype(BF16)
                copies[d, k, c] = start(
                    remote(out.at[d, k, c], inn.at[d, k, c], send, recv.at[d, k - 1, c], at(1 - 2 * d))
                )

        def owned(h):
            values = []
            for c in range(h * pieces // 2, (h + 1) * pieces // 2):
                copies[0, last, c].wait_recv()
                copies[1, last, c].wait_recv()
                value = part[0, c * size : (c + 1) * size]
                value = value + inn[0, last, c].astype(F32) + inn[1, last, c].astype(F32)
                values.append((value * inv_root).astype(BF16))
            return jnp.concatenate(values, axis=0)

        return step, owned

    z_send, z_owned = ring(psrc, nz, fz_out, fz_in, sends.at[5], rfz, z_at)
    y_send, y_owned = ring(ptgt, NY, fy_out, fy_in, sends.at[6], rfy, y_at)
    gradient(mid)
    source_part(mid)
    z_send(0, 1, 0)
    z_send(1, 1, 1)
    for r in (mid + 1, mid - 1):
        gradient(r)
        source_part(r)
    z_send(0, 2, 1)
    z_send(1, 2, 0)
    for r in (mid + 2, mid - 2, mid + 3, mid - 3, 0):
        gradient(r)
    target_part(NY // 2)
    y_send(0, 1, 0)
    y_send(1, 1, 1)
    z_send(0, 2, 0)
    z_send(1, 2, 1)
    for q in (1, 3):
        target_part(q)
    y_send(0, 2, 1)
    y_send(1, 2, 0)
    for r in (mid + 2, mid - 2):
        source_part(r)
    z_send(0, 3, 1)
    z_send(1, 3, 0)
    y_send(0, 2, 0)
    y_send(1, 2, 1)
    target_part(0)

    own_rows = jnp.where(lane + first_row(0) < live, row_lse(0), 0.0)
    own_cols = jnp.where(colok[0:1] > 0.5, col_lse[0:1], 0.0)
    pos_sum = functools.reduce(jnp.add, [total_pos[0][:, q * rows : (q + 1) * rows] for q in range(NY)])
    lz_out[...] = jnp.broadcast_to(own_rows + own_cols - 2.0 * pos_sum, lz_out.shape)
    for k in range(1, nz):
        start(remote(lz_out, lz_in.at[k], sends.at[7], rls.at[0], z_at(k)))
    z_send(0, 3, 0)
    z_send(1, 3, 1)
    for r in (mid + 3, mid - 3):
        source_part(r)

    def send_back(h):
        value = y_owned(h)
        for i in range(nl // 2):
            p = h * (nl // 2) + i
            if p == 0:
                ret[0] = value[0:per]
            else:
                back[p] = value[i * per : (i + 1) * per]
                start(remote(back.at[p], ret.at[p], sends.at[9], rls.at[2], lang_at(p)))

    send_back(1)
    send_back(0)
    z_send(0, 4, 1)
    z_send(1, 4, 0)
    z_send(0, 4, 0)
    z_send(1, 4, 1)
    source_part(0)
    wait_for(lz_in.at[1:nz], rls.at[0])
    ly_out[...] = functools.reduce(jnp.add, [lz_out[...]] + [lz_in[k] for k in range(1, nz)])
    for k in range(1, NY):
        start(remote(ly_out, ly_in.at[k], sends.at[8], rls.at[1], y_at(k)))
    wait_for(ly_in.at[1:NY], rls.at[1])
    everything = functools.reduce(jnp.add, [ly_out[...]] + [ly_in[k] for k in range(1, NY)])
    loss[...] = jnp.broadcast_to(jnp.sum(everything[0:1], keepdims=True) / live.astype(F32), loss.shape)
    wait_for(ret.at[1:nl], rls.at[2])
    for s in range(nl):
        gtgt[s] = ret[slots[s] ^ lang]
    for h in (1, 0):
        gsrc[h * half : (h + 1) * half] = z_owned(h)
    sent = [xs.at[1:nz], ys.at[1:NY], staged.at[1:nl], rst_in.at[:, 1:nz], cst_in.at[1:NY]]
    sent += [xs.at[1:nz], ys.at[1:NY], lz_in.at[1:nz], ly_in.at[1:NY], back.at[1:nl]]
    for i, ref in enumerate(sent):
        wait_for(ref, sends.at[i])


def write_out(gsrc, gtgt, loss, gsrc_hbm, gtgt_hbm, loss_hbm, total, sem):
    copies = [pltpu.make_async_copy(gsrc, gsrc_hbm, sem.at[0]), pltpu.make_async_copy(gtgt, gtgt_hbm, sem.at[1])]
    for copy in copies:
        copy.start()
    total[0] = loss[0, 0]
    copies.append(pltpu.make_async_copy(total, loss_hbm, sem.at[2]))
    copies[2].start()
    for copy in copies:
        copy.wait()


def per_device(src_emb, tgt_emb, slot_group, counts, align, pair_weight):
    rows, width = src_emb.shape
    nl, per = tgt_emb.shape[0], tgt_emb.shape[1]
    nd = lax.axis_size("dp")
    nz = nd // NY
    cols = NY * rows
    half = rows // 2
    kz, ky = nz // 2 + 1, NY // 2 + 1
    vmem, smem, dma = pltpu.VMEM, pltpu.SMEM, pltpu.SemaphoreType.DMA
    in_vmem, in_smem = pl.BlockSpec(memory_space=vmem), pl.BlockSpec(memory_space=smem)
    scratch = [
        smem((nl,), jnp.int32), smem((nl,), jnp.int32), smem((nl,), F32),
        vmem((1, nd * rows), jnp.int32), vmem((nl, per, width), BF16),
        vmem((nz, rows, width), BF16), vmem((NY, rows, width), BF16), vmem((nl, per, width), BF16),
        vmem((nz, rows, rows), F32), vmem((8, rows), F32),
        vmem((nz, rows, cols), F32), vmem((nz, rows, cols), F32),
        vmem((nz, rows, rows), F32), vmem((nz, 8, cols), F32),
        vmem((nz, rows, cols), BF16), vmem((nz, rows, width), F32), vmem((NY, rows, width), F32),
        vmem((3, nz, rows), F32), vmem((3, nz, nz, rows), F32), vmem((8, rows), F32), vmem((NY, 8, rows), F32),
        vmem((8, rows), F32), vmem((nz, 8, rows), F32), vmem((8, rows), F32), vmem((NY, 8, rows), F32),
        vmem((2, kz, CZ, rows // CZ, width), BF16), vmem((2, kz, CZ, rows // CZ, width), BF16),
        vmem((2, ky, 2, half, width), BF16), vmem((2, ky, 2, half, width), BF16),
        vmem((nl, per, width), BF16), vmem((nl, per, width), BF16),
        dma((10,)), dma((4,)), dma((nz, CZ)), dma((NY, 4)), dma((5,)), dma((1,)), dma((3,)),
        dma((2, nz // 2, CZ)), dma((2, NY // 2, 2)), dma((6,)),
    ]
    found = tuple(
        pl.pallas_call(
            kernel,
            out_shape=(
                pltpu.VMEM((rows, width), BF16),
                pltpu.VMEM((nl, per, width), BF16),
                pltpu.VMEM((8, rows), F32),
            ),
            in_specs=[pl.BlockSpec(memory_space=pl.ANY)] * 6,
            out_specs=(in_vmem, in_vmem, in_vmem),
            scratch_shapes=scratch,
            compiler_params=pltpu.CompilerParams(
                collective_id=0, has_side_effects=True, vmem_limit_bytes=58 << 20
            ),
        )(slot_group, counts, pair_weight, align, src_emb, tgt_emb)
    )
    shapes = [(src_emb.shape, BF16), (tgt_emb.shape, BF16), ((1,), F32)]
    return pl.pallas_call(
        write_out,
        out_shape=tuple(jax.ShapeDtypeStruct(*shape) for shape in shapes),
        in_specs=[in_vmem] * 3,
        out_specs=(pl.BlockSpec(memory_space=pl.ANY),) * 3,
        scratch_shapes=[smem((1,), F32), dma((3,))],
    )(*(pltpu.with_memory_space_constraint(a, pltpu.VMEM) for a in found))


def solution(mesh):
    in_specs = (
        P(("lang", "dp"), None),
        P(None, ("lang", "dp"), None),
        P(),
        P(),
        P("lang", None),
        P(),
    )
    out_specs = (P(("lang", "dp"), None), P(None, ("lang", "dp"), None), P("lang"))
    return jax.shard_map(
        per_device, mesh=mesh, in_specs=in_specs, out_specs=out_specs, check_vma=False
    )
```

```python
import functools
import math

import jax
import jax.numpy as jnp
from jax import lax
from jax.experimental import pallas as pl
from jax.experimental.pallas import tpu as pltpu
from jax.sharding import PartitionSpec as P

MARGIN = 0.3
LOW = -1e30
NY = 4
CZ = 4
F32 = jnp.float32
BF16 = jnp.bfloat16


def kernel(
    slots_hbm, counts_hbm, weights_hbm, align_hbm, x, t_hbm, gsrc, gtgt, loss,
    slots, counts, weights, align, t, xs, ys, staged, acol, colok, er, ec, rmax, cmax, gm, psrc, ptgt,
    rst_out, rst_in, cst_out, cst_in, lz_out, lz_in, ly_out, ly_in,
    fz_out, fz_in, fy_out, fy_in, back, ret,
    sends, ra, rgz, rgy, rrs, rcs, rls, rfz, rfy, fetched,
):
    nl, per = t.shape[0], t.shape[1]
    nz = xs.shape[0]
    rows, width = x.shape
    half = rows // 2
    cz = rgz.shape[1]
    inv_root = 1.0 / math.sqrt(width)
    lang, dp = lax.axis_index("lang"), lax.axis_index("dp")
    z, y = dp // NY, dp % NY

    def z_at(k):
        return {"dp": lax.rem(z + k + nz, nz) * NY + y}

    def y_at(k):
        return {"dp": z * NY + lax.rem(y + k + NY, NY)}

    def lang_at(p):
        return {"lang": lang ^ p}

    def remote(src, dst, send, recv, to):
        return pltpu.make_async_remote_copy(
            src_ref=src, dst_ref=dst, send_sem=send, recv_sem=recv,
            device_id=to, device_id_type=pl.DeviceIdType.MESH,
        )

    def start(copy):
        copy.start()
        return copy

    def wait_for(ref, sem):
        pltpu.make_async_copy(ref, ref, sem).wait()

    fetches = [
        pltpu.make_async_copy(src, dst, fetched.at[i])
        for i, (src, dst) in enumerate(
            [(x, xs.at[0]), (slots_hbm, slots), (t_hbm, t), (align_hbm, align), (counts_hbm, counts), (weights_hbm, weights)]
        )
    ]

    barrier = pltpu.get_barrier_semaphore()
    peers = [z_at(k) for k in range(1, nz)] + [y_at(k) for k in range(1, NY)]
    peers += [lang_at(k) for k in range(1, nl)]
    for to in peers:
        pl.semaphore_signal(barrier, inc=1, device_id=to, device_id_type=pl.DeviceIdType.MESH)
    for copy in fetches:
        copy.start()
    for copy in fetches[1:3]:
        copy.wait()
    for p in range(nl):
        group = lang ^ p
        slot = jnp.int32(0)
        for s in range(nl):
            slot = jnp.where(slots[s] == group, s, slot)
        if p == 0:
            ys[0, 0:per] = t[slot]
        else:
            staged[p] = t[slot]
    pl.semaphore_wait(barrier, len(peers))

    def gather_copies(first, buf, n, onward, send, recv, at):
        copies = {}
        chunks = len(onward[0]) + len(onward[1])
        size = rows // chunks
        for d in (0, 1):
            for k in range(n // 2):
                for c in range(chunks) if k < n // 2 - 1 else onward[d]:
                    part = pl.ds(c * size, size)
                    src, dst = (k, k + 1) if d == 0 else ((n - k) % n, n - 1 - k)
                    copies[d, k, c] = remote(
                        (buf.at[src] if k else first).at[part], buf.at[dst, part],
                        send, recv.at[dst, c], at(1 - 2 * d),
                    )
        return copies

    gz = gather_copies(x, xs, nz, (range(cz // 2), range(cz // 2, cz)), sends.at[0], rgz, z_at)

    def z_begin():
        for i in range(cz):
            start(gz[0, 0, i])
            start(gz[1, 0, cz - 1 - i])

    z_begin()
    for p in (1, 4, 5, 2, 6, 3, 7):
        start(remote(staged.at[p], ys.at[0, pl.ds(p * per, per)], sends.at[2], ra.at[p // 2], lang_at(p)))
    gy = gather_copies(ys.at[0], ys, NY, ((0, 2), (1, 3)), sends.at[1], rgy, y_at)

    def y_first():
        wait_for(ys.at[0, pl.ds(per, per)], ra.at[0])
        for d in (0, 1):
            start(gy[d, 0, 0])

    y_first()
    for copy in fetches[0:1] + fetches[3:]:
        copy.wait()
    live = counts[lang]
    weight = weights[lang]

    lane = lax.broadcasted_iota(jnp.int32, (1, rows), 1)
    sub = lax.broadcasted_iota(jnp.int32, (rows, rows), 0)

    def target_of(q, position):
        source = lang ^ (position // per)
        return (source * (nz * NY) + z * NY + lax.rem(y - q + NY, NY)) * per + position % per

    def first_row(r):
        return (lax.rem(z - r + nz, nz) * NY + y) * rows

    def prepare():
        for q in range(NY):
            mine = target_of(q, sub)

            def seen(ch, so_far, mine=mine):
                at = pl.multiple_of(ch * rows, rows)
                own = align[0:1, pl.ds(at, rows)]
                own = jnp.where(lane + at < live, own, -1)
                return jnp.where(mine == own, 1.0, so_far)

            hit = lax.fori_loop(0, nz * NY, seen, jnp.zeros((rows, rows), F32))
            hit = jnp.broadcast_to(jnp.max(hit, axis=1, keepdims=True), (rows, rows))
            colok[q : q + 1] = hit.T[0:1]
        for r in range(nz):
            own = align[0:1, pl.ds(pl.multiple_of(first_row(r), rows), rows)]
            acol[r] = jnp.broadcast_to(own.astype(F32), (rows, rows)).T

    prepare()

    target_row = jnp.concatenate([target_of(q, lane) for q in range(NY)], axis=1).astype(F32)
    row_in = lax.broadcasted_iota(jnp.int32, (rows, 1), 0)

    def masks(r):
        column = acol[r][:, 0:1]
        pos = column == target_row
        row_ok = row_in + first_row(r) < live
        return pos, row_ok

    def all_targets():
        return ys[...].reshape(NY * rows, width)

    total_pos = [jnp.zeros((1, NY * rows), F32)]

    def column_scores(r):
        raw = lax.dot_general(
            xs[r], all_targets(), (((1,), (1,)), ((), ())), preferred_element_type=F32
        )
        pos, row_ok = masks(r)
        col_ok = jnp.concatenate([colok[q : q + 1] for q in range(NY)], axis=1) > 0.5
        s = raw * inv_root - jnp.where(pos, MARGIN, 0.0)
        total_pos[0] += jnp.sum(jnp.where(pos & row_ok, s, 0.0), axis=0, keepdims=True)
        s = jnp.where(row_ok & col_ok, s, LOW)
        er[r] = s
        top = jnp.max(s, axis=0, keepdims=True)
        e = jnp.exp(s - top)
        ec[r] = e
        cmax[r, 0:1] = top
        cmax[r, 1:2] = top + jnp.log(jnp.sum(e, axis=0, keepdims=True))

    def row_scores(r, group):
        s = er[r]
        top = jnp.max(s, axis=1, keepdims=True)
        e = jnp.exp(s - top)
        er[r] = e
        row_lse = top + jnp.log(jnp.sum(e, axis=1, keepdims=True))
        rmax[r] = jnp.broadcast_to(top, (rows, rows))
        rst_out[group, r : r + 1] = jnp.broadcast_to(row_lse, (rows, rows)).T[0:1]

    def scores(r, group):
        column_scores(r)
        row_scores(r, group)

    def z_step(k, h):
        for i in range(h * cz // 2, (h + 1) * cz // 2):
            for d in (0, 1):
                part = i if d == 0 else cz - 1 - i
                if (d, k, part) in gz:
                    gz[d, k, part].wait_recv()
                    if (d, k + 1, part) in gz:
                        start(gz[d, k + 1, part])

    def rows_from(group, k):
        return 0 if group < 2 else min(k, nz - k)

    def send_rows(group):
        for k in range(1, nz):
            recv = rrs.at[rows_from(group, k)]
            start(remote(rst_out.at[group], rst_in.at[group, k], sends.at[3], recv, z_at(k)))

    def y_begin(c):
        wait_for(ys.at[0, pl.ds(2 * c * per, 2 * per)], ra.at[c])
        for d in (0, 1):
            start(gy[d, 0, c])

    def y_on(d, c):
        gy[d, 0, c].wait_recv()
        start(gy[d, 1, c])

    def y_rest(k):
        for d in (0, 1):
            for c in (d, d + 2) if k else (1 - d, 3 - d):
                gy[d, k, c].wait_recv()

    y_begin(1)
    z_step(0, 0)
    y_begin(3)
    z_step(0, 1)
    y_begin(2)
    y_on(0, 0)
    y_on(1, 1)
    z_step(1, 0)
    y_on(1, 3)
    y_on(0, 2)
    z_step(1, 1)
    y_rest(0)
    z_step(2, 0)
    y_rest(1)

    mid = nz // 2
    scores(0, 0)
    for r in (1, nz - 1):
        scores(r, 0)
    for r in (2, nz - 2):
        scores(r, 0)
    send_rows(0)
    z_step(2, 1)
    for r in (mid - 1, mid + 1):
        scores(r, 1)
    send_rows(1)
    z_step(3, 0)
    column_scores(mid)

    parts = cmax[:, 1, :]
    top = jnp.max(parts, axis=0, keepdims=True)
    col_part = top + jnp.log(jnp.sum(jnp.exp(parts - top), axis=0, keepdims=True))
    for q in range(NY):
        cst_out[q : q + 1] = col_part[:, q * rows : (q + 1) * rows]
        cst_out[q + NY : q + NY + 1] = col_part[:, q * rows : (q + 1) * rows]
    for k in range(1, NY):
        start(remote(cst_out, cst_in.at[k], sends.at[4], rcs.at[0], y_at(k)))
    row_scores(mid, 2)
    send_rows(2)

    def combine(pieces):
        top = functools.reduce(jnp.maximum, pieces)
        return top + jnp.log(functools.reduce(jnp.add, [jnp.exp(p - top) for p in pieces]))

    def turn(piece, k):
        return jnp.concatenate([piece[piece.shape[0] - k :], piece[: piece.shape[0] - k]], axis=0)

    def group_of(r):
        return {mid: 2, mid - 1: 1, mid + 1: 1}.get(r, 0)

    arrived = set()
    row_lses = {}

    def row_lse(r):
        if r in row_lses:
            return row_lses[r]
        pieces = [rst_out[group_of(r), r : r + 1]]
        for k in range(1, nz):
            there = (r - k) % nz
            group = group_of(there)
            which = rows_from(group, k)
            if which not in arrived:
                arrived.add(which)
                together = {0: rst_in.at[0:2, 1:nz], nz // 2: rst_in.at[2, 1:2]}
                wait_for(together.get(which, rst_in.at[2, 1:3]), rrs.at[which])
            pieces.append(rst_in[group, k, there : there + 1])
        row_lses[r] = combine(pieces)
        return row_lses[r]


    def row_gradient(r):
        pos, row_ok = masks(r)
        own = jnp.broadcast_to(row_lse(r), (rows, rows)).T
        by_row = jnp.where(row_ok, weight * jnp.exp(rmax[r] - own), 0.0)
        for q in range(NY):
            at = slice(q * rows, (q + 1) * rows)
            er[r, :, at] = er[r, :, at] * by_row - jnp.where(pos[:, at] & row_ok, 2.0 * weight, 0.0)

    row_gradient(mid)
    wait_for(cst_in.at[1:NY], rcs.at[0])
    col_lse = combine([cst_out[0:NY]] + [turn(cst_in[k, 0:NY], k) for k in range(1, NY)])

    def gradient(r):
        if r != mid:
            row_gradient(r)
        for q in range(NY):
            at = slice(q * rows, (q + 1) * rows)
            by_col = jnp.where(
                colok[q : q + 1] > 0.5, weight * jnp.exp(cmax[r, 0:1, at] - col_lse[q : q + 1]), 0.0
            )
            gm[r, :, at] = (er[r, :, at] + ec[r, :, at] * by_col).astype(BF16)

    def source_part(r):
        psrc[r] = jnp.dot(gm[r], all_targets(), preferred_element_type=F32)

    def target_part(q):
        ptgt[q] = lax.dot_general(
            gm[:, :, q * rows : (q + 1) * rows].reshape(nz * rows, rows),
            xs[...].reshape(nz * rows, width),
            (((0,), (0,)), ((), ())),
            preferred_element_type=F32,
        )

    def ring(part, n, out, inn, send, recv, at):
        last = n // 2
        copies = {}
        pieces = out.shape[2]
        size = rows // pieces

        def slot(d, k):
            return (n - (last + 1 - k)) % n if d == 0 else last + 1 - k

        def step(k, h):
            for i in range(pieces // 2):
                for d in (0, 1):
                    c = (h if d == 0 else 1 - h) * pieces // 2 + i
                    value = part[slot(d, k), c * size : (c + 1) * size]
                    if k > 1 + h:
                        copies[d, k - 1, c].wait_recv()
                        value = value + inn[d, k - 1, c].astype(F32)
                    out[d, k, c] = value.astype(BF16)
                    copies[d, k, c] = start(
                        remote(out.at[d, k, c], inn.at[d, k, c], send, recv.at[d, k - 1, c], at(1 - 2 * d))
                    )

        def owned(h):
            values = []
            for c in range(h * pieces // 2, (h + 1) * pieces // 2):
                copies[0, last, c].wait_recv()
                copies[1, last, c].wait_recv()
                value = part[0, c * size : (c + 1) * size]
                value = value + inn[0, last, c].astype(F32) + inn[1, last, c].astype(F32)
                values.append((value * inv_root).astype(BF16))
            return jnp.concatenate(values, axis=0)

        return step, owned

    z_send, z_owned = ring(psrc, nz, fz_out, fz_in, sends.at[5], rfz, z_at)
    y_send, y_owned = ring(ptgt, NY, fy_out, fy_in, sends.at[6], rfy, y_at)
    gradient(mid)
    source_part(mid)
    z_send(1, 0)
    for r in (mid + 1, mid - 1):
        gradient(r)
        source_part(r)
    z_send(2, 1)
    for r in (mid + 2, mid - 2, mid + 3, mid - 3, 0):
        gradient(r)
    target_part(NY // 2)
    y_send(1, 0)
    z_send(2, 0)
    for q in (1, 3):
        target_part(q)
    y_send(2, 1)
    for r in (mid + 2, mid - 2):
        source_part(r)
    z_send(3, 1)
    y_send(2, 0)
    target_part(0)

    own_rows = jnp.where(lane + first_row(0) < live, row_lse(0), 0.0)
    own_cols = jnp.where(colok[0:1] > 0.5, col_lse[0:1], 0.0)
    pos_sum = functools.reduce(jnp.add, [total_pos[0][:, q * rows : (q + 1) * rows] for q in range(NY)])
    lz_out[...] = jnp.broadcast_to(own_rows + own_cols - 2.0 * pos_sum, lz_out.shape)
    for k in range(1, nz):
        start(remote(lz_out, lz_in.at[k], sends.at[7], rls.at[0], z_at(k)))
    z_send(3, 0)
    for r in (mid + 3, mid - 3):
        source_part(r)

    def send_back(h):
        value = y_owned(h)
        for i in range(nl // 2):
            p = h * (nl // 2) + i
            if p == 0:
                ret[0] = value[0:per]
            else:
                back[p] = value[i * per : (i + 1) * per]
                start(remote(back.at[p], ret.at[p], sends.at[9], rls.at[2], lang_at(p)))

    send_back(1)
    send_back(0)
    z_send(4, 1)
    z_send(4, 0)
    source_part(0)
    wait_for(lz_in.at[1:nz], rls.at[0])
    ly_out[...] = functools.reduce(jnp.add, [lz_out[...]] + [lz_in[k] for k in range(1, nz)])
    for k in range(1, NY):
        start(remote(ly_out, ly_in.at[k], sends.at[8], rls.at[1], y_at(k)))
    wait_for(ly_in.at[1:NY], rls.at[1])
    everything = functools.reduce(jnp.add, [ly_out[...]] + [ly_in[k] for k in range(1, NY)])
    loss[...] = jnp.broadcast_to(jnp.sum(everything[0:1], keepdims=True) / live.astype(F32), loss.shape)
    wait_for(ret.at[1:nl], rls.at[2])
    for s in range(nl):
        gtgt[s] = ret[slots[s] ^ lang]
    for h in (1, 0):
        gsrc[h * half : (h + 1) * half] = z_owned(h)
    sent = [xs.at[1:nz], ys.at[1:NY], staged.at[1:nl], rst_in.at[:, 1:nz], cst_in.at[1:NY]]
    sent += [xs.at[1:nz], ys.at[1:NY], lz_in.at[1:nz], ly_in.at[1:NY], back.at[1:nl]]
    for i, ref in enumerate(sent):
        wait_for(ref, sends.at[i])


def write_out(gsrc, gtgt, loss, gsrc_hbm, gtgt_hbm, loss_hbm, total, sem):
    copies = [pltpu.make_async_copy(gsrc, gsrc_hbm, sem.at[0]), pltpu.make_async_copy(gtgt, gtgt_hbm, sem.at[1])]
    for copy in copies:
        copy.start()
    total[0] = loss[0, 0]
    copies.append(pltpu.make_async_copy(total, loss_hbm, sem.at[2]))
    copies[2].start()
    for copy in copies:
        copy.wait()


def per_device(src_emb, tgt_emb, slot_group, counts, align, pair_weight):
    rows, width = src_emb.shape
    nl, per = tgt_emb.shape[0], tgt_emb.shape[1]
    nd = lax.axis_size("dp")
    nz = nd // NY
    cols = NY * rows
    half = rows // 2
    kz, ky = nz // 2 + 1, NY // 2 + 1
    vmem, smem, dma = pltpu.VMEM, pltpu.SMEM, pltpu.SemaphoreType.DMA
    in_vmem, in_smem = pl.BlockSpec(memory_space=vmem), pl.BlockSpec(memory_space=smem)
    scratch = [
        smem((nl,), jnp.int32), smem((nl,), jnp.int32), smem((nl,), F32),
        vmem((1, nd * rows), jnp.int32), vmem((nl, per, width), BF16),
        vmem((nz, rows, width), BF16), vmem((NY, rows, width), BF16), vmem((nl, per, width), BF16),
        vmem((nz, rows, rows), F32), vmem((8, rows), F32),
        vmem((nz, rows, cols), F32), vmem((nz, rows, cols), F32),
        vmem((nz, rows, rows), F32), vmem((nz, 8, cols), F32),
        vmem((nz, rows, cols), BF16), vmem((nz, rows, width), F32), vmem((NY, rows, width), F32),
        vmem((3, nz, rows), F32), vmem((3, nz, nz, rows), F32), vmem((8, rows), F32), vmem((NY, 8, rows), F32),
        vmem((8, rows), F32), vmem((nz, 8, rows), F32), vmem((8, rows), F32), vmem((NY, 8, rows), F32),
        vmem((2, kz, CZ, rows // CZ, width), BF16), vmem((2, kz, CZ, rows // CZ, width), BF16),
        vmem((2, ky, 2, half, width), BF16), vmem((2, ky, 2, half, width), BF16),
        vmem((nl, per, width), BF16), vmem((nl, per, width), BF16),
        dma((10,)), dma((4,)), dma((nz, CZ)), dma((NY, 4)), dma((5,)), dma((1,)), dma((3,)),
        dma((2, nz // 2, CZ)), dma((2, NY // 2, 2)), dma((6,)),
    ]
    found = tuple(
        pl.pallas_call(
            kernel,
            out_shape=(
                pltpu.VMEM((rows, width), BF16),
                pltpu.VMEM((nl, per, width), BF16),
                pltpu.VMEM((8, rows), F32),
            ),
            in_specs=[pl.BlockSpec(memory_space=pl.ANY)] * 6,
            out_specs=(in_vmem, in_vmem, in_vmem),
            scratch_shapes=scratch,
            compiler_params=pltpu.CompilerParams(
                collective_id=0, has_side_effects=True, vmem_limit_bytes=58 << 20
            ),
        )(slot_group, counts, pair_weight, align, src_emb, tgt_emb)
    )
    shapes = [(src_emb.shape, BF16), (tgt_emb.shape, BF16), ((1,), F32)]
    return pl.pallas_call(
        write_out,
        out_shape=tuple(jax.ShapeDtypeStruct(*shape) for shape in shapes),
        in_specs=[in_vmem] * 3,
        out_specs=(pl.BlockSpec(memory_space=pl.ANY),) * 3,
        scratch_shapes=[smem((1,), F32), dma((3,))],
    )(*(pltpu.with_memory_space_constraint(a, pltpu.VMEM) for a in found))


def solution(mesh):
    in_specs = (
        P(("lang", "dp"), None),
        P(None, ("lang", "dp"), None),
        P(),
        P(),
        P("lang", None),
        P(),
    )
    out_specs = (P(("lang", "dp"), None), P(None, ("lang", "dp"), None), P("lang"))
    return jax.shard_map(
        per_device, mesh=mesh, in_specs=in_specs, out_specs=out_specs, check_vma=False
    )
```

```python
import functools
import math

import jax
import jax.numpy as jnp
from jax import lax
from jax.experimental import pallas as pl
from jax.experimental.pallas import tpu as pltpu
from jax.sharding import PartitionSpec as P

MARGIN = 0.3
LOW = -1e30
NY = 4
CZ = 4
F32 = jnp.float32
BF16 = jnp.bfloat16


def kernel(
    slots_hbm, counts_hbm, weights_hbm, align_hbm, x, t_hbm, gsrc, gtgt, loss,
    slots, counts, weights, align, t, xs, ys, staged, acol, colok, er, ec, rmax, cmax, gm, psrc, ptgt,
    rst_out, rst_in, cst_out, cst_in, lz_out, lz_in, ly_out, ly_in,
    fz_out, fz_in, fy_out, fy_in, back, ret,
    sends, ra, rgz, rgy, rrs, rcs, rls, rfz, rfy, fetched,
):
    nl, per = t.shape[0], t.shape[1]
    nz = xs.shape[0]
    rows, width = x.shape
    half = rows // 2
    cz = rgz.shape[1]
    inv_root = 1.0 / math.sqrt(width)
    lang, dp = lax.axis_index("lang"), lax.axis_index("dp")
    z, y = dp // NY, dp % NY

    def z_at(k):
        return {"dp": lax.rem(z + k + nz, nz) * NY + y}

    def y_at(k):
        return {"dp": z * NY + lax.rem(y + k + NY, NY)}

    def lang_at(p):
        return {"lang": lang ^ p}

    def remote(src, dst, send, recv, to):
        return pltpu.make_async_remote_copy(
            src_ref=src, dst_ref=dst, send_sem=send, recv_sem=recv,
            device_id=to, device_id_type=pl.DeviceIdType.MESH,
        )

    def start(copy):
        copy.start()
        return copy

    def wait_for(ref, sem):
        pltpu.make_async_copy(ref, ref, sem).wait()

    fetches = [
        pltpu.make_async_copy(src, dst, fetched.at[i])
        for i, (src, dst) in enumerate(
            [(x, xs.at[0]), (slots_hbm, slots), (t_hbm, t), (align_hbm, align), (counts_hbm, counts), (weights_hbm, weights)]
        )
    ]

    barrier = pltpu.get_barrier_semaphore()
    peers = [z_at(k) for k in range(1, nz)] + [y_at(k) for k in range(1, NY)]
    peers += [lang_at(k) for k in range(1, nl)]
    for to in peers:
        pl.semaphore_signal(barrier, inc=1, device_id=to, device_id_type=pl.DeviceIdType.MESH)
    for copy in fetches:
        copy.start()
    for copy in fetches[1:3]:
        copy.wait()
    for p in range(nl):
        group = lang ^ p
        slot = jnp.int32(0)
        for s in range(nl):
            slot = jnp.where(slots[s] == group, s, slot)
        if p == 0:
            ys[0, 0:per] = t[slot]
        else:
            staged[p] = t[slot]
    pl.semaphore_wait(barrier, len(peers))

    def gather_copies(first, buf, n, onward, send, recv, at):
        copies = {}
        chunks = len(onward[0]) + len(onward[1])
        size = rows // chunks
        for d in (0, 1):
            for k in range(n // 2):
                for c in range(chunks) if k < n // 2 - 1 else onward[d]:
                    part = pl.ds(c * size, size)
                    src, dst = (k, k + 1) if d == 0 else ((n - k) % n, n - 1 - k)
                    copies[d, k, c] = remote(
                        (buf.at[src] if k else first).at[part], buf.at[dst, part],
                        send, recv.at[dst, c], at(1 - 2 * d),
                    )
        return copies

    gz = gather_copies(x, xs, nz, (range(cz // 2), range(cz // 2, cz)), sends.at[0], rgz, z_at)

    def z_begin():
        for i in range(cz):
            start(gz[0, 0, i])
            start(gz[1, 0, cz - 1 - i])

    z_begin()
    for p in (1, 4, 5, 2, 6, 3, 7):
        start(remote(staged.at[p], ys.at[0, pl.ds(p * per, per)], sends.at[2], ra.at[p // 2], lang_at(p)))
    gy = gather_copies(ys.at[0], ys, NY, ((0, 2), (1, 3)), sends.at[1], rgy, y_at)

    def y_first():
        wait_for(ys.at[0, pl.ds(per, per)], ra.at[0])
        for d in (0, 1):
            start(gy[d, 0, 0])

    y_first()
    for copy in fetches[0:1] + fetches[3:]:
        copy.wait()
    live = counts[lang]
    weight = weights[lang]

    lane = lax.broadcasted_iota(jnp.int32, (1, rows), 1)
    sub = lax.broadcasted_iota(jnp.int32, (rows, rows), 0)

    def target_of(q, position):
        source = lang ^ (position // per)
        return (source * (nz * NY) + z * NY + lax.rem(y - q + NY, NY)) * per + position % per

    def first_row(r):
        return (lax.rem(z - r + nz, nz) * NY + y) * rows

    def prepare():
        for q in range(NY):
            mine = target_of(q, sub)

            def seen(ch, so_far, mine=mine):
                at = pl.multiple_of(ch * rows, rows)
                own = align[0:1, pl.ds(at, rows)]
                own = jnp.where(lane + at < live, own, -1)
                return jnp.where(mine == own, 1.0, so_far)

            hit = lax.fori_loop(0, nz * NY, seen, jnp.zeros((rows, rows), F32))
            hit = jnp.broadcast_to(jnp.max(hit, axis=1, keepdims=True), (rows, rows))
            colok[q : q + 1] = hit.T[0:1]
        for r in range(nz):
            own = align[0:1, pl.ds(pl.multiple_of(first_row(r), rows), rows)]
            acol[r] = jnp.broadcast_to(own.astype(F32), (rows, rows)).T

    prepare()

    target_row = jnp.concatenate([target_of(q, lane) for q in range(NY)], axis=1).astype(F32)
    row_in = lax.broadcasted_iota(jnp.int32, (rows, 1), 0)

    def masks(r):
        column = acol[r][:, 0:1]
        pos = column == target_row
        row_ok = row_in + first_row(r) < live
        return pos, row_ok

    def all_targets():
        return ys[...].reshape(NY * rows, width)

    total_pos = [jnp.zeros((1, NY * rows), F32)]

    def column_scores(r):
        raw = lax.dot_general(
            xs[r], all_targets(), (((1,), (1,)), ((), ())), preferred_element_type=F32
        )
        pos, row_ok = masks(r)
        col_ok = jnp.concatenate([colok[q : q + 1] for q in range(NY)], axis=1) > 0.5
        s = raw * inv_root - jnp.where(pos, MARGIN, 0.0)
        total_pos[0] += jnp.sum(jnp.where(pos & row_ok, s, 0.0), axis=0, keepdims=True)
        s = jnp.where(row_ok & col_ok, s, LOW)
        er[r] = s
        top = jnp.max(s, axis=0, keepdims=True)
        e = jnp.exp(s - top)
        ec[r] = e
        cmax[r, 0:1] = top
        cmax[r, 1:2] = top + jnp.log(jnp.sum(e, axis=0, keepdims=True))

    def row_scores(r, group):
        s = er[r]
        top = jnp.max(s, axis=1, keepdims=True)
        e = jnp.exp(s - top)
        er[r] = e
        row_lse = top + jnp.log(jnp.sum(e, axis=1, keepdims=True))
        rmax[r] = jnp.broadcast_to(top, (rows, rows))
        rst_out[group, r : r + 1] = jnp.broadcast_to(row_lse, (rows, rows)).T[0:1]

    def scores(r, group):
        column_scores(r)
        row_scores(r, group)

    def z_step(k, h):
        for i in range(h * cz // 2, (h + 1) * cz // 2):
            for d in (0, 1):
                part = i if d == 0 else cz - 1 - i
                if (d, k, part) in gz:
                    gz[d, k, part].wait_recv()
                    if (d, k + 1, part) in gz:
                        start(gz[d, k + 1, part])

    def rows_from(group, k):
        return 0 if group < 2 else min(k, nz - k)

    def send_rows(group):
        for k in range(1, nz):
            recv = rrs.at[rows_from(group, k)]
            start(remote(rst_out.at[group], rst_in.at[group, k], sends.at[3], recv, z_at(k)))

    def y_begin(c):
        wait_for(ys.at[0, pl.ds(2 * c * per, 2 * per)], ra.at[c])
        for d in (0, 1):
            start(gy[d, 0, c])

    def y_on(d, c):
        gy[d, 0, c].wait_recv()
        start(gy[d, 1, c])

    def y_rest(k):
        for d in (0, 1):
            for c in (d, d + 2) if k else (1 - d, 3 - d):
                gy[d, k, c].wait_recv()

    y_begin(1)
    z_step(0, 0)
    y_begin(3)
    z_step(0, 1)
    y_begin(2)
    y_on(0, 0)
    y_on(1, 1)
    z_step(1, 0)
    y_on(1, 3)
    y_on(0, 2)
    z_step(1, 1)
    y_rest(0)
    z_step(2, 0)
    y_rest(1)

    mid = nz // 2
    scores(0, 0)
    for r in (1, nz - 1):
        scores(r, 0)
    for r in (2, nz - 2):
        scores(r, 0)
    send_rows(0)
    z_step(2, 1)
    for r in (mid - 1, mid + 1):
        scores(r, 1)
    send_rows(1)
    z_step(3, 0)
    column_scores(mid)

    parts = cmax[:, 1, :]
    top = jnp.max(parts, axis=0, keepdims=True)
    col_part = top + jnp.log(jnp.sum(jnp.exp(parts - top), axis=0, keepdims=True))
    for q in range(NY):
        cst_out[q : q + 1] = col_part[:, q * rows : (q + 1) * rows]
        cst_out[q + NY : q + NY + 1] = col_part[:, q * rows : (q + 1) * rows]
    for k in range(1, NY):
        start(remote(cst_out, cst_in.at[k], sends.at[4], rcs.at[0], y_at(k)))
    row_scores(mid, 2)
    send_rows(2)

    def combine(pieces):
        top = functools.reduce(jnp.maximum, pieces)
        return top + jnp.log(functools.reduce(jnp.add, [jnp.exp(p - top) for p in pieces]))

    def turn(piece, k):
        return jnp.concatenate([piece[piece.shape[0] - k :], piece[: piece.shape[0] - k]], axis=0)

    def group_of(r):
        return {mid: 2, mid - 1: 1, mid + 1: 1}.get(r, 0)

    arrived = set()
    row_lses = {}

    def row_lse(r):
        if r in row_lses:
            return row_lses[r]
        pieces = [rst_out[group_of(r), r : r + 1]]
        for k in range(1, nz):
            there = (r - k) % nz
            group = group_of(there)
            which = rows_from(group, k)
            if which not in arrived:
                arrived.add(which)
                together = {0: rst_in.at[0:2, 1:nz], nz // 2: rst_in.at[2, 1:2]}
                wait_for(together.get(which, rst_in.at[2, 1:3]), rrs.at[which])
            pieces.append(rst_in[group, k, there : there + 1])
        row_lses[r] = combine(pieces)
        return row_lses[r]


    def row_gradient(r):
        pos, row_ok = masks(r)
        own = jnp.broadcast_to(row_lse(r), (rows, rows)).T
        by_row = jnp.where(row_ok, weight * jnp.exp(rmax[r] - own), 0.0)
        for q in range(NY):
            at = slice(q * rows, (q + 1) * rows)
            er[r, :, at] = er[r, :, at] * by_row - jnp.where(pos[:, at] & row_ok, 2.0 * weight, 0.0)

    row_gradient(mid)
    wait_for(cst_in.at[1:NY], rcs.at[0])
    col_lse = combine([cst_out[0:NY]] + [turn(cst_in[k, 0:NY], k) for k in range(1, NY)])

    def gradient(r):
        if r != mid:
            row_gradient(r)
        for q in range(NY):
            at = slice(q * rows, (q + 1) * rows)
            by_col = jnp.where(
                colok[q : q + 1] > 0.5, weight * jnp.exp(cmax[r, 0:1, at] - col_lse[q : q + 1]), 0.0
            )
            gm[r, :, at] = (er[r, :, at] + ec[r, :, at] * by_col).astype(BF16)

    def source_part(r):
        psrc[r] = jnp.dot(gm[r], all_targets(), preferred_element_type=F32)

    def target_part(q):
        ptgt[q] = lax.dot_general(
            gm[:, :, q * rows : (q + 1) * rows].reshape(nz * rows, rows),
            xs[...].reshape(nz * rows, width),
            (((0,), (0,)), ((), ())),
            preferred_element_type=F32,
        )

    def ring(part, n, out, inn, send, recv, at):
        last = n // 2
        copies = {}
        pieces = out.shape[2]
        size = rows // pieces

        def slot(d, k):
            return (n - (last + 1 - k)) % n if d == 0 else last + 1 - k

        def step(k, h):
            for i in range(pieces // 2):
                for d in (0, 1):
                    c = (h if d == 0 else 1 - h) * pieces // 2 + i
                    value = part[slot(d, k), c * size : (c + 1) * size]
                    if k > 1 + h:
                        copies[d, k - 1, c].wait_recv()
                        value = value + inn[d, k - 1, c].astype(F32)
                    out[d, k, c] = value.astype(BF16)
                    copies[d, k, c] = start(
                        remote(out.at[d, k, c], inn.at[d, k, c], send, recv.at[d, k - 1, c], at(1 - 2 * d))
                    )

        def owned(h):
            values = []
            for c in range(h * pieces // 2, (h + 1) * pieces // 2):
                copies[0, last, c].wait_recv()
                copies[1, last, c].wait_recv()
                value = part[0, c * size : (c + 1) * size]
                value = value + inn[0, last, c].astype(F32) + inn[1, last, c].astype(F32)
                values.append((value * inv_root).astype(BF16))
            return jnp.concatenate(values, axis=0)

        return step, owned

    z_send, z_owned = ring(psrc, nz, fz_out, fz_in, sends.at[5], rfz, z_at)
    y_send, y_owned = ring(ptgt, NY, fy_out, fy_in, sends.at[6], rfy, y_at)
    gradient(mid)
    source_part(mid)
    z_send(1, 0)
    for r in (mid + 1, mid - 1):
        gradient(r)
        source_part(r)
    z_send(2, 1)
    for r in (mid + 2, mid - 2, mid + 3, mid - 3, 0):
        gradient(r)
    target_part(NY // 2)
    y_send(1, 0)
    z_send(2, 0)
    for q in (1, 3):
        target_part(q)
    y_send(2, 1)
    for r in (mid + 2, mid - 2):
        source_part(r)
    z_send(3, 1)
    y_send(2, 0)
    target_part(0)

    own_rows = jnp.where(lane + first_row(0) < live, row_lse(0), 0.0)
    own_cols = jnp.where(colok[0:1] > 0.5, col_lse[0:1], 0.0)
    pos_sum = functools.reduce(jnp.add, [total_pos[0][:, q * rows : (q + 1) * rows] for q in range(NY)])
    lz_out[...] = jnp.broadcast_to(own_rows + own_cols - 2.0 * pos_sum, lz_out.shape)
    for k in range(1, nz):
        start(remote(lz_out, lz_in.at[k], sends.at[7], rls.at[0], z_at(k)))
    z_send(3, 0)
    for r in (mid + 3, mid - 3):
        source_part(r)

    def send_back(h):
        value = y_owned(h)
        for i in range(nl // 2):
            p = h * (nl // 2) + i
            if p == 0:
                ret[0] = value[0:per]
            else:
                back[p] = value[i * per : (i + 1) * per]
                start(remote(back.at[p], ret.at[p], sends.at[9], rls.at[2], lang_at(p)))

    send_back(1)
    send_back(0)
    z_send(4, 1)
    z_send(4, 0)
    source_part(0)
    wait_for(lz_in.at[1:nz], rls.at[0])
    ly_out[...] = functools.reduce(jnp.add, [lz_out[...]] + [lz_in[k] for k in range(1, nz)])
    for k in range(1, NY):
        start(remote(ly_out, ly_in.at[k], sends.at[8], rls.at[1], y_at(k)))
    wait_for(ly_in.at[1:NY], rls.at[1])
    everything = functools.reduce(jnp.add, [ly_out[...]] + [ly_in[k] for k in range(1, NY)])
    loss[...] = jnp.broadcast_to(jnp.sum(everything[0:1], keepdims=True) / live.astype(F32), loss.shape)
    wait_for(ret.at[1:nl], rls.at[2])
    for s in range(nl):
        gtgt[s] = ret[slots[s] ^ lang]
    for h in (1, 0):
        gsrc[h * half : (h + 1) * half] = z_owned(h)
    sent = [xs.at[1:nz], ys.at[1:NY], staged.at[1:nl], rst_in.at[:, 1:nz], cst_in.at[1:NY]]
    sent += [xs.at[1:nz], ys.at[1:NY], lz_in.at[1:nz], ly_in.at[1:NY], back.at[1:nl]]
    for i, ref in enumerate(sent):
        wait_for(ref, sends.at[i])


def write_out(gsrc, gtgt, loss, gsrc_hbm, gtgt_hbm, loss_hbm, total, sem):
    copies = [pltpu.make_async_copy(gsrc, gsrc_hbm, sem.at[0]), pltpu.make_async_copy(gtgt, gtgt_hbm, sem.at[1])]
    for copy in copies:
        copy.start()
    total[0] = loss[0, 0]
    copies.append(pltpu.make_async_copy(total, loss_hbm, sem.at[2]))
    copies[2].start()
    for copy in copies:
        copy.wait()


def per_device(src_emb, tgt_emb, slot_group, counts, align, pair_weight):
    rows, width = src_emb.shape
    nl, per = tgt_emb.shape[0], tgt_emb.shape[1]
    nd = lax.axis_size("dp")
    nz = nd // NY
    cols = NY * rows
    half = rows // 2
    kz, ky = nz // 2 + 1, NY // 2 + 1
    vmem, smem, dma = pltpu.VMEM, pltpu.SMEM, pltpu.SemaphoreType.DMA
    in_vmem, in_smem = pl.BlockSpec(memory_space=vmem), pl.BlockSpec(memory_space=smem)
    scratch = [
        smem((nl,), jnp.int32), smem((nl,), jnp.int32), smem((nl,), F32),
        vmem((1, nd * rows), jnp.int32), vmem((nl, per, width), BF16),
        vmem((nz, rows, width), BF16), vmem((NY, rows, width), BF16), vmem((nl, per, width), BF16),
        vmem((nz, rows, rows), F32), vmem((8, rows), F32),
        vmem((nz, rows, cols), F32), vmem((nz, rows, cols), F32),
        vmem((nz, rows, rows), F32), vmem((nz, 8, cols), F32),
        vmem((nz, rows, cols), BF16), vmem((nz, rows, width), F32), vmem((NY, rows, width), F32),
        vmem((3, nz, rows), F32), vmem((3, nz, nz, rows), F32), vmem((8, rows), F32), vmem((NY, 8, rows), F32),
        vmem((8, rows), F32), vmem((nz, 8, rows), F32), vmem((8, rows), F32), vmem((NY, 8, rows), F32),
        vmem((2, kz, CZ, rows // CZ, width), BF16), vmem((2, kz, CZ, rows // CZ, width), BF16),
        vmem((2, ky, 4, half // 2, width), BF16), vmem((2, ky, 4, half // 2, width), BF16),
        vmem((nl, per, width), BF16), vmem((nl, per, width), BF16),
        dma((10,)), dma((4,)), dma((nz, CZ)), dma((NY, 4)), dma((5,)), dma((1,)), dma((3,)),
        dma((2, nz // 2, CZ)), dma((2, NY // 2, 4)), dma((6,)),
    ]
    found = tuple(
        pl.pallas_call(
            kernel,
            out_shape=(
                pltpu.VMEM((rows, width), BF16),
                pltpu.VMEM((nl, per, width), BF16),
                pltpu.VMEM((8, rows), F32),
            ),
            in_specs=[pl.BlockSpec(memory_space=pl.ANY)] * 6,
            out_specs=(in_vmem, in_vmem, in_vmem),
            scratch_shapes=scratch,
            compiler_params=pltpu.CompilerParams(
                collective_id=0, has_side_effects=True, vmem_limit_bytes=58 << 20
            ),
        )(slot_group, counts, pair_weight, align, src_emb, tgt_emb)
    )
    shapes = [(src_emb.shape, BF16), (tgt_emb.shape, BF16), ((1,), F32)]
    return pl.pallas_call(
        write_out,
        out_shape=tuple(jax.ShapeDtypeStruct(*shape) for shape in shapes),
        in_specs=[in_vmem] * 3,
        out_specs=(pl.BlockSpec(memory_space=pl.ANY),) * 3,
        scratch_shapes=[smem((1,), F32), dma((3,))],
    )(*(pltpu.with_memory_space_constraint(a, pltpu.VMEM) for a in found))


def solution(mesh):
    in_specs = (
        P(("lang", "dp"), None),
        P(None, ("lang", "dp"), None),
        P(),
        P(),
        P("lang", None),
        P(),
    )
    out_specs = (P(("lang", "dp"), None), P(None, ("lang", "dp"), None), P("lang"))
    return jax.shard_map(
        per_device, mesh=mesh, in_specs=in_specs, out_specs=out_specs, check_vma=False
    )
```

```python
import functools
import math

import jax
import jax.numpy as jnp
from jax import lax
from jax.experimental import pallas as pl
from jax.experimental.pallas import tpu as pltpu
from jax.sharding import PartitionSpec as P

MARGIN = 0.3
LOW = -1e30
NY = 4
CZ = 4
F32 = jnp.float32
BF16 = jnp.bfloat16


def kernel(
    slots_hbm, counts_hbm, weights_hbm, align_hbm, x, t_hbm, gsrc, gtgt, loss,
    slots, counts, weights, align, t, xs, ys, staged, acol, colok, er, ec, rmax, cmax, gm, psrc, ptgt,
    rst_out, rst_in, cst_out, cst_in, lz_out, lz_in, ly_out, ly_in,
    fz_out, fz_in, fy_out, fy_in, back, ret,
    sends, ra, rgz, rgy, rrs, rcs, rls, rfz, rfy, fetched,
):
    nl, per = t.shape[0], t.shape[1]
    nz = xs.shape[0]
    rows, width = x.shape
    half = rows // 2
    cz = rgz.shape[1]
    inv_root = 1.0 / math.sqrt(width)
    lang, dp = lax.axis_index("lang"), lax.axis_index("dp")
    z, y = dp // NY, dp % NY

    def z_at(k):
        return {"dp": lax.rem(z + k + nz, nz) * NY + y}

    def y_at(k):
        return {"dp": z * NY + lax.rem(y + k + NY, NY)}

    def lang_at(p):
        return {"lang": lang ^ p}

    def remote(src, dst, send, recv, to):
        return pltpu.make_async_remote_copy(
            src_ref=src, dst_ref=dst, send_sem=send, recv_sem=recv,
            device_id=to, device_id_type=pl.DeviceIdType.MESH,
        )

    def start(copy):
        copy.start()
        return copy

    def wait_for(ref, sem):
        pltpu.make_async_copy(ref, ref, sem).wait()

    fetches = [
        pltpu.make_async_copy(src, dst, fetched.at[i])
        for i, (src, dst) in enumerate(
            [(x, xs.at[0]), (slots_hbm, slots), (t_hbm, t), (align_hbm, align), (counts_hbm, counts), (weights_hbm, weights)]
        )
    ]

    barrier = pltpu.get_barrier_semaphore()
    peers = [z_at(k) for k in range(1, nz)] + [y_at(k) for k in range(1, NY)]
    peers += [lang_at(k) for k in range(1, nl)]
    for to in peers:
        pl.semaphore_signal(barrier, inc=1, device_id=to, device_id_type=pl.DeviceIdType.MESH)
    for copy in fetches:
        copy.start()
    for copy in fetches[1:3]:
        copy.wait()
    for p in range(nl):
        group = lang ^ p
        slot = jnp.int32(0)
        for s in range(nl):
            slot = jnp.where(slots[s] == group, s, slot)
        if p == 0:
            ys[0, 0:per] = t[slot]
        else:
            staged[p] = t[slot]
    pl.semaphore_wait(barrier, len(peers))

    def gather_copies(first, buf, n, onward, send, recv, at):
        copies = {}
        chunks = len(onward[0]) + len(onward[1])
        size = rows // chunks
        for d in (0, 1):
            for k in range(n // 2):
                for c in range(chunks) if k < n // 2 - 1 else onward[d]:
                    part = pl.ds(c * size, size)
                    src, dst = (k, k + 1) if d == 0 else ((n - k) % n, n - 1 - k)
                    copies[d, k, c] = remote(
                        (buf.at[src] if k else first).at[part], buf.at[dst, part],
                        send, recv.at[dst, c], at(1 - 2 * d),
                    )
        return copies

    gz = gather_copies(x, xs, nz, (range(cz // 2), range(cz // 2, cz)), sends.at[0], rgz, z_at)

    def z_begin():
        for i in range(cz):
            start(gz[0, 0, i])
            start(gz[1, 0, cz - 1 - i])

    z_begin()
    for p in (1, 4, 5, 2, 6, 3, 7):
        start(remote(staged.at[p], ys.at[0, pl.ds(p * per, per)], sends.at[2], ra.at[p // 2], lang_at(p)))
    gy = gather_copies(ys.at[0], ys, NY, ((0, 2), (1, 3)), sends.at[1], rgy, y_at)

    def y_first():
        wait_for(ys.at[0, pl.ds(per, per)], ra.at[0])
        for d in (0, 1):
            start(gy[d, 0, 0])

    y_first()
    for copy in fetches[0:1] + fetches[3:]:
        copy.wait()
    live = counts[lang]
    weight = weights[lang]

    lane = lax.broadcasted_iota(jnp.int32, (1, rows), 1)
    sub = lax.broadcasted_iota(jnp.int32, (rows, rows), 0)

    def target_of(q, position):
        source = lang ^ (position // per)
        return (source * (nz * NY) + z * NY + lax.rem(y - q + NY, NY)) * per + position % per

    def first_row(r):
        return (lax.rem(z - r + nz, nz) * NY + y) * rows

    def prepare():
        for q in range(NY):
            mine = target_of(q, sub)

            def seen(ch, so_far, mine=mine):
                at = pl.multiple_of(ch * rows, rows)
                own = align[0:1, pl.ds(at, rows)]
                own = jnp.where(lane + at < live, own, -1)
                return jnp.where(mine == own, 1.0, so_far)

            hit = lax.fori_loop(0, nz * NY, seen, jnp.zeros((rows, rows), F32))
            hit = jnp.broadcast_to(jnp.max(hit, axis=1, keepdims=True), (rows, rows))
            colok[q : q + 1] = hit.T[0:1]
        for r in range(nz):
            own = align[0:1, pl.ds(pl.multiple_of(first_row(r), rows), rows)]
            acol[r] = jnp.broadcast_to(own.astype(F32), (rows, rows)).T

    prepare()

    target_row = jnp.concatenate([target_of(q, lane) for q in range(NY)], axis=1).astype(F32)
    row_in = lax.broadcasted_iota(jnp.int32, (rows, 1), 0)

    def masks(r):
        column = acol[r][:, 0:1]
        pos = column == target_row
        row_ok = row_in + first_row(r) < live
        return pos, row_ok

    def all_targets():
        return ys[...].reshape(NY * rows, width)

    total_pos = [jnp.zeros((1, NY * rows), F32)]

    def column_scores(r):
        raw = lax.dot_general(
            xs[r], all_targets(), (((1,), (1,)), ((), ())), preferred_element_type=F32
        )
        pos, row_ok = masks(r)
        col_ok = jnp.concatenate([colok[q : q + 1] for q in range(NY)], axis=1) > 0.5
        s = raw * inv_root - jnp.where(pos, MARGIN, 0.0)
        total_pos[0] += jnp.sum(jnp.where(pos & row_ok, s, 0.0), axis=0, keepdims=True)
        s = jnp.where(row_ok & col_ok, s, LOW)
        er[r] = s
        top = jnp.max(s, axis=0, keepdims=True)
        e = jnp.exp(s - top)
        ec[r] = e
        cmax[r, 0:1] = top
        cmax[r, 1:2] = top + jnp.log(jnp.sum(e, axis=0, keepdims=True))

    def row_scores(r, group):
        s = er[r]
        top = jnp.max(s, axis=1, keepdims=True)
        e = jnp.exp(s - top)
        er[r] = e
        row_lse = top + jnp.log(jnp.sum(e, axis=1, keepdims=True))
        rmax[r] = jnp.broadcast_to(top, (rows, rows))
        rst_out[group, r : r + 1] = jnp.broadcast_to(row_lse, (rows, rows)).T[0:1]

    def scores(r, group):
        column_scores(r)
        row_scores(r, group)

    def z_step(k, h):
        for i in range(h * cz // 2, (h + 1) * cz // 2):
            for d in (0, 1):
                part = i if d == 0 else cz - 1 - i
                if (d, k, part) in gz:
                    gz[d, k, part].wait_recv()
                    if (d, k + 1, part) in gz:
                        start(gz[d, k + 1, part])

    def rows_from(group, k):
        return 0 if group < 2 else min(k, nz - k)

    def send_rows(group):
        for k in range(1, nz):
            recv = rrs.at[rows_from(group, k)]
            start(remote(rst_out.at[group], rst_in.at[group, k], sends.at[3], recv, z_at(k)))

    def y_begin(c):
        wait_for(ys.at[0, pl.ds(2 * c * per, 2 * per)], ra.at[c])
        for d in (0, 1):
            start(gy[d, 0, c])

    def y_on(d, c):
        gy[d, 0, c].wait_recv()
        start(gy[d, 1, c])

    def y_rest(k):
        for d in (0, 1):
            for c in (d, d + 2) if k else (1 - d, 3 - d):
                gy[d, k, c].wait_recv()

    y_begin(1)
    z_step(0, 0)
    y_begin(3)
    z_step(0, 1)
    y_begin(2)
    z_step(1, 0)
    y_on(0, 0)
    y_on(1, 1)
    y_on(1, 3)
    y_on(0, 2)
    z_step(1, 1)
    y_rest(0)
    z_step(2, 0)
    y_rest(1)

    mid = nz // 2
    scores(0, 0)
    for r in (1, nz - 1):
        scores(r, 0)
    for r in (2, nz - 2):
        scores(r, 0)
    send_rows(0)
    z_step(2, 1)
    for r in (mid - 1, mid + 1):
        scores(r, 1)
    send_rows(1)
    z_step(3, 0)
    column_scores(mid)

    parts = cmax[:, 1, :]
    top = jnp.max(parts, axis=0, keepdims=True)
    col_part = top + jnp.log(jnp.sum(jnp.exp(parts - top), axis=0, keepdims=True))
    for q in range(NY):
        cst_out[q : q + 1] = col_part[:, q * rows : (q + 1) * rows]
        cst_out[q + NY : q + NY + 1] = col_part[:, q * rows : (q + 1) * rows]
    for k in range(1, NY):
        start(remote(cst_out, cst_in.at[k], sends.at[4], rcs.at[0], y_at(k)))
    row_scores(mid, 2)
    send_rows(2)

    def combine(pieces):
        top = functools.reduce(jnp.maximum, pieces)
        return top + jnp.log(functools.reduce(jnp.add, [jnp.exp(p - top) for p in pieces]))

    def turn(piece, k):
        return jnp.concatenate([piece[piece.shape[0] - k :], piece[: piece.shape[0] - k]], axis=0)

    def group_of(r):
        return {mid: 2, mid - 1: 1, mid + 1: 1}.get(r, 0)

    arrived = set()
    row_lses = {}

    def row_lse(r):
        if r in row_lses:
            return row_lses[r]
        pieces = [rst_out[group_of(r), r : r + 1]]
        for k in range(1, nz):
            there = (r - k) % nz
            group = group_of(there)
            which = rows_from(group, k)
            if which not in arrived:
                arrived.add(which)
                together = {0: rst_in.at[0:2, 1:nz], nz // 2: rst_in.at[2, 1:2]}
                wait_for(together.get(which, rst_in.at[2, 1:3]), rrs.at[which])
            pieces.append(rst_in[group, k, there : there + 1])
        row_lses[r] = combine(pieces)
        return row_lses[r]


    def row_gradient(r):
        pos, row_ok = masks(r)
        own = jnp.broadcast_to(row_lse(r), (rows, rows)).T
        by_row = jnp.where(row_ok, weight * jnp.exp(rmax[r] - own), 0.0)
        for q in range(NY):
            at = slice(q * rows, (q + 1) * rows)
            er[r, :, at] = er[r, :, at] * by_row - jnp.where(pos[:, at] & row_ok, 2.0 * weight, 0.0)

    row_gradient(mid)
    wait_for(cst_in.at[1:NY], rcs.at[0])
    col_lse = combine([cst_out[0:NY]] + [turn(cst_in[k, 0:NY], k) for k in range(1, NY)])

    def gradient(r):
        if r != mid:
            row_gradient(r)
        for q in range(NY):
            at = slice(q * rows, (q + 1) * rows)
            by_col = jnp.where(
                colok[q : q + 1] > 0.5, weight * jnp.exp(cmax[r, 0:1, at] - col_lse[q : q + 1]), 0.0
            )
            gm[r, :, at] = (er[r, :, at] + ec[r, :, at] * by_col).astype(BF16)

    def source_part(r):
        psrc[r] = jnp.dot(gm[r], all_targets(), preferred_element_type=F32)

    def target_part(q):
        ptgt[q] = lax.dot_general(
            gm[:, :, q * rows : (q + 1) * rows].reshape(nz * rows, rows),
            xs[...].reshape(nz * rows, width),
            (((0,), (0,)), ((), ())),
            preferred_element_type=F32,
        )

    def ring(part, n, out, inn, send, recv, at):
        last = n // 2
        copies = {}
        pieces = out.shape[2]
        size = rows // pieces

        def slot(d, k):
            return (n - (last + 1 - k)) % n if d == 0 else last + 1 - k

        def step(k, h):
            for i in range(pieces // 2):
                for d in (0, 1):
                    c = (h if d == 0 else 1 - h) * pieces // 2 + i
                    value = part[slot(d, k), c * size : (c + 1) * size]
                    if k > 1 + h:
                        copies[d, k - 1, c].wait_recv()
                        value = value + inn[d, k - 1, c].astype(F32)
                    out[d, k, c] = value.astype(BF16)
                    copies[d, k, c] = start(
                        remote(out.at[d, k, c], inn.at[d, k, c], send, recv.at[d, k - 1, c], at(1 - 2 * d))
                    )

        def owned(h):
            values = []
            for c in range(h * pieces // 2, (h + 1) * pieces // 2):
                copies[0, last, c].wait_recv()
                copies[1, last, c].wait_recv()
                value = part[0, c * size : (c + 1) * size]
                value = value + inn[0, last, c].astype(F32) + inn[1, last, c].astype(F32)
                values.append((value * inv_root).astype(BF16))
            return jnp.concatenate(values, axis=0)

        return step, owned

    z_send, z_owned = ring(psrc, nz, fz_out, fz_in, sends.at[5], rfz, z_at)
    y_send, y_owned = ring(ptgt, NY, fy_out, fy_in, sends.at[6], rfy, y_at)
    gradient(mid)
    source_part(mid)
    z_send(1, 0)
    for r in (mid + 1, mid - 1):
        gradient(r)
        source_part(r)
    z_send(2, 1)
    for r in (mid + 2, mid - 2, mid + 3, mid - 3, 0):
        gradient(r)
    target_part(NY // 2)
    y_send(1, 0)
    z_send(2, 0)
    for q in (1, 3):
        target_part(q)
    y_send(2, 1)
    for r in (mid + 2, mid - 2):
        source_part(r)
    z_send(3, 1)
    y_send(2, 0)
    target_part(0)

    own_rows = jnp.where(lane + first_row(0) < live, row_lse(0), 0.0)
    own_cols = jnp.where(colok[0:1] > 0.5, col_lse[0:1], 0.0)
    pos_sum = functools.reduce(jnp.add, [total_pos[0][:, q * rows : (q + 1) * rows] for q in range(NY)])
    lz_out[...] = jnp.broadcast_to(own_rows + own_cols - 2.0 * pos_sum, lz_out.shape)
    for k in range(1, nz):
        start(remote(lz_out, lz_in.at[k], sends.at[7], rls.at[0], z_at(k)))
    z_send(3, 0)
    for r in (mid + 3, mid - 3):
        source_part(r)

    def send_back(h):
        value = y_owned(h)
        for i in range(nl // 2):
            p = h * (nl // 2) + i
            if p == 0:
                ret[0] = value[0:per]
            else:
                back[p] = value[i * per : (i + 1) * per]
                start(remote(back.at[p], ret.at[p], sends.at[9], rls.at[2], lang_at(p)))

    send_back(1)
    send_back(0)
    z_send(4, 1)
    z_send(4, 0)
    source_part(0)
    wait_for(lz_in.at[1:nz], rls.at[0])
    ly_out[...] = functools.reduce(jnp.add, [lz_out[...]] + [lz_in[k] for k in range(1, nz)])
    for k in range(1, NY):
        start(remote(ly_out, ly_in.at[k], sends.at[8], rls.at[1], y_at(k)))
    wait_for(ly_in.at[1:NY], rls.at[1])
    everything = functools.reduce(jnp.add, [ly_out[...]] + [ly_in[k] for k in range(1, NY)])
    loss[...] = jnp.broadcast_to(jnp.sum(everything[0:1], keepdims=True) / live.astype(F32), loss.shape)
    wait_for(ret.at[1:nl], rls.at[2])
    for s in range(nl):
        gtgt[s] = ret[slots[s] ^ lang]
    for h in (1, 0):
        gsrc[h * half : (h + 1) * half] = z_owned(h)
    sent = [xs.at[1:nz], ys.at[1:NY], staged.at[1:nl], rst_in.at[:, 1:nz], cst_in.at[1:NY]]
    sent += [xs.at[1:nz], ys.at[1:NY], lz_in.at[1:nz], ly_in.at[1:NY], back.at[1:nl]]
    for i, ref in enumerate(sent):
        wait_for(ref, sends.at[i])


def write_out(gsrc, gtgt, loss, gsrc_hbm, gtgt_hbm, loss_hbm, total, sem):
    copies = [pltpu.make_async_copy(gsrc, gsrc_hbm, sem.at[0]), pltpu.make_async_copy(gtgt, gtgt_hbm, sem.at[1])]
    for copy in copies:
        copy.start()
    total[0] = loss[0, 0]
    copies.append(pltpu.make_async_copy(total, loss_hbm, sem.at[2]))
    copies[2].start()
    for copy in copies:
        copy.wait()


def per_device(src_emb, tgt_emb, slot_group, counts, align, pair_weight):
    rows, width = src_emb.shape
    nl, per = tgt_emb.shape[0], tgt_emb.shape[1]
    nd = lax.axis_size("dp")
    nz = nd // NY
    cols = NY * rows
    half = rows // 2
    kz, ky = nz // 2 + 1, NY // 2 + 1
    vmem, smem, dma = pltpu.VMEM, pltpu.SMEM, pltpu.SemaphoreType.DMA
    in_vmem, in_smem = pl.BlockSpec(memory_space=vmem), pl.BlockSpec(memory_space=smem)
    scratch = [
        smem((nl,), jnp.int32), smem((nl,), jnp.int32), smem((nl,), F32),
        vmem((1, nd * rows), jnp.int32), vmem((nl, per, width), BF16),
        vmem((nz, rows, width), BF16), vmem((NY, rows, width), BF16), vmem((nl, per, width), BF16),
        vmem((nz, rows, rows), F32), vmem((8, rows), F32),
        vmem((nz, rows, cols), F32), vmem((nz, rows, cols), F32),
        vmem((nz, rows, rows), F32), vmem((nz, 8, cols), F32),
        vmem((nz, rows, cols), BF16), vmem((nz, rows, width), F32), vmem((NY, rows, width), F32),
        vmem((3, nz, rows), F32), vmem((3, nz, nz, rows), F32), vmem((8, rows), F32), vmem((NY, 8, rows), F32),
        vmem((8, rows), F32), vmem((nz, 8, rows), F32), vmem((8, rows), F32), vmem((NY, 8, rows), F32),
        vmem((2, kz, CZ, rows // CZ, width), BF16), vmem((2, kz, CZ, rows // CZ, width), BF16),
        vmem((2, ky, 2, half, width), BF16), vmem((2, ky, 2, half, width), BF16),
        vmem((nl, per, width), BF16), vmem((nl, per, width), BF16),
        dma((10,)), dma((4,)), dma((nz, CZ)), dma((NY, 4)), dma((5,)), dma((1,)), dma((3,)),
        dma((2, nz // 2, CZ)), dma((2, NY // 2, 2)), dma((6,)),
    ]
    found = tuple(
        pl.pallas_call(
            kernel,
            out_shape=(
                pltpu.VMEM((rows, width), BF16),
                pltpu.VMEM((nl, per, width), BF16),
                pltpu.VMEM((8, rows), F32),
            ),
            in_specs=[pl.BlockSpec(memory_space=pl.ANY)] * 6,
            out_specs=(in_vmem, in_vmem, in_vmem),
            scratch_shapes=scratch,
            compiler_params=pltpu.CompilerParams(
                collective_id=0, has_side_effects=True, vmem_limit_bytes=58 << 20
            ),
        )(slot_group, counts, pair_weight, align, src_emb, tgt_emb)
    )
    shapes = [(src_emb.shape, BF16), (tgt_emb.shape, BF16), ((1,), F32)]
    return pl.pallas_call(
        write_out,
        out_shape=tuple(jax.ShapeDtypeStruct(*shape) for shape in shapes),
        in_specs=[in_vmem] * 3,
        out_specs=(pl.BlockSpec(memory_space=pl.ANY),) * 3,
        scratch_shapes=[smem((1,), F32), dma((3,))],
    )(*(pltpu.with_memory_space_constraint(a, pltpu.VMEM) for a in found))


def solution(mesh):
    in_specs = (
        P(("lang", "dp"), None),
        P(None, ("lang", "dp"), None),
        P(),
        P(),
        P("lang", None),
        P(),
    )
    out_specs = (P(("lang", "dp"), None), P(None, ("lang", "dp"), None), P("lang"))
    return jax.shard_map(
        per_device, mesh=mesh, in_specs=in_specs, out_specs=out_specs, check_vma=False
    )
```
